32 devices in a mesh: dp: 2 (over y), seq: 16 (over z, x, core).
Axes of the slice: x: 2, y: 2, z: 4, core: 2. Of those that a mesh axis runs over, the one named last changes fastest.
Arguments:
- frames_in: bfloat16 [2, 32, 256, 1024], P(None, ('dp', 'seq')), may hold values from -6 to 6
- cotangent: bfloat16 [2, 32, 256, 1024], P(None, ('dp', 'seq')), may hold values from -6 to 6
- lengths: int32 [2, 2], P(None, 'dp'), may hold values from 4 to 16, as said below
- actions: int32 [2, 32], P(None, ('dp', 'seq')), may hold values from 0 to 7
- spatial_in: bfloat16 [1024, 3072], P('seq', 'dp'), may hold values from -0.1875 to 0.1875
- spatial_out: bfloat16 [1024, 1024], P('seq', 'dp'), may hold values from -1 to 1
- temporal_in: bfloat16 [1024, 3072], P('seq', 'dp'), may hold values from -0.1875 to 0.1875
- temporal_out: bfloat16 [1024, 1024], P('seq', 'dp'), may hold values from -0.375 to 0.375
- hidden_in: bfloat16 [1024, 4096], P('seq', 'dp'), may hold values from -0.1875 to 0.1875
- hidden_out: bfloat16 [4096, 1024], P('seq', 'dp'), may hold values from -0.09375 to 0.09375
- norm_gains: bfloat16 [3, 1024], P(None, 'seq'), may hold values from 0.25 to 1.75
- norm_shifts: bfloat16 [3, 1024], P(None, 'seq'), may hold values from -4 to 4
- bias_up: bfloat16 [4096], P('seq'), may hold values from -6 to 6
- bias_down: bfloat16 [1024], P('seq'), may hold values from -4 to 4
- action_table: bfloat16 [8, 1024], P(None, 'seq'), may hold values from -6 to 6
Outputs:
- layer_out: bfloat16 [2, 32, 256, 1024], P(None, ('dp', 'seq'))
- frames_gradient: bfloat16 [2, 32, 256, 1024], P(None, ('dp', 'seq'))
- spatial_in_gradient: float32 [1024, 3072], P('seq', 'dp')
- spatial_out_gradient: float32 [1024, 1024], P('seq', 'dp')
- temporal_in_gradient: float32 [1024, 3072], P('seq', 'dp')
- temporal_out_gradient: float32 [1024, 1024], P('seq', 'dp')
- hidden_in_gradient: float32 [1024, 4096], P('seq', 'dp')
- hidden_out_gradient: float32 [4096, 1024], P('seq', 'dp')
- gains_gradient: float32 [3, 1024], P(None, 'seq')
- shifts_gradient: float32 [3, 1024], P(None, 'seq')
- bias_up_gradient: float32 [4096], P('seq')
- bias_down_gradient: float32 [1024], P('seq')
- table_gradient: float32 [8, 1024], P(None, 'seq')
The draws below stay inside these ranges and needn't reach their ends.
Inputs may be any that keep to these rules, and one draw needn't show every extreme that they name: `lengths`: frames at or past a video's length are padding. In each micro-batch, among the 1 videos of each index of dp, exactly one has 16 live frames.
All inputs are finite; a program needn't handle non-finite values.
Results may differ from the reference program's by a relative error of at most 0.018.
Values may be sent and summed in bfloat16 or wider, within the bound.
A program may use at most 256 MiB of HBM per device.

```python
import jax
import jax.numpy as jnp
from jax import lax

HEADS = 16
HDIM = 64
D = 1024
FF = 4096
ACTIONS = 8
FRAMES = 16
SPATIAL = 256
MB = 2
VIDS = 1
VIDEOS = 2
FRAME_ROWS = 32


def draw_lengths(key, part):
    key = jax.random.fold_in(key, 11)
    key_span, key_pick = jax.random.split(key)
    spans = jax.random.randint(key_span, (MB, VIDEOS), 4, FRAMES)
    picked = jax.random.randint(key_pick, (MB, VIDEOS // VIDS, 1), 0, VIDS)
    places = jnp.arange(VIDS)[None, None, :]
    longest = (places == picked).reshape(MB, VIDEOS)
    return jnp.where(longest, FRAMES, spans).astype(jnp.int32)


def with_ends(values, stream_key, smallest, largest):
    extent = values.shape
    index_at = [jax.random.randint(jax.random.fold_in(stream_key, axis), (), 0, extent[axis]) for axis in range(len(extent))]
    values = values.at[tuple(index_at)].set(smallest)
    longest = extent.index(max(extent))
    index_at[longest] = (index_at[longest] + 1) % extent[longest]
    return values.at[tuple(index_at)].set(largest)


def steps_of(own_key, shape, cuts, least, largest):
    factor_of, own = 1.0, jax.random.fold_in(own_key, 6)
    for axis_at, blocks in cuts:
        steps = jnp.exp(jax.random.uniform(jax.random.fold_in(own, axis_at), (blocks,), jnp.float32, least / len(cuts), largest / len(cuts)))
        factor_of = factor_of * jnp.repeat(steps, shape[axis_at] // blocks).reshape([-1 if axis == axis_at else 1 for axis in range(len(shape))])
    return factor_of


def centred(rng, extent, deviation, limit, cuts=(), dtype=jnp.bfloat16):
    array = deviation * jax.random.normal(rng, extent, jnp.float32)
    if cuts:
        array = array * steps_of(rng, extent, cuts, -0.22, 0.18)
    return jnp.clip(array, -limit, limit).astype(dtype)


def setup_inputs(seed: int = 0) -> dict:
    key_list = jax.random.split(jax.random.key(seed), 16)
    return {
        "frames_in": centred(key_list[0], (MB, FRAME_ROWS, SPATIAL, D), 1.0, 6.0, ((1, 32),)),
        "cotangent": centred(key_list[1], (MB, FRAME_ROWS, SPATIAL, D), 1.0, 6.0, ((1, 32),)),
        "lengths": draw_lengths(jax.random.fold_in(key_list[15], 71), 0),
        "actions": with_ends(jax.random.randint(key_list[3], (MB, FRAME_ROWS), 0, ACTIONS), jax.random.fold_in(key_list[3], 1), 0, ACTIONS - 1).astype(jnp.int32),
        "spatial_in": centred(key_list[4], (D, 3 * D), D ** -0.5, 0.1875, ((0, 16), (1, 2))),
        "spatial_out": centred(key_list[5], (D, D), (D // 32) ** -0.5, 1.0, ((0, 16), (1, 2))),
        "temporal_in": centred(key_list[6], (D, 3 * D), D ** -0.5, 0.1875, ((0, 16), (1, 2))),
        "temporal_out": centred(key_list[7], (D, D), (D // 4) ** -0.5, 0.375, ((0, 16), (1, 2))),
        "hidden_in": centred(key_list[8], (D, FF), D ** -0.5, 0.1875, ((0, 16), (1, 2))),
        "hidden_out": centred(key_list[9], (FF, D), FF ** -0.5, 0.09375, ((0, 16), (1, 2))),
        "norm_gains": jnp.clip(1.0 + 0.15 * jax.random.normal(key_list[10], (3, D), jnp.float32), 0.25, 1.75).astype(jnp.bfloat16),
        "norm_shifts": centred(key_list[11], (3, D), 0.3, 4.0, ((1, 16),)),
        "bias_up": centred(key_list[12], (FF,), 0.5, 6.0, ((0, 16),)),
        "bias_down": centred(key_list[13], (D,), 0.3, 4.0, ((0, 16),)),
        "action_table": centred(key_list[14], (ACTIONS, D), 0.5, 6.0, ((1, 16),)),
    }


EPS = 1e-05
NEG = -1e+30
HIGH = lax.Precision.HIGHEST

@jax.custom_vjp
def low(v):
    return lax.optimization_barrier(v.astype(jnp.bfloat16)).astype(jnp.float32)

@jax.custom_vjp
def low_back(v):
    return v

def low_keep(v):
    return (low(v), None)

def low_pass(kept, grad):
    return (grad,)

def back_keep(v):
    return (v, None)

def back_low(kept, grad):
    return (low(grad),)
low.defvjp(low_keep, low_pass)
low_back.defvjp(back_keep, back_low)

def matmul(left, right):
    return jnp.dot(left, right, precision=HIGH)

def layer_norm(value, gain_row, shift_row):
    centre = lax.optimization_barrier(jnp.mean(value, axis=-1, keepdims=True))
    offset = value - centre
    spread = lax.optimization_barrier(jnp.mean(offset * offset, axis=-1, keepdims=True))
    return offset * lax.rsqrt(spread + EPS) * gain_row + shift_row

def attention(queries, key_rows, values, allowed, score_form, mix_form):
    scale = HDIM ** (-0.5)
    scores = low_back(jnp.einsum(score_form, queries, key_rows, precision=HIGH)) * scale
    if allowed is not None:
        scores = jnp.where(allowed, scores, NEG)
    prob_rows = low(jax.nn.softmax(scores, axis=-1))
    return low(low_back(jnp.einsum(mix_form, prob_rows, values, precision=HIGH)))

def video_layer(weight_set, video_clip, frame_actions, length):
    spatial_in, spatial_out, temporal_in, temporal_out, hidden_in, hidden_out, norm_gains, norm_shifts, bias_up, bias_down, action_table = weight_set
    frame_ids = jnp.arange(FRAMES)
    frame_live = (frame_ids < length).astype(jnp.float32)
    onehot = (frame_actions[:, None] == jnp.arange(ACTIONS)[None, :]).astype(jnp.float32)
    stream_in = video_clip + matmul(onehot, action_table)[:, None, :]
    normed_one = low(layer_norm(stream_in, norm_gains[0], norm_shifts[0]))
    packed_one = low(low_back(matmul(normed_one, spatial_in))).reshape(FRAMES, SPATIAL, 3, HEADS, HDIM)
    mixed_one = attention(packed_one[:, :, 0], packed_one[:, :, 1], packed_one[:, :, 2], None, 'fqhd,fkhd->fhqk', 'fhqk,fkhd->fqhd')
    stream_one = stream_in + low_back(matmul(mixed_one.reshape(FRAMES, SPATIAL, D), spatial_out))
    normed_two = low(layer_norm(stream_one, norm_gains[1], norm_shifts[1]))
    packed_two = low(low_back(matmul(normed_two, temporal_in))).reshape(FRAMES, SPATIAL, 3, HEADS, HDIM)
    allowed = (frame_ids[None, :] <= frame_ids[:, None]) & (frame_ids[None, :] < length)
    mixed_two = attention(packed_two[:, :, 0], packed_two[:, :, 1], packed_two[:, :, 2], allowed, 'qshd,kshd->shqk', 'shqk,kshd->qshd')
    stream_two = stream_one + low_back(matmul(mixed_two.reshape(FRAMES, SPATIAL, D), temporal_out))
    normed_three = low(layer_norm(stream_two, norm_gains[2], norm_shifts[2]))
    expand = low_back(matmul(normed_three, hidden_in)) + bias_up
    active = low(jax.nn.gelu(expand, approximate=True))
    stream_end = stream_two + low_back(matmul(active, hidden_out)) + bias_down
    return stream_end * frame_live[:, None, None]

def reference(frames_in, cotangent, lengths, actions, spatial_in, spatial_out, temporal_in, temporal_out, hidden_in, hidden_out, norm_gains, norm_shifts, bias_up, bias_down, action_table):
    weight_set = (spatial_in.astype(jnp.float32), spatial_out.astype(jnp.float32), temporal_in.astype(jnp.float32), temporal_out.astype(jnp.float32), hidden_in.astype(jnp.float32), hidden_out.astype(jnp.float32), norm_gains.astype(jnp.float32), norm_shifts.astype(jnp.float32), bias_up.astype(jnp.float32), bias_down.astype(jnp.float32), action_table.astype(jnp.float32))
    clip_set = frames_in.astype(jnp.float32).reshape(MB * VIDEOS, FRAMES, SPATIAL, D)
    chosen_set = actions.reshape(MB * VIDEOS, FRAMES)
    span_set = lengths.reshape(MB * VIDEOS)

    def whole(weights_now, clips_now):

        def one_video(pieces):
            return video_layer(weights_now, pieces[0], pieces[1], pieces[2])
        return lax.map(jax.checkpoint(one_video), (clips_now, chosen_set, span_set))
    outcome, pullback = jax.vjp(whole, weight_set, clip_set)
    weight_grads, clip_grad = pullback(cotangent.astype(jnp.float32).reshape(outcome.shape))
    layer_out = outcome.reshape(frames_in.shape).astype(jnp.bfloat16)
    frames_gradient = clip_grad.reshape(frames_in.shape).astype(jnp.bfloat16)
    return (layer_out, frames_gradient, weight_grads[0], weight_grads[1], weight_grads[2], weight_grads[3], weight_grads[4], weight_grads[5], weight_grads[6], weight_grads[7], weight_grads[8], weight_grads[9], weight_grads[10])
```

```python
import functools
import jax
import jax.numpy as jnp
from jax import lax
from jax.experimental import pallas as pl
from jax.experimental.pallas import tpu as pltpu
from jax.sharding import PartitionSpec as P

MESH = pl.DeviceIdType.MESH


class Place:
    def __init__(self, seq_count, dp_count):
        self.size = {"z": 4, "x": seq_count // 8, "y": dp_count}
        seq = lax.axis_index("seq")
        self.core = lax.rem(seq, 2)
        self.at = {
            "z": seq // (2 * self.size["x"]),
            "x": lax.rem(seq // 2, self.size["x"]),
            "y": lax.axis_index("dp"),
        }

    def device(self, core=None, **moved):
        at = dict(self.at, **moved)
        core = self.core if core is None else core
        return (at["y"], (at["z"] * self.size["x"] + at["x"]) * 2 + core)

    def sibling(self):
        return self.device(core=1 - self.core)


def when(condition, action):
    if condition is True:
        action()
    elif condition is not False:
        pl.when(condition)(action)


def entry_barrier(place):
    barrier = pltpu.get_barrier_semaphore()

    def greet(device):
        pl.semaphore_signal(barrier, inc=1, device_id=device, device_id_type=MESH)

    count = 1
    greet(place.sibling())
    for axis in ("x", "y", "z"):
        here, size = place.at[axis], place.size[axis]
        if size == 2:
            greet(place.device(**{axis: 1 - here}))
            count = count + 1
            continue
        pl.when(here > 0)(lambda axis=axis, here=here: greet(place.device(**{axis: here - 1})))
        pl.when(here < size - 1)(lambda axis=axis, here=here: greet(place.device(**{axis: here + 1})))
        count = count + (here > 0).astype(jnp.int32) + (here < size - 1).astype(jnp.int32)
    pl.semaphore_wait(barrier, count)


def line_steps(here, size, distance):
    if size == 2:
        return [(1 - here, True, False, 0)]
    return [
        (here - distance, here - distance >= 0, here < size - 1, 1),
        (here + distance, here + distance < size, here > 0, -1),
    ]


class Gather:
    def __init__(self, place, order, shard, whole, rows, sems):
        self.place, self.order = place, order
        self.shard, self.whole, self.rows = shard, whole, rows
        self.n = [place.size[axis] for axis in order]
        self.me = [place.at[axis] for axis in order]
        self.recv, self.send, self.sib_send, self.sib_recv, self.own_sem = sems
        self.sent = []
        n1, n2, n3 = self.n
        self.ticks = n1 - 1 + n2 + max(n3 - 1, 1)

    @staticmethod
    def sem_shapes(n):
        n1, n2, n3 = n
        count = n1 + n2 + n2 * n3
        return (
            pltpu.SemaphoreType.DMA((count,)),
            pltpu.SemaphoreType.DMA((2, count)),
            pltpu.SemaphoreType.DMA((n2, n3)),
            pltpu.SemaphoreType.DMA((n2, n3)),
            pltpu.SemaphoreType.DMA((1,)),
        )

    def block(self, first, second, third, core=None):
        at = dict(zip(self.order, (first, second, third)))
        core = self.place.core if core is None else core
        return self.whole.at[at["y"], at["z"], at["x"], core, self.rows]

    def own(self):
        return pltpu.make_async_copy(
            self.shard.at[self.rows], self.block(*self.me), self.own_sem.at[0]
        )

    def pass_on(self, stage, slot, src, dst, direction, condition):
        axis, here = self.order[stage], self.me[stage]
        target = self.place.device(**{axis: here + direction})
        sem = self.send.at[(direction + 1) // 2, slot]

        def copy():
            return pltpu.make_async_remote_copy(
                src_ref=src, dst_ref=dst, send_sem=sem, recv_sem=self.recv.at[slot],
                device_id=target, device_id_type=MESH,
            )

        when(condition, lambda: copy().start())
        self.sent.append((condition, copy))

    def spread(self, stage, slot, src, dst):
        here, size = self.me[stage], self.n[stage]
        if size == 2:
            axis = self.order[stage]
            target = self.place.device(**{axis: 1 - here})

            def copy():
                return pltpu.make_async_remote_copy(
                    src_ref=src, dst_ref=dst, send_sem=self.send.at[0, slot],
                    recv_sem=self.recv.at[slot], device_id=target, device_id_type=MESH,
                )

            copy().start()
            self.sent.append((True, copy))
            return
        self.pass_on(stage, slot, src, dst, 1, here < size - 1)
        self.pass_on(stage, slot, src, dst, -1, here > 0)

    def arrive(self, slot, ref):
        pltpu.make_async_copy(ref, ref, self.recv.at[slot]).wait()

    def to_sibling(self, second, third):
        ref = self.block(slice(None), second, third)

        def copy():
            return pltpu.make_async_remote_copy(
                src_ref=ref, dst_ref=ref, send_sem=self.sib_send.at[second, third],
                recv_sem=self.sib_recv.at[second, third],
                device_id=self.place.sibling(), device_id_type=MESH,
            )

        return copy

    def hand(self, second, third, condition=True):
        copy = self.to_sibling(second, third)
        when(condition, lambda: copy().start())

    def tick(self, now):
        n1, n2, n3 = self.n
        me1, me2, me3 = self.me
        if now == 0:
            self.own().start()
            src = self.shard.at[self.rows]
            self.spread(0, me1, src, self.block(*self.me))
        if 1 <= now <= n1 - 1:
            for index, here, go, way in line_steps(me1, n1, now):
                self.step_one(index, here, go, way)
        base = n1 - 1
        if now == base:
            self.own().wait()
            self.group_ready(me2)
            ref = self.block(slice(None), me2, me3)
            self.spread(1, n1 + me2, ref, ref)
        for distance in range(1, n2):
            if now == base + distance:
                for index, here, go, way in line_steps(me2, n2, distance):
                    self.step_two(index, here, go, way)
        for far in range(1, n3):
            for distance in range(0, n2):
                if now == base + distance + far:
                    choices = [(me2, True)] if distance == 0 else [
                        (index, here) for index, here, _, _ in line_steps(me2, n2, distance)
                    ]
                    for second, there in choices:
                        for index, here, go, way in line_steps(me3, n3, far):
                            self.step_three(second, there, index, here, go, way)

    def step_one(self, index, here, go, way):
        ref = self.block(index, *self.me[1:])
        both = here if go is True or go is False else jnp.logical_and(here, go)

        when(here, lambda: self.arrive(index, ref))
        if go is not False:
            self.pass_on(0, index, ref, ref, way, both)

    def group_ready(self, second, condition=True):
        self.hand(second, self.me[2], condition)
        ref = self.block(slice(None), second, self.me[2])
        slot = self.n[0] + self.n[1] + second * self.n[2] + self.me[2]
        if condition is True:
            self.spread(2, slot, ref, ref)
            return
        here, size = self.me[2], self.n[2]
        if size == 2:
            axis = self.order[2]
            target = self.place.device(**{axis: 1 - here})

            def copy():
                return pltpu.make_async_remote_copy(
                    src_ref=ref, dst_ref=ref, send_sem=self.send.at[0, slot],
                    recv_sem=self.recv.at[slot], device_id=target, device_id_type=MESH,
                )

            when(condition, lambda: copy().start())
            self.sent.append((condition, copy))
            return
        self.pass_on(2, slot, ref, ref, 1, jnp.logical_and(condition, here < size - 1))
        self.pass_on(2, slot, ref, ref, -1, jnp.logical_and(condition, here > 0))

    def step_two(self, index, here, go, way):
        slot = self.n[0] + index
        ref = self.block(slice(None), index, self.me[2])
        when(here, lambda: self.arrive(slot, ref))
        if go is not False:
            both = here if go is True else jnp.logical_and(here, go)
            self.pass_on(1, slot, ref, ref, way, both)
        self.group_ready(index, here)

    def step_three(self, second, there, index, here, go, way):
        slot = self.n[0] + self.n[1] + second * self.n[2] + index
        ref = self.block(slice(None), second, index)
        here = here if there is True else (there if here is True else jnp.logical_and(here, there))
        when(here, lambda: self.arrive(slot, ref))
        if go is not False:
            both = here if go is True else (go if here is True else jnp.logical_and(here, go))
            self.pass_on(2, slot, ref, ref, way, both)
        self.hand(second, index, here)

    def finish_recv(self):
        other = 1 - self.place.core
        for second in range(self.n[1]):
            for third in range(self.n[2]):
                ref = self.block(slice(None), second, third, core=other)
                pltpu.make_async_copy(ref, ref, self.sib_recv.at[second, third]).wait()

    def finish_send(self):
        for condition, copy in self.sent:
            when(condition, lambda copy=copy: copy().wait_send())
        for second in range(self.n[1]):
            for third in range(self.n[2]):
                self.to_sibling(second, third)().wait_send()


ORDERS = (("x", "z", "y"), ("y", "z", "x"))
ORDERS_LOW = (("z", "x", "y"), ("z", "y", "x"))


def piece_plan(weights):
    plan = []
    for index in range(weights):
        orders = ORDERS if index % 2 == 0 else ORDERS_LOW
        for half in range(2):
            plan.append((index, half, orders[half]))
    return plan


def gather_kernel(seq_count, dp_count, plan, skew, count, *refs):
    shards, wholes, sems = refs[:count], refs[count : 2 * count], refs[2 * count :]
    place = Place(seq_count, dp_count)
    entry_barrier(place)
    pieces = []
    for number, (index, half, order) in enumerate(plan):
        rows = shards[index].shape[0] // 2
        pieces.append(
            Gather(place, order, shards[index], wholes[index], pl.ds(half * rows, rows),
                   sems[5 * number : 5 * number + 5])
        )
    last = max(p.ticks + i * skew for i, p in enumerate(pieces))
    for now in range(last + 1):
        for i, piece in enumerate(pieces):
            if 0 <= now - i * skew <= piece.ticks:
                piece.tick(now - i * skew)
    for piece in pieces:
        piece.finish_recv()
        piece.finish_send()


def gather_all(shards, seq_count, dp_count, skew=1, collective_id=0):
    plan = piece_plan(len(shards))
    size = {"z": 4, "x": seq_count // 8, "y": dp_count}
    scratch = []
    for index, half, order in plan:
        scratch += list(Gather.sem_shapes([size[a] for a in order]))
    out_shape = [
        jax.ShapeDtypeStruct((dp_count, 4, size["x"], 2) + s.shape, s.dtype) for s in shards
    ]
    return pl.pallas_call(
        functools.partial(gather_kernel, seq_count, dp_count, plan, skew, len(shards)),
        out_shape=out_shape,
        in_specs=[pl.BlockSpec(memory_space=pltpu.HBM)] * len(shards),
        out_specs=[pl.BlockSpec(memory_space=pltpu.HBM)] * len(shards),
        scratch_shapes=scratch,
        compiler_params=pltpu.CompilerParams(collective_id=collective_id, has_side_effects=True),
        name="gather_weights",
    )(*shards)

D_EPS = 1e-05
NEG = -1e30
HEADS = 16
HDIM = 64
SCALE = HDIM ** (-0.5)
NT = (((1,), (1,)), ((), ()))
TN = (((0,), (0,)), ((), ()))
ROWS = 32
VMEM_LIMIT = 60 * 1024 * 1024


def dot(left, right, dims=(((1,), (0,)), ((), ()))):
    return lax.dot_general(left, right, dims, preferred_element_type=jnp.float32)


def tile_of(size, largest=512):
    return max(t for t in (128, 256, 384, 512, 1024) if t <= largest and size % t == 0)


def loop(count, action):
    def step(index, carry):
        action(index)
        return carry

    lax.fori_loop(0, count, step, 0)


def at_rows(index, size):
    return pl.ds(pl.multiple_of(index * size, size), size)


def moments(value):
    width = value.shape[-1]
    centre = jnp.sum(value, axis=-1, keepdims=True) * (1.0 / width)
    offset = value - centre
    spread = jnp.sum(offset * offset, axis=-1, keepdims=True) * (1.0 / width)
    return offset, lax.rsqrt(spread + D_EPS)


def norm_forward(read, gain, shift, out):
    def step(index):
        rows = at_rows(index, ROWS)
        offset, rate = moments(read(rows))
        out[rows, :] = (offset * rate * gain[...] + shift[...]).astype(jnp.bfloat16)

    loop(out.shape[0] // ROWS, step)


def fold8(value):
    return jnp.sum(value.reshape(-1, 8, value.shape[-1]), axis=0)


def norm_backward(read, gain, grad, upstream, write, gain_out, shift_out):
    tokens, width = grad.shape

    def step(index, carry):
        gain_sum, shift_sum = carry
        rows = at_rows(index, ROWS)
        offset, rate = moments(read(rows))
        unit = offset * rate
        dy = grad[rows, :]
        gain_sum = gain_sum + fold8(dy * unit)
        shift_sum = shift_sum + fold8(dy)
        scaled = dy * gain[...]
        mean = jnp.sum(scaled, axis=-1, keepdims=True) * (1.0 / width)
        slope = jnp.sum(scaled * unit, axis=-1, keepdims=True) * (1.0 / width)
        write(index, rows, upstream(rows) + rate * (scaled - mean - unit * slope))
        return gain_sum, shift_sum

    zero = jnp.zeros((8, width), jnp.float32)
    gain_sum, shift_sum = lax.fori_loop(0, tokens // ROWS, step, (zero, zero))
    gain_out[...] = jnp.sum(gain_sum, axis=0, keepdims=True)
    shift_out[...] = jnp.sum(shift_sum, axis=0, keepdims=True)


def project(rows, weight, emit, tile_max=512):
    parts, _, size = weight.shape
    tile = tile_of(size, tile_max)
    for part in range(parts):

        def step(index, part=part):
            inner = at_rows(index, tile)
            columns = pl.ds(pl.multiple_of(part * size + index * tile, 128), tile)
            emit(columns, dot(rows[...], weight[part, :, inner]))

        loop(size // tile, step)


def project_back(grad, weight, emit, tile_max=512):
    parts, depth, size = weight.shape
    tile = tile_of(depth, tile_max)

    def step(index):
        inner = at_rows(index, tile)
        total = None
        for part in range(parts):
            term = dot(grad[:, part * size : (part + 1) * size], weight[part, inner, :], NT)
            total = term if total is None else total + term
        emit(inner, total)

    loop(depth // tile, step)


def outer(rows, grad, out, tile_max=512):
    parts, depth, size = out.shape
    tile = tile_of(depth, tile_max)

    def step(index):
        inner = at_rows(index, tile)
        left = rows[:, inner]
        for part in range(parts):
            out[part, inner, :] = dot(
                left, grad[:, part * size : (part + 1) * size], TN
            ).astype(out.dtype)

    loop(depth // tile, step)


def head_mask(shape, axis, head):
    lane = lax.broadcasted_iota(jnp.int32, shape, axis)
    return (lane // HDIM) == head


def pick(value, head):
    return jnp.where(head_mask(value.shape, 1, head), value, jnp.zeros_like(value))


def pick_rows(value, head):
    return jnp.where(head_mask(value.shape, 0, head), value, jnp.zeros_like(value))


def pair_slices(index, width, tokens):
    pairs = width // 128
    micro, pair = index // pairs, lax.rem(index, pairs)
    rows = pl.ds(pl.multiple_of(micro * tokens, tokens), tokens)
    return micro, rows, [
        pl.ds(pl.multiple_of(part * width + pair * 128, 128), 128) for part in range(3)
    ]


def attention_forward(packed, allowed, probs, mixed, tokens):
    width = mixed.shape[1]

    def step(index):
        micro, rows, (q_at, k_at, v_at) = pair_slices(index, width, tokens)
        queries = packed[rows, q_at] * jnp.bfloat16(SCALE)
        keys, values = packed[rows, k_at], packed[rows, v_at]
        values_t = values.astype(jnp.float32).T.astype(jnp.bfloat16)
        total = None
        for head in range(2):
            scores = dot(keys, pick(queries, head), NT)
            if allowed is not None:
                scores = jnp.where(allowed[micro] > 0, scores, NEG)
            raised = jnp.exp(scores - jnp.max(scores, axis=0, keepdims=True))
            prob = raised * (1.0 / jnp.sum(raised, axis=0, keepdims=True))
            prob = prob.astype(jnp.bfloat16)
            probs[2 * index + head] = prob
            term = dot(pick_rows(values_t, head), prob)
            total = term if total is None else total + term
        mixed[rows, q_at] = total.T.astype(jnp.bfloat16)

    loop(mixed.shape[0] // tokens * (width // 128), step)


def attention_backward(packed, probs, grad, packed_grad, tokens):
    width = grad.shape[1]

    def step(index):
        _, rows, (q_at, k_at, v_at) = pair_slices(index, width, tokens)
        queries, keys, values = packed[rows, q_at], packed[rows, k_at], packed[rows, v_at]
        upstream = grad[rows, q_at]
        keys_t = keys.astype(jnp.float32).T.astype(jnp.bfloat16)
        query_grad = key_grad = value_grad = None
        for head in range(2):
            low = probs[2 * index + head]
            prob = low.astype(jnp.float32)
            up = pick(upstream, head)
            prob_grad = dot(values, up, NT)
            inner = jnp.sum(prob * prob_grad, axis=0, keepdims=True)
            score_grad = (prob * (prob_grad - inner) * SCALE).astype(jnp.bfloat16)
            terms = (
                dot(pick_rows(keys_t, head), score_grad),
                dot(score_grad, pick(queries, head)),
                dot(low, up),
            )
            if head == 0:
                query_grad, key_grad, value_grad = terms
            else:
                query_grad = query_grad + terms[0]
                key_grad = key_grad + terms[1]
                value_grad = value_grad + terms[2]
        packed_grad[rows, q_at] = query_grad.T.astype(jnp.bfloat16)
        packed_grad[rows, k_at] = key_grad.astype(jnp.bfloat16)
        packed_grad[rows, v_at] = value_grad.astype(jnp.bfloat16)

    loop(grad.shape[0] // tokens * (width // 128), step)


class Fetch:
    def __init__(self, src, dst, sem):
        self.copy = pltpu.make_async_copy(src, dst, sem)

    def start(self):
        self.copy.start()
        return self

    def wait(self):
        self.copy.wait()


def spatial_reader(frames, row_pair, tokens):
    def read(rows):
        micro = rows.start // tokens
        return frames[rows, :].astype(jnp.float32) + row_pair[pl.ds(micro, 1), :]

    return read


def attend_forward_kernel(spatial, tokens, *refs):
    if spatial:
        stream, row_pair, gain, shift, w_in, w_out, out, packed, probs, mixed, *rest = refs
        allowed = None
        read = spatial_reader(stream, row_pair, tokens)
    else:
        stream, allowed, gain, shift, w_in, w_out, out, packed, probs, mixed, *rest = refs
        read = lambda rows: stream[rows, :].astype(jnp.float32)
    normed, v_in, v_out, sems = rest
    first = Fetch(w_in, v_in, sems.at[0]).start()
    second = Fetch(w_out, v_out, sems.at[1]).start()
    norm_forward(read, gain, shift, normed)
    first.wait()

    def emit(columns, value):
        packed[:, columns] = value.astype(jnp.bfloat16)

    project(normed, v_in, emit)
    attention_forward(packed, allowed, probs, mixed, tokens)
    second.wait()

    def emit_out(columns, value):
        if spatial:
            for micro in range(stream.shape[0] // tokens):
                rows = slice(micro * tokens, (micro + 1) * tokens)
                base = stream[rows, columns].astype(jnp.float32) + row_pair[micro : micro + 1, columns]
                out[rows, columns] = (base + value[rows]).astype(out.dtype)
        else:
            out[:, columns] = (stream[:, columns].astype(jnp.float32) + value).astype(out.dtype)

    project(mixed, v_out, emit_out)


def vmem(count):
    return [pl.BlockSpec(memory_space=pltpu.VMEM)] * count


def hbm(count):
    return [pl.BlockSpec(memory_space=pltpu.HBM)] * count


def attend_forward(spatial, tokens, stream, extra, gain, shift, w_in, w_out):
    total, width = stream.shape
    heads = total // tokens * HEADS
    low = jnp.bfloat16
    return pl.pallas_call(
        functools.partial(attend_forward_kernel, spatial, tokens),
        out_shape=(
            jax.ShapeDtypeStruct((total, width), low if spatial else jnp.float32),
            jax.ShapeDtypeStruct((total, 3 * width), low),
            jax.ShapeDtypeStruct((heads, tokens, tokens), low),
            jax.ShapeDtypeStruct((total, width), low),
        ),
        in_specs=vmem(4) + hbm(2),
        out_specs=vmem(4),
        scratch_shapes=[
            pltpu.VMEM((total, width), low),
            pltpu.VMEM(w_in.shape, low),
            pltpu.VMEM(w_out.shape, low),
            pltpu.SemaphoreType.DMA((2,)),
        ],
        compiler_params=pltpu.CompilerParams(vmem_limit_bytes=VMEM_LIMIT),
        name="space_forward" if spatial else "time_forward",
    )(stream, extra, gain, shift, w_in, w_out)


def attend_backward_kernel(spatial, tokens, *refs):
    if spatial:
        (up, stream, row_pair, gain, shift, packed_h, probs_h, mixed, w_in_h, w_out_h,
         down, w_in_grad, w_out_grad, gain_out, shift_out, sums, *rest) = refs
        read = spatial_reader(stream, row_pair, tokens)
    else:
        (up, stream, gain, shift, packed_h, probs_h, mixed, w_in_h, w_out_h,
         down, w_in_grad, w_out_grad, gain_out, shift_out, *rest) = refs
        read = lambda rows: stream[rows, :].astype(jnp.float32)
    normed, up_low, mixed_grad, packed_grad, normed_grad, packed, probs, w_in, w_out, sems = rest
    fetches = [
        Fetch(src, dst, sems.at[i]).start()
        for i, (src, dst) in enumerate(
            ((w_out_h, w_out), (packed_h, packed), (probs_h, probs), (w_in_h, w_in))
        )
    ]

    def lower(index):
        rows = at_rows(index, ROWS)
        up_low[rows, :] = up[rows, :].astype(jnp.bfloat16)

    loop(up.shape[0] // ROWS, lower)
    norm_forward(read, gain, shift, normed)
    fetches[0].wait()

    def emit_mixed(columns, value):
        mixed_grad[:, columns] = value.astype(jnp.bfloat16)

    project_back(up_low, w_out, emit_mixed)
    outer(mixed, up_low, w_out_grad)
    fetches[1].wait()
    fetches[2].wait()
    attention_backward(packed, probs, mixed_grad, packed_grad, tokens)
    fetches[3].wait()
    outer(normed, packed_grad, w_in_grad)

    def emit_normed(columns, value):
        normed_grad[:, columns] = value

    project_back(packed_grad, w_in, emit_normed)
    if spatial:
        sums[...] = jnp.zeros_like(sums)

        def write(index, rows, value):
            down[rows, :] = value.astype(down.dtype)
            micro = rows.start // tokens
            sums[pl.ds(micro, 1), :] += jnp.sum(fold8(value), axis=0, keepdims=True)
    else:

        def write(index, rows, value):
            down[rows, :] = value.astype(down.dtype)

    norm_backward(
        read, gain, normed_grad, lambda rows: up[rows, :].astype(jnp.float32), write, gain_out, shift_out
    )


def attend_backward(spatial, tokens, up, stream, extra, gain, shift, packed, probs, mixed, w_in, w_out):
    total, width = stream.shape
    low, full = jnp.bfloat16, jnp.float32
    shape = jax.ShapeDtypeStruct
    outs = [
        shape((total, width), low),
        shape(w_in.shape, low),
        shape(w_out.shape, low),
        shape((1, width), full),
        shape((1, width), full),
    ]
    if spatial:
        outs.append(shape((total // tokens, width), full))
    front = (up, stream) + ((extra,) if spatial else ()) + (gain, shift)
    return pl.pallas_call(
        functools.partial(attend_backward_kernel, spatial, tokens),
        out_shape=tuple(outs),
        in_specs=vmem(len(front)) + hbm(2) + vmem(1) + hbm(2),
        out_specs=vmem(len(outs)),
        scratch_shapes=[
            pltpu.VMEM((total, width), low),
            pltpu.VMEM((total, width), low),
            pltpu.VMEM((total, width), low),
            pltpu.VMEM((total, 3 * width), low),
            pltpu.VMEM((total, width), full),
            pltpu.VMEM(packed.shape, low),
            pltpu.VMEM(probs.shape, low),
            pltpu.VMEM(w_in.shape, low),
            pltpu.VMEM(w_out.shape, low),
            pltpu.SemaphoreType.DMA((4,)),
        ],
        compiler_params=pltpu.CompilerParams(vmem_limit_bytes=VMEM_LIMIT),
        name="space_backward" if spatial else "time_backward",
    )(*front, packed, probs, mixed, w_in, w_out)


GELU_A = 0.7978845608028654
GELU_B = 0.044715


def gelu_pair(value):
    square = value * value
    bent = jnp.tanh(GELU_A * value * (1.0 + GELU_B * square))
    half = 0.5 * (1.0 + bent)
    slope = half + 0.5 * value * (1.0 - bent * bent) * (GELU_A * (1.0 + 3.0 * GELU_B * square))
    return value * half, slope


def hidden_kernel(stream, cotangent, live, gain, shift, up_bias, down_bias, w_up_h, w_down_h,
                  out, down, up_grad_h, down_grad_h, gain_out, shift_out, up_bias_out, down_bias_out,
                  normed, end_low, active, slope, expand_low, normed_grad, w_up, w_down, up_stage, down_stage, sems):
    low = jnp.bfloat16
    first = Fetch(w_up_h, w_up, sems.at[0]).start()
    second = Fetch(w_down_h, w_down, sems.at[1]).start()
    tokens, width = stream.shape
    parts = w_up.shape[0]
    norm_forward(lambda rows: stream[rows, :], gain, shift, normed)

    def lower(index, total):
        rows = at_rows(index, ROWS)
        value = cotangent[rows, :].astype(jnp.float32) * live[rows, :]
        end_low[rows, :] = value.astype(low)
        return total + fold8(value)

    total = lax.fori_loop(0, tokens // ROWS, lower, jnp.zeros((8, width), jnp.float32))
    down_bias_out[...] = jnp.sum(total, axis=0, keepdims=True)
    first.wait()

    def emit_expand(columns, value):
        act, rate = gelu_pair(value + up_bias[:, columns])
        active[:, columns] = act.astype(low)
        slope[:, columns] = rate.astype(low)

    project(normed, w_up, emit_expand, 256)
    second.wait()

    def emit_out(columns, value):
        end = stream[:, columns] + value + down_bias[:, columns]
        out[:, columns] = (end * live[...]).astype(out.dtype)

    project(active, w_down, emit_out, 256)

    def emit_active(columns, value):
        grad = value * slope[:, columns].astype(jnp.float32)
        up_bias_out[:, columns] = jnp.sum(grad, axis=0, keepdims=True)
        expand_low[:, columns] = grad.astype(low)

    project_back(end_low, w_down, emit_active, 256)

    hidden, size = w_down.shape[1], w_down.shape[2]
    tile = down_stage.shape[2]

    def send_down(index, slot):
        return pltpu.make_async_copy(
            down_stage.at[slot], down_grad_h.at[:, at_rows(index, tile), :], sems.at[2 + slot]
        )

    def step_down(index):
        slot = lax.rem(index, 2)
        pl.when(index >= 2)(lambda: send_down(index - 2, slot).wait())
        left = active[:, at_rows(index, tile)]
        for part in range(parts):
            down_stage[slot, part] = dot(
                left, end_low[:, part * size : (part + 1) * size], TN
            ).astype(low)
        send_down(index, slot).start()

    count = hidden // tile
    loop(count, step_down)
    send_down(count - 2, (count - 2) % 2).wait()
    send_down(count - 1, (count - 1) % 2).wait()

    size_up = w_up.shape[2]
    tile_up = up_stage.shape[2]

    def send_up(index, slot):
        return pltpu.make_async_copy(
            up_stage.at[slot], up_grad_h.at[:, at_rows(index, tile_up), :], sems.at[4 + slot]
        )

    def step_up(index):
        slot = lax.rem(index, 2)
        pl.when(index >= 2)(lambda: send_up(index - 2, slot).wait())
        left = normed[:, at_rows(index, tile_up)]
        for part in range(parts):
            up_stage[slot, part] = dot(
                left, expand_low[:, part * size_up : (part + 1) * size_up], TN
            ).astype(low)
        send_up(index, slot).start()

    count_up = width // tile_up
    loop(count_up, step_up)

    def emit_normed(columns, value):
        normed_grad[:, columns] = value

    project_back(expand_low, w_up, emit_normed, 256)
    send_up(count_up - 2, (count_up - 2) % 2).wait()
    send_up(count_up - 1, (count_up - 1) % 2).wait()

    def write(index, rows, value):
        down[rows, :] = value

    def upstream(rows):
        return cotangent[rows, :].astype(jnp.float32) * live[rows, :]

    norm_backward(lambda rows: stream[rows, :], gain, normed_grad, upstream, write, gain_out, shift_out)


def hidden_layer(stream, cotangent, live, gain, shift, up_bias, down_bias, w_up, w_down):
    tokens, width = stream.shape
    hidden = up_bias.shape[1]
    parts = w_up.shape[0]
    low, full = jnp.bfloat16, jnp.float32
    shape = jax.ShapeDtypeStruct
    return pl.pallas_call(
        hidden_kernel,
        out_shape=(
            shape((tokens, width), low),
            shape((tokens, width), full),
            shape(w_up.shape, low),
            shape(w_down.shape, low),
            shape((1, width), full),
            shape((1, width), full),
            shape((1, hidden), full),
            shape((1, width), full),
        ),
        in_specs=vmem(7) + hbm(2),
        out_specs=vmem(2) + hbm(2) + vmem(4),
        scratch_shapes=[
            pltpu.VMEM((tokens, width), low),
            pltpu.VMEM((tokens, width), low),
            pltpu.VMEM((tokens, hidden), low),
            pltpu.VMEM((tokens, hidden), low),
            pltpu.VMEM((tokens, hidden), low),
            pltpu.VMEM((tokens, width), full),
            pltpu.VMEM(w_up.shape, low),
            pltpu.VMEM(w_down.shape, low),
            pltpu.VMEM((2, parts, 256, w_up.shape[2]), low),
            pltpu.VMEM((2, parts, 256, w_down.shape[2]), low),
            pltpu.SemaphoreType.DMA((6,)),
        ],
        compiler_params=pltpu.CompilerParams(vmem_limit_bytes=VMEM_LIMIT),
        name="hidden_layer",
    )(stream, cotangent, live, gain, shift, up_bias, down_bias, w_up, w_down)

class Reduce:
    def __init__(self, place, order, partial_sum, rows, out, bufs, sems):
        self.place, self.order, self.rows = place, order, rows
        self.partial, self.out = partial_sum, out
        self.kept, self.from_core, self.from_third, self.from_second, self.from_first = bufs
        self.core_sems, self.third_sems, self.second_sems, self.first_sems = sems
        self.n = [place.size[axis] for axis in order]
        self.me = [place.at[axis] for axis in order]
        self.sent = []
        n1, n2, n3 = self.n
        self.pair = n3 == 2
        self.third_ticks = 0 if self.pair else n3
        self.ticks = 1 + self.third_ticks + n2 + (1 if n1 == 2 else n1)

    @staticmethod
    def scratch(n, sizes, rows, columns, dtype):
        n1, n2, n3 = n
        slots = lambda count: 1 if count == 2 else count + 1
        return (
            [
                pltpu.VMEM(sizes + (rows, columns), dtype),
                pltpu.VMEM(sizes + (rows, columns), dtype),
                pltpu.VMEM((slots(n3), n2, n1, rows, columns), dtype),
                pltpu.VMEM((slots(n2), n1, rows, columns), dtype),
                pltpu.VMEM((slots(n1), rows, columns), dtype),
            ],
            [
                pltpu.SemaphoreType.DMA((3,)),
                pltpu.SemaphoreType.DMA((2, n3 + 1, n2)),
                pltpu.SemaphoreType.DMA((2, n2 + 1)),
                pltpu.SemaphoreType.DMA((2, n1 + 1)),
            ],
        )

    def block(self, first, second, third):
        at = dict(zip(self.order, (first, second, third)))
        return self.kept.at[at["y"], at["z"], at["x"]]

    def core_copy(self):
        return pltpu.make_async_remote_copy(
            src_ref=self.partial.at[:, :, :, 1 - self.place.core, self.rows],
            dst_ref=self.from_core,
            send_sem=self.core_sems.at[0], recv_sem=self.core_sems.at[1],
            device_id=self.place.sibling(), device_id_type=MESH,
        )

    def own_copy(self):
        return pltpu.make_async_copy(
            self.partial.at[:, :, :, self.place.core, self.rows], self.kept, self.core_sems.at[2]
        )

    def add_rows(self, dst, src, index):
        rows = dst.shape[-2]

        def step(i):
            at = index + (at_rows(i, 16),)
            dst[at] = dst[at] + src[at]

        loop(rows // 16, step)

    def send(self, stage, slot_sem, src, dst, moved, recv_sem, condition=True):
        axis = self.order[stage]

        def copy():
            return pltpu.make_async_remote_copy(
                src_ref=src, dst_ref=dst, send_sem=slot_sem, recv_sem=recv_sem,
                device_id=self.place.device(**{axis: moved}), device_id_type=MESH,
            )

        when(condition, lambda: copy().start())
        self.sent.append((condition, copy))

    def arrived(self, sem, ref):
        pltpu.make_async_copy(ref, ref, sem).wait()

    def second_order(self):
        order = []
        for step in range(1, self.n[1] + 1):
            for index in (self.n[1] - step, step - 1):
                if index not in order:
                    order.append(index)
        return order

    def tick(self, now):
        n1, n2, n3 = self.n
        if now == 0:
            self.core_copy().start()
            self.own_copy().start()
            return
        if now == 1:
            self.own_copy().wait()
            self.arrived(self.core_sems.at[1], self.from_core)
            sizes = self.kept.shape[:3]

            def add(index):
                y, rest = index // (sizes[1] * sizes[2]), lax.rem(index, sizes[1] * sizes[2])
                at = (y, rest // sizes[2], lax.rem(rest, sizes[2]))
                self.add_rows(self.kept, self.from_core, at)

            loop(sizes[0] * sizes[1] * sizes[2], add)
            if self.pair:
                other = 1 - self.me[2]
                for second in self.second_order():
                    self.send(
                        2, self.third_sems.at[0, 0, second], self.block(slice(None), second, other),
                        self.from_third.at[0, second], other, self.third_sems.at[1, 0, second],
                    )
        now = now - 1
        if not self.pair:
            if now < n3:
                self.line(2, now)
        now = now - self.third_ticks
        if 0 <= now < n2:
            self.line(1, now)
        now = now - n2
        if 0 <= now and now < (1 if n1 == 2 else n1):
            self.line(0, now)
        if now == (1 if n1 == 2 else n1):
            pass

    def stage_ref(self, stage, index):
        if stage == 2:
            return self.block(slice(None), slice(None), index)
        if stage == 1:
            return self.block(slice(None), index, self.me[2])
        return self.block(index, self.me[1], self.me[2])

    def buffers(self, stage):
        if stage == 2:
            return self.from_third, self.third_sems.at[0, :, 0], self.third_sems.at[1, :, 0]
        if stage == 1:
            return self.from_second, self.second_sems.at[0], self.second_sems.at[1]
        return self.from_first, self.first_sems.at[0], self.first_sems.at[1]

    def absorb(self, stage, index, buffer_slot):
        buffer, sems = (
            (self.from_third, lambda s: self.third_sems.at[1, s, 0]),
            (self.from_second, lambda s: self.second_sems.at[1, s]),
            (self.from_first, lambda s: self.first_sems.at[1, s]),
        )[2 - stage]
        self.arrived(sems(buffer_slot), buffer.at[buffer_slot])
        target = self.stage_ref(stage, index)
        source = buffer.at[buffer_slot]
        self.add_all(target, source)

    def add_all(self, target, source):
        lead = target.shape[:-2]
        count = 1
        for size in lead:
            count *= size

        def add(index):
            at, rest = (), index
            for size in reversed(lead):
                at = (lax.rem(rest, size),) + at
                rest = rest // size
            self.add_rows(target, source, at)

        if count == 1 and not lead:
            self.add_rows(target, source, ())
        else:
            loop(count, add)

    def third_ready(self, second):
        if not self.pair:
            return
        self.arrived(self.third_sems.at[1, 0, second], self.from_third.at[0, second])
        self.add_all(self.block(slice(None), second, self.me[2]), self.from_third.at[0, second])

    def line(self, stage, now):
        size, here = self.n[stage], self.me[stage]
        sems = (self.first_sems, self.second_sems, None)[stage]
        send_sem = lambda s: self.third_sems.at[0, s, 0] if stage == 2 else sems.at[0, s]
        recv_sem = lambda s: self.third_sems.at[1, s, 0] if stage == 2 else sems.at[1, s]
        buffer = (self.from_first, self.from_second, self.from_third)[stage]
        if size == 2:
            if stage == 1:
                if now == 0:
                    for second in range(2):
                        self.third_ready(second)
                    self.send(stage, send_sem(0), self.stage_ref(stage, 1 - here), buffer.at[0], 1 - here, recv_sem(0))
                if now == 1:
                    self.absorb(stage, here, 0)
                    self.start_first()
            if stage == 0:
                self.arrived(recv_sem(0), buffer.at[0])
                self.finish(buffer.at[0])
            return
        if now < size - 1:
            up = size - 1 - now + here
            goes_up = jnp.logical_and(here <= now, here < size - 1)

            def go_up():
                if stage == 1:
                    self.third_ready(up)
                pl.when(here > 0)(lambda: self.absorb(stage, up, up))

            up = jnp.minimum(up, size - 1)
            pl.when(goes_up)(go_up)
            self.send(stage, send_sem(up), self.stage_ref(stage, up), buffer.at[up], here + 1, recv_sem(up), goes_up)
            down = jnp.maximum(now + here - (size - 1), 0)
            goes_down = jnp.logical_and(size - 1 - here <= now, here > 0)

            def go_down():
                if stage == 1:
                    self.third_ready(down)
                pl.when(here < size - 1)(lambda: self.absorb(stage, down, down))

            pl.when(goes_down)(go_down)
            self.send(stage, send_sem(down), self.stage_ref(stage, down), buffer.at[self.down_slot(stage, down)],
                      here - 1, recv_sem(self.down_slot(stage, down)), goes_down)
            return
        if stage == 1:
            self.third_ready(here)
        pl.when(here > 0)(lambda: self.absorb(stage, here, here))
        pl.when(here < size - 1)(lambda: self.absorb(stage, here, size))
        if stage == 1:
            self.start_first()
        if stage == 0:
            self.finish(None)

    def down_slot(self, stage, target):
        here, size = self.me[stage], self.n[stage]
        return jnp.where(target == here - 1, size, target)

    def start_first(self):
        if self.n[0] == 2:
            other = 1 - self.me[0]
            self.send(0, self.first_sems.at[0, 0], self.stage_ref(0, other), self.from_first.at[0], other,
                      self.first_sems.at[1, 0])

    def finish(self, extra):
        own = self.stage_ref(0, self.me[0])

        def step(i):
            rows = at_rows(i, 16)
            value = own[rows, :].astype(jnp.float32)
            if extra is not None:
                value = value + extra[rows, :].astype(jnp.float32)
            self.out[pl.ds(pl.multiple_of(self.rows.start + i * 16, 16), 16), :] = value

        loop(own.shape[0] // 16, step)

    def finish_send(self):
        self.core_copy().wait_send()
        for condition, copy in self.sent:
            when(condition, lambda copy=copy: copy().wait_send())


def split_plan(heights, parts_of, orders_of):
    plan = []
    for index, height in enumerate(heights):
        parts = min(parts_of, height // 16)
        rows = height // parts
        for part in range(parts):
            plan.append((index, part * rows, rows, orders_of(index)[part]))
    return plan


def run_pieces(pieces, offsets, skew, work=()):
    events = []
    for i, piece in enumerate(pieces):
        for e in range(piece.ticks + 1):
            own = offsets[piece.order[2]] if isinstance(offsets, dict) else offsets
            when_at = own[e] if e < len(own) else own[-1] + e - len(own) + 1
            events.append((when_at + i * skew, i, e))
    events.sort()
    for _, i, e in events:
        pieces[i].tick(e)


def reduce_kernel(seq_count, dp_count, plan, offsets, skew, count, *refs):
    partials, outs, rest = refs[:count], refs[count : 2 * count], refs[2 * count :]
    place = Place(seq_count, dp_count)
    entry_barrier(place)
    pieces = []
    for number, (index, first, rows, order) in enumerate(plan):
        own = rest[9 * number : 9 * number + 9]
        pieces.append(Reduce(place, order, partials[index], pl.ds(first, rows), outs[index], own[:5], own[5:]))
    run_pieces(pieces, offsets, skew)
    for piece in pieces:
        piece.finish_send()


def weight_orders(index):
    if index in (0, 1, 4):
        return (("z", "x", "y"), ("z", "y", "x"), ("x", "y", "z"), ("x", "z", "y"))
    return (("z", "x", "y"), ("z", "y", "x"), ("y", "x", "z"), ("y", "z", "x"))


def reduce_all(partials, seq_count, dp_count, parts=2, offsets=(0, 1, 3, 4, 5, 6, 7), skew=1, collective_id=0, orders=weight_orders):
    size = {"z": 4, "x": seq_count // 8, "y": dp_count}
    sizes = (dp_count, 4, size["x"])
    scratch = []
    blocked, outs = [], []
    for p in partials:
        rows = p.shape[1] // seq_count
        blocked.append(p.reshape((dp_count, 4, size["x"], 2, rows, p.shape[2])))
        outs.append(jax.ShapeDtypeStruct((rows, p.shape[2]), jnp.float32))
    plan = split_plan([o.shape[0] for o in outs], parts, orders)
    for index, first, rows, order in plan:
        bufs, sems = Reduce.scratch(
            [size[a] for a in order], sizes, rows, outs[index].shape[1], partials[index].dtype
        )
        scratch += bufs + sems
    return pl.pallas_call(
        functools.partial(reduce_kernel, seq_count, dp_count, plan, offsets, skew, len(partials)),
        out_shape=outs,
        in_specs=hbm(len(partials)),
        out_specs=vmem(len(partials)),
        scratch_shapes=scratch,
        compiler_params=pltpu.CompilerParams(
            collective_id=collective_id, has_side_effects=True, vmem_limit_bytes=VMEM_LIMIT
        ),
        name="reduce_gradients",
    )(*blocked)

ACTIONS = 8
FRAMES = 16


def body(
    frames_in,
    cotangent,
    lengths,
    actions,
    spatial_in,
    spatial_out,
    temporal_in,
    temporal_out,
    hidden_in,
    hidden_out,
    norm_gains,
    norm_shifts,
    bias_up,
    bias_down,
    action_table,
):
    seq_count, dp_count = lax.axis_size("seq"), lax.axis_size("dp")
    micro, frame_count, spatial, width = frames_in.shape
    tokens = micro * frame_count * spatial
    frames = seq_count * frame_count
    places = spatial // seq_count
    group = frames * places
    cut = norm_gains.shape[1]
    low, full = jnp.bfloat16, jnp.float32

    up_rows = bias_up.shape[0] // cut
    small = jnp.concatenate(
        [norm_gains, norm_shifts, action_table, bias_down[None], bias_up.reshape(up_rows, cut)], axis=0
    )
    used = small.shape[0]
    small = jnp.pad(small, ((0, 32 - used), (0, 128 - cut)))
    shards = [spatial_in, spatial_out, temporal_in, temporal_out, hidden_in, hidden_out, small]
    wholes = gather_all(shards, seq_count, dp_count, skew=0, collective_id=1)
    weights = [
        whole.reshape(dp_count, shard.shape[0] * seq_count, shard.shape[1])
        for whole, shard in zip(wholes[:6], shards)
    ]
    w_sin, w_sout, w_tin, w_tout, w_hin, w_hout = weights
    small = wholes[6][0].reshape(seq_count, 32, 128)[:, :, :cut].astype(full)
    rows = small[:, : used - up_rows].transpose(1, 0, 2).reshape(used - up_rows, width)
    gain, shift = [rows[i : i + 1] for i in range(3)], [rows[i : i + 1] for i in range(3, 6)]
    table, down_bias = rows[6:14], rows[14:15]
    up_bias = small[:, used - up_rows : used].reshape(1, -1)

    at = jnp.arange(group, dtype=jnp.int32)
    frame, place = at // places, at % places
    video, frame = frame // FRAMES, frame % FRAMES
    span = lengths[:, video]
    alive = frame[None] < span
    allowed = (
        (place[:, None] == place[None]) & (video[:, None] == video[None]) & (frame[:, None] <= frame[None])
    )[None] & alive[:, :, None]
    allowed = allowed.astype(full)
    live = alive.astype(full).reshape(tokens, 1)
    onehot = (actions.reshape(-1)[:, None] == jnp.arange(ACTIONS)[None, :]).astype(full)
    row_pair = jnp.dot(onehot, table, precision=lax.Precision.HIGHEST)

    def to_places(value):
        value = value.reshape(micro, frame_count, seq_count, places, width)
        value = lax.all_to_all(value, "seq", split_axis=2, concat_axis=2, tiled=True)
        return value.transpose(0, 2, 1, 3, 4).reshape(tokens, width)

    def to_frames(value):
        value = value.reshape(micro, seq_count, frame_count, places, width)
        value = lax.all_to_all(value, "seq", split_axis=1, concat_axis=1, tiled=True)
        return value.transpose(0, 2, 1, 3, 4).reshape(tokens, width)

    frames_flat = frames_in.reshape(tokens, width)
    end_grad = to_places(cotangent)
    stream_one, packed_one, probs_one, mixed_one = attend_forward(
        True, spatial, frames_flat, row_pair, gain[0], shift[0], w_sin, w_sout
    )
    stream_one = to_places(stream_one)
    stream_two, packed_two, probs_two, mixed_two = attend_forward(
        False, group, stream_one, allowed, gain[1], shift[1], w_tin, w_tout
    )
    out, two_grad, hin_grad, hout_grad, gain_three, shift_three, up_grad, down_grad = hidden_layer(
        stream_two, end_grad, live, gain[2], shift[2], up_bias, down_bias, w_hin, w_hout
    )
    layer_out = to_frames(out).reshape(frames_in.shape)
    one_grad, tin_grad, tout_grad, gain_two, shift_two = attend_backward(
        False, group, two_grad, stream_one, None, gain[1], shift[1], packed_two, probs_two, mixed_two, w_tin, w_tout
    )
    one_grad = to_frames(one_grad)
    in_grad, sin_grad, sout_grad, gain_one, shift_one, sums = attend_backward(
        True, spatial, one_grad, frames_flat, row_pair, gain[0], shift[0], packed_one, probs_one, mixed_one, w_sin, w_sout
    )
    table_grad = lax.dot_general(onehot, sums, (((0,), (0,)), ((), ())), precision=lax.Precision.HIGHEST)

    rows = jnp.concatenate(
        [gain_one, gain_two, gain_three, shift_one, shift_two, shift_three, table_grad, down_grad], axis=0
    )
    rows = rows.reshape(used - up_rows, seq_count, cut).transpose(1, 0, 2)
    rows = jnp.concatenate([rows, up_grad.reshape(seq_count, up_rows, cut)], axis=1)
    rows = jnp.pad(rows, ((0, 0), (0, 32 - used), (0, 128 - cut))).astype(low).reshape(1, seq_count * 32, 128)
    rows = jnp.broadcast_to(rows, (dp_count,) + rows.shape[1:])
    first = reduce_all([hin_grad, hout_grad], seq_count, dp_count, collective_id=2)
    second = reduce_all([sin_grad, sout_grad, tin_grad, tout_grad, rows], seq_count, dp_count, collective_id=3)
    small = second[4][:, :cut]
    return (
        layer_out,
        in_grad.reshape(frames_in.shape),
        second[0],
        second[1],
        second[2],
        second[3],
        first[0],
        first[1],
        small[0:3],
        small[3:6],
        small[15:used].reshape(-1),
        small[14],
        small[6:14],
    )


def solution(mesh):
    rows = P(None, ("dp", "seq"), None, None)
    matrix = P("seq", "dp")
    cut = P(None, "seq")
    in_specs = (rows, rows, P(None, "dp"), P(None, ("dp", "seq"))) + (matrix,) * 6 + (cut, cut, P("seq"), P("seq"), cut)
    out_specs = (rows, rows) + (matrix,) * 6 + (cut, cut, P("seq"), P("seq"), cut)
    return jax.shard_map(body, mesh=mesh, in_specs=in_specs, out_specs=out_specs, check_vma=False)
```

```python
import functools
import jax
import jax.numpy as jnp
from jax import lax
from jax.experimental import pallas as pl
from jax.experimental.pallas import tpu as pltpu
from jax.sharding import PartitionSpec as P

MESH = pl.DeviceIdType.MESH


class Place:
    def __init__(self, seq_count, dp_count):
        self.size = {"z": 4, "x": seq_count // 8, "y": dp_count}
        seq = lax.axis_index("seq")
        self.core = lax.rem(seq, 2)
        self.at = {
            "z": seq // (2 * self.size["x"]),
            "x": lax.rem(seq // 2, self.size["x"]),
            "y": lax.axis_index("dp"),
        }

    def device(self, core=None, **moved):
        at = dict(self.at, **moved)
        core = self.core if core is None else core
        return (at["y"], (at["z"] * self.size["x"] + at["x"]) * 2 + core)

    def sibling(self):
        return self.device(core=1 - self.core)


def when(condition, action):
    if condition is True:
        action()
    elif condition is not False:
        pl.when(condition)(action)


def entry_barrier(place, change=None):
    barrier = pltpu.get_barrier_semaphore()

    def greet(device):
        pl.semaphore_signal(barrier, inc=1, device_id=device, device_id_type=MESH)

    count = 1
    if change is not None:
        count = count + change.greet()
    greet(place.sibling())
    for axis in ("x", "y", "z"):
        here, size = place.at[axis], place.size[axis]
        if size == 2:
            greet(place.device(**{axis: 1 - here}))
            count = count + 1
            continue
        pl.when(here > 0)(lambda axis=axis, here=here: greet(place.device(**{axis: here - 1})))
        pl.when(here < size - 1)(lambda axis=axis, here=here: greet(place.device(**{axis: here + 1})))
        count = count + (here > 0).astype(jnp.int32) + (here < size - 1).astype(jnp.int32)
    pl.semaphore_wait(barrier, count)


def line_steps(here, size, distance):
    if size == 2:
        return [(1 - here, True, False, 0)]
    return [
        (here - distance, here - distance >= 0, here < size - 1, 1),
        (here + distance, here + distance < size, here > 0, -1),
    ]


class Gather:
    def __init__(self, place, order, shard, whole, rows, sems):
        self.place, self.order = place, order
        self.shard, self.whole, self.rows = shard, whole, rows
        self.n = [place.size[axis] for axis in order]
        self.me = [place.at[axis] for axis in order]
        self.recv, self.send, self.sib_send, self.sib_recv, self.own_sem = sems
        self.sent = []
        n1, n2, n3 = self.n
        self.ticks = n1 - 1 + n2 + max(n3 - 1, 1)

    @staticmethod
    def sem_shapes(n):
        n1, n2, n3 = n
        count = n1 + n2 + n2 * n3
        return (
            pltpu.SemaphoreType.DMA((count,)),
            pltpu.SemaphoreType.DMA((2, count)),
            pltpu.SemaphoreType.DMA((n2, n3)),
            pltpu.SemaphoreType.DMA((n2, n3)),
            pltpu.SemaphoreType.DMA((1,)),
        )

    def block(self, first, second, third, core=None):
        at = dict(zip(self.order, (first, second, third)))
        core = self.place.core if core is None else core
        return self.whole.at[at["y"], at["z"], at["x"], core, self.rows]

    def own(self):
        return pltpu.make_async_copy(
            self.shard.at[self.rows], self.block(*self.me), self.own_sem.at[0]
        )

    def pass_on(self, stage, slot, src, dst, direction, condition):
        axis, here = self.order[stage], self.me[stage]
        target = self.place.device(**{axis: here + direction})
        sem = self.send.at[(direction + 1) // 2, slot]

        def copy():
            return pltpu.make_async_remote_copy(
                src_ref=src, dst_ref=dst, send_sem=sem, recv_sem=self.recv.at[slot],
                device_id=target, device_id_type=MESH,
            )

        when(condition, lambda: copy().start())
        self.sent.append((condition, copy))

    def spread(self, stage, slot, src, dst):
        here, size = self.me[stage], self.n[stage]
        if size == 2:
            axis = self.order[stage]
            target = self.place.device(**{axis: 1 - here})

            def copy():
                return pltpu.make_async_remote_copy(
                    src_ref=src, dst_ref=dst, send_sem=self.send.at[0, slot],
                    recv_sem=self.recv.at[slot], device_id=target, device_id_type=MESH,
                )

            copy().start()
            self.sent.append((True, copy))
            return
        self.pass_on(stage, slot, src, dst, 1, here < size - 1)
        self.pass_on(stage, slot, src, dst, -1, here > 0)

    def arrive(self, slot, ref):
        pltpu.make_async_copy(ref, ref, self.recv.at[slot]).wait()

    def to_sibling(self, second, third):
        ref = self.block(slice(None), second, third)

        def copy():
            return pltpu.make_async_remote_copy(
                src_ref=ref, dst_ref=ref, send_sem=self.sib_send.at[second, third],
                recv_sem=self.sib_recv.at[second, third],
                device_id=self.place.sibling(), device_id_type=MESH,
            )

        return copy

    def hand(self, second, third, condition=True):
        copy = self.to_sibling(second, third)
        when(condition, lambda: copy().start())

    def tick(self, now):
        n1, n2, n3 = self.n
        me1, me2, me3 = self.me
        if now == 0:
            self.own().start()
            src = self.shard.at[self.rows]
            self.spread(0, me1, src, self.block(*self.me))
        if 1 <= now <= n1 - 1:
            for index, here, go, way in line_steps(me1, n1, now):
                self.step_one(index, here, go, way)
        base = n1 - 1
        if now == base:
            self.own().wait()
            self.group_ready(me2)
            ref = self.block(slice(None), me2, me3)
            self.spread(1, n1 + me2, ref, ref)
        for distance in range(1, n2):
            if now == base + distance:
                for index, here, go, way in line_steps(me2, n2, distance):
                    self.step_two(index, here, go, way)
        for far in range(1, n3):
            for distance in range(0, n2):
                if now == base + distance + far:
                    choices = [(me2, True)] if distance == 0 else [
                        (index, here) for index, here, _, _ in line_steps(me2, n2, distance)
                    ]
                    for second, there in choices:
                        for index, here, go, way in line_steps(me3, n3, far):
                            self.step_three(second, there, index, here, go, way)

    def step_one(self, index, here, go, way):
        ref = self.block(index, *self.me[1:])
        both = here if go is True or go is False else jnp.logical_and(here, go)

        when(here, lambda: self.arrive(index, ref))
        if go is not False:
            self.pass_on(0, index, ref, ref, way, both)

    def group_ready(self, second, condition=True):
        self.hand(second, self.me[2], condition)
        ref = self.block(slice(None), second, self.me[2])
        slot = self.n[0] + self.n[1] + second * self.n[2] + self.me[2]
        if condition is True:
            self.spread(2, slot, ref, ref)
            return
        here, size = self.me[2], self.n[2]
        if size == 2:
            axis = self.order[2]
            target = self.place.device(**{axis: 1 - here})

            def copy():
                return pltpu.make_async_remote_copy(
                    src_ref=ref, dst_ref=ref, send_sem=self.send.at[0, slot],
                    recv_sem=self.recv.at[slot], device_id=target, device_id_type=MESH,
                )

            when(condition, lambda: copy().start())
            self.sent.append((condition, copy))
            return
        self.pass_on(2, slot, ref, ref, 1, jnp.logical_and(condition, here < size - 1))
        self.pass_on(2, slot, ref, ref, -1, jnp.logical_and(condition, here > 0))

    def step_two(self, index, here, go, way):
        slot = self.n[0] + index
        ref = self.block(slice(None), index, self.me[2])
        when(here, lambda: self.arrive(slot, ref))
        if go is not False:
            both = here if go is True else jnp.logical_and(here, go)
            self.pass_on(1, slot, ref, ref, way, both)
        self.group_ready(index, here)

    def step_three(self, second, there, index, here, go, way):
        slot = self.n[0] + self.n[1] + second * self.n[2] + index
        ref = self.block(slice(None), second, index)
        here = here if there is True else (there if here is True else jnp.logical_and(here, there))
        when(here, lambda: self.arrive(slot, ref))
        if go is not False:
            both = here if go is True else (go if here is True else jnp.logical_and(here, go))
            self.pass_on(2, slot, ref, ref, way, both)
        self.hand(second, index, here)

    def finish_recv(self):
        other = 1 - self.place.core
        for second in range(self.n[1]):
            for third in range(self.n[2]):
                ref = self.block(slice(None), second, third, core=other)
                pltpu.make_async_copy(ref, ref, self.sib_recv.at[second, third]).wait()

    def finish_send(self):
        for condition, copy in self.sent:
            when(condition, lambda copy=copy: copy().wait_send())
        for second in range(self.n[1]):
            for third in range(self.n[2]):
                self.to_sibling(second, third)().wait_send()


ORDERS = (("x", "z", "y"), ("y", "z", "x"))
ORDERS_LOW = (("z", "x", "y"), ("z", "y", "x"))


def piece_plan(weights):
    plan = []
    for index in range(weights):
        orders = ORDERS if index % 2 == 0 else ORDERS_LOW
        for half in range(2):
            plan.append((index, half, orders[half]))
    return plan


def gather_kernel(seq_count, dp_count, plan, skew, count, *refs):
    shards, wholes, sems = refs[:count], refs[count : 2 * count], refs[2 * count :]
    place = Place(seq_count, dp_count)
    entry_barrier(place)
    pieces = []
    for number, (index, half, order) in enumerate(plan):
        rows = shards[index].shape[0] // 2
        pieces.append(
            Gather(place, order, shards[index], wholes[index], pl.ds(half * rows, rows),
                   sems[5 * number : 5 * number + 5])
        )
    last = max(p.ticks + i * skew for i, p in enumerate(pieces))
    for now in range(last + 1):
        for i, piece in enumerate(pieces):
            if 0 <= now - i * skew <= piece.ticks:
                piece.tick(now - i * skew)
    for piece in pieces:
        piece.finish_recv()
        piece.finish_send()


def gather_all(shards, seq_count, dp_count, skew=1, collective_id=0):
    plan = piece_plan(len(shards))
    size = {"z": 4, "x": seq_count // 8, "y": dp_count}
    scratch = []
    for index, half, order in plan:
        scratch += list(Gather.sem_shapes([size[a] for a in order]))
    out_shape = [
        jax.ShapeDtypeStruct((dp_count, 4, size["x"], 2) + s.shape, s.dtype) for s in shards
    ]
    return pl.pallas_call(
        functools.partial(gather_kernel, seq_count, dp_count, plan, skew, len(shards)),
        out_shape=out_shape,
        in_specs=[pl.BlockSpec(memory_space=pltpu.HBM)] * len(shards),
        out_specs=[pl.BlockSpec(memory_space=pltpu.HBM)] * len(shards),
        scratch_shapes=scratch,
        compiler_params=pltpu.CompilerParams(collective_id=collective_id, has_side_effects=True),
        name="gather_weights",
    )(*shards)

D_EPS = 1e-05
NEG = -1e30
HEADS = 16
HDIM = 64
SCALE = HDIM ** (-0.5)
NT = (((1,), (1,)), ((), ()))
TN = (((0,), (0,)), ((), ()))
ROWS = 32
VMEM_LIMIT = 60 * 1024 * 1024


def dot(left, right, dims=(((1,), (0,)), ((), ()))):
    return lax.dot_general(left, right, dims, preferred_element_type=jnp.float32)


def tile_of(size, largest=512):
    return max(t for t in (128, 256, 384, 512, 1024) if t <= largest and size % t == 0)


def loop(count, action):
    def step(index, carry):
        action(index)
        return carry

    lax.fori_loop(0, count, step, 0)


def at_rows(index, size):
    return pl.ds(pl.multiple_of(index * size, size), size)


def moments(value):
    width = value.shape[-1]
    centre = jnp.sum(value, axis=-1, keepdims=True) * (1.0 / width)
    offset = value - centre
    spread = jnp.sum(offset * offset, axis=-1, keepdims=True) * (1.0 / width)
    return offset, lax.rsqrt(spread + D_EPS)


def norm_forward(read, gain, shift, out):
    def step(index):
        rows = at_rows(index, ROWS)
        offset, rate = moments(read(rows))
        out[rows, :] = (offset * rate * gain[...] + shift[...]).astype(jnp.bfloat16)

    loop(out.shape[0] // ROWS, step)


def fold8(value):
    return jnp.sum(value.reshape(-1, 8, value.shape[-1]), axis=0)


def norm_backward(read, gain, grad, upstream, write, gain_out, shift_out):
    tokens, width = grad.shape

    def step(index, carry):
        gain_sum, shift_sum = carry
        rows = at_rows(index, ROWS)
        offset, rate = moments(read(rows))
        unit = offset * rate
        dy = grad[rows, :]
        gain_sum = gain_sum + fold8(dy * unit)
        shift_sum = shift_sum + fold8(dy)
        scaled = dy * gain[...]
        mean = jnp.sum(scaled, axis=-1, keepdims=True) * (1.0 / width)
        slope = jnp.sum(scaled * unit, axis=-1, keepdims=True) * (1.0 / width)
        write(index, rows, upstream(rows) + rate * (scaled - mean - unit * slope))
        return gain_sum, shift_sum

    zero = jnp.zeros((8, width), jnp.float32)
    gain_sum, shift_sum = lax.fori_loop(0, tokens // ROWS, step, (zero, zero))
    gain_out[...] = jnp.sum(gain_sum, axis=0, keepdims=True)
    shift_out[...] = jnp.sum(shift_sum, axis=0, keepdims=True)


def chunks(count, step, units):
    units = max(u for u in range(1, min(units, count) + 1) if count % u == 0)
    each = count // units
    for unit in range(units):
        loop(each, lambda index, unit=unit: step(unit * each + index))
        yield


def drain(work):
    for _ in work:
        pass


def project(rows, weight, emit, tile_max=512, units=1):
    parts, _, size = weight.shape
    tile = tile_of(size, tile_max)
    for part in range(parts):

        def step(index, part=part):
            inner = at_rows(index, tile)
            columns = pl.ds(pl.multiple_of(part * size + index * tile, 128), tile)
            emit(columns, dot(rows[...], weight[part, :, inner]))

        yield from chunks(size // tile, step, units)


def project_back(grad, weight, emit, tile_max=512, units=1):
    parts, depth, size = weight.shape
    tile = tile_of(depth, tile_max)

    def step(index):
        inner = at_rows(index, tile)
        total = None
        for part in range(parts):
            term = dot(grad[:, part * size : (part + 1) * size], weight[part, inner, :], NT)
            total = term if total is None else total + term
        emit(inner, total)

    yield from chunks(depth // tile, step, units)


def outer(rows, grad, out, stage, sems, units=1):
    parts, depth, size = out.shape
    tile = stage.shape[2]

    def leave(index, slot):
        return pltpu.make_async_copy(stage.at[slot], out.at[:, at_rows(index, tile), :], sems.at[slot])

    def step(index):
        slot = lax.rem(index, 2)
        pl.when(index >= 2)(lambda: leave(index - 2, slot).wait())
        left = rows[:, at_rows(index, tile)]
        for part in range(parts):
            stage[slot, part] = dot(left, grad[:, part * size : (part + 1) * size], TN).astype(out.dtype)
        leave(index, slot).start()

    count = depth // tile
    yield from chunks(count, step, units)
    leave(count - 2, (count - 2) % 2).wait()
    leave(count - 1, (count - 1) % 2).wait()


def head_mask(shape, axis, head):
    lane = lax.broadcasted_iota(jnp.int32, shape, axis)
    return (lane // HDIM) == head


def pick(value, head):
    return jnp.where(head_mask(value.shape, 1, head), value, jnp.zeros_like(value))


def pick_rows(value, head):
    return jnp.where(head_mask(value.shape, 0, head), value, jnp.zeros_like(value))


def pair_slices(index, width, tokens):
    pairs = width // 128
    micro, pair = index // pairs, lax.rem(index, pairs)
    rows = pl.ds(pl.multiple_of(micro * tokens, tokens), tokens)
    return micro, rows, [
        pl.ds(pl.multiple_of(part * width + pair * 128, 128), 128) for part in range(3)
    ]


def attention_forward(packed, allowed, probs, mixed, tokens, units=1):
    width = mixed.shape[1]

    def step(index):
        micro, rows, (q_at, k_at, v_at) = pair_slices(index, width, tokens)
        queries = packed[rows, q_at] * jnp.bfloat16(SCALE)
        keys, values = packed[rows, k_at], packed[rows, v_at]
        values_t = values.astype(jnp.float32).T.astype(jnp.bfloat16)
        total = None
        for head in range(2):
            scores = dot(keys, pick(queries, head), NT)
            if allowed is not None:
                scores = jnp.where(allowed[micro] > 0, scores, NEG)
            raised = jnp.exp(scores - jnp.max(scores, axis=0, keepdims=True))
            prob = raised * (1.0 / jnp.sum(raised, axis=0, keepdims=True))
            prob = prob.astype(jnp.bfloat16)
            probs[2 * index + head] = prob
            term = dot(pick_rows(values_t, head), prob)
            total = term if total is None else total + term
        mixed[rows, q_at] = total.T.astype(jnp.bfloat16)

    yield from chunks(mixed.shape[0] // tokens * (width // 128), step, units)


def attention_backward(packed, probs, grad, packed_grad, tokens, units=1):
    width = grad.shape[1]

    def step(index):
        _, rows, (q_at, k_at, v_at) = pair_slices(index, width, tokens)
        queries, keys, values = packed[rows, q_at], packed[rows, k_at], packed[rows, v_at]
        upstream = grad[rows, q_at]
        keys_t = keys.astype(jnp.float32).T.astype(jnp.bfloat16)
        query_grad = key_grad = value_grad = None
        for head in range(2):
            low = probs[2 * index + head]
            prob = low.astype(jnp.float32)
            up = pick(upstream, head)
            prob_grad = dot(values, up, NT)
            inner = jnp.sum(prob * prob_grad, axis=0, keepdims=True)
            score_grad = (prob * (prob_grad - inner) * SCALE).astype(jnp.bfloat16)
            terms = (
                dot(pick_rows(keys_t, head), score_grad),
                dot(score_grad, pick(queries, head)),
                dot(low, up),
            )
            if head == 0:
                query_grad, key_grad, value_grad = terms
            else:
                query_grad = query_grad + terms[0]
                key_grad = key_grad + terms[1]
                value_grad = value_grad + terms[2]
        packed_grad[rows, q_at] = query_grad.T.astype(jnp.bfloat16)
        packed_grad[rows, k_at] = key_grad.astype(jnp.bfloat16)
        packed_grad[rows, v_at] = value_grad.astype(jnp.bfloat16)

    yield from chunks(grad.shape[0] // tokens * (width // 128), step, units)


class Fetch:
    def __init__(self, src, dst, sem):
        self.copy = pltpu.make_async_copy(src, dst, sem)

    def start(self):
        self.copy.start()
        return self

    def wait(self):
        self.copy.wait()


def spatial_reader(frames, row_pair, tokens):
    def read(rows):
        micro = rows.start // tokens
        return frames[rows, :].astype(jnp.float32) + row_pair[pl.ds(micro, 1), :]

    return read


def attend_forward_kernel(spatial, tokens, *refs):
    if spatial:
        stream, row_pair, gain, shift, w_in, w_out, out, packed, probs, mixed, *rest = refs
        allowed = None
        read = spatial_reader(stream, row_pair, tokens)
    else:
        stream, allowed, gain, shift, w_in, w_out, out, packed, probs, mixed, *rest = refs
        read = lambda rows: stream[rows, :].astype(jnp.float32)
    normed, v_in, v_out, sems = rest
    first = Fetch(w_in, v_in, sems.at[0]).start()
    second = Fetch(w_out, v_out, sems.at[1]).start()
    norm_forward(read, gain, shift, normed)
    first.wait()

    def emit(columns, value):
        packed[:, columns] = value.astype(jnp.bfloat16)

    drain(project(normed, v_in, emit))
    drain(attention_forward(packed, allowed, probs, mixed, tokens))
    second.wait()

    def emit_out(columns, value):
        if spatial:
            for micro in range(stream.shape[0] // tokens):
                rows = slice(micro * tokens, (micro + 1) * tokens)
                base = stream[rows, columns].astype(jnp.float32) + row_pair[micro : micro + 1, columns]
                out[rows, columns] = (base + value[rows]).astype(out.dtype)
        else:
            out[:, columns] = (stream[:, columns].astype(jnp.float32) + value).astype(out.dtype)

    drain(project(mixed, v_out, emit_out))


def vmem(count):
    return [pl.BlockSpec(memory_space=pltpu.VMEM)] * count


def hbm(count):
    return [pl.BlockSpec(memory_space=pltpu.HBM)] * count


def attend_forward(spatial, tokens, stream, extra, gain, shift, w_in, w_out):
    total, width = stream.shape
    heads = total // tokens * HEADS
    low = jnp.bfloat16
    return pl.pallas_call(
        functools.partial(attend_forward_kernel, spatial, tokens),
        out_shape=(
            jax.ShapeDtypeStruct((total, width), low if spatial else jnp.float32),
            jax.ShapeDtypeStruct((total, 3 * width), low),
            jax.ShapeDtypeStruct((heads, tokens, tokens), low),
            jax.ShapeDtypeStruct((total, width), low),
        ),
        in_specs=vmem(4) + hbm(2),
        out_specs=vmem(4),
        scratch_shapes=[
            pltpu.VMEM((total, width), low),
            pltpu.VMEM(w_in.shape, low),
            pltpu.VMEM(w_out.shape, low),
            pltpu.SemaphoreType.DMA((2,)),
        ],
        compiler_params=pltpu.CompilerParams(vmem_limit_bytes=VMEM_LIMIT),
        name="space_forward" if spatial else "time_forward",
    )(stream, extra, gain, shift, w_in, w_out)


def attend_backward_work(spatial, tokens, up, stream, extra, gain, shift, packed_h, probs_h, mixed, w_in_h, w_out_h,
                         down, w_in_grad, w_out_grad, gain_out, shift_out, sums,
                         normed, up_low, mixed_grad, packed_grad, normed_grad, packed, probs, w_in, w_out,
                         in_stage, out_stage, sems):
    read = spatial_reader(stream, extra, tokens) if spatial else (lambda rows: stream[rows, :].astype(jnp.float32))
    fetches = [
        Fetch(src, dst, sems.at[i]).start()
        for i, (src, dst) in enumerate(
            ((w_out_h, w_out), (packed_h, packed), (probs_h, probs), (w_in_h, w_in))
        )
    ]

    def lower(index):
        rows = at_rows(index, ROWS)
        up_low[rows, :] = up[rows, :].astype(jnp.bfloat16)

    loop(up.shape[0] // ROWS, lower)
    norm_forward(read, gain, shift, normed)
    yield
    fetches[0].wait()

    def emit_mixed(columns, value):
        mixed_grad[:, columns] = value.astype(jnp.bfloat16)

    yield from project_back(up_low, w_out, emit_mixed, units=2)
    yield from outer(mixed, up_low, w_out_grad, out_stage, sems.at[pl.ds(4, 2)], units=2)
    fetches[1].wait()
    fetches[2].wait()
    yield from attention_backward(packed, probs, mixed_grad, packed_grad, tokens, units=8)
    fetches[3].wait()
    yield from outer(normed, packed_grad, w_in_grad, in_stage, sems.at[pl.ds(6, 2)], units=4)

    def emit_normed(columns, value):
        normed_grad[:, columns] = value

    yield from project_back(packed_grad, w_in, emit_normed, 256, units=4)
    block = down.shape[1]

    def put(index, value):
        down[pl.ds(index * (ROWS // block), ROWS // block)] = value.reshape(-1, block, value.shape[1]).astype(down.dtype)

    if spatial:
        sums[...] = jnp.zeros_like(sums)

        def write(index, rows, value):
            put(index, value)
            micro = rows.start // tokens
            sums[pl.ds(micro, 1), :] += jnp.sum(fold8(value), axis=0, keepdims=True)
    else:

        def write(index, rows, value):
            put(index, value)

    norm_backward(
        read, gain, normed_grad, lambda rows: up[rows, :].astype(jnp.float32), write, gain_out, shift_out
    )
    yield


END = object()


def weave(work, events, ratio):
    due = 0.0
    for event in events:
        event()
        due += ratio
        while due >= 1:
            due -= 1
            next(work, END)
    drain(work)


GELU_A = 0.7978845608028654
GELU_B = 0.044715


def gelu_pair(value):
    square = value * value
    bent = jnp.tanh(GELU_A * value * (1.0 + GELU_B * square))
    half = 0.5 * (1.0 + bent)
    slope = half + 0.5 * value * (1.0 - bent * bent) * (GELU_A * (1.0 + 3.0 * GELU_B * square))
    return value * half, slope


def hidden_kernel(stream, cotangent, live, gain, shift, up_bias, down_bias, w_up_h, w_down_h,
                  out, down, up_grad_h, down_grad_h, gain_out, shift_out, up_bias_out, down_bias_out,
                  normed, end_low, active, slope, expand_low, normed_grad, w_up, w_down, up_stage, down_stage, sems):
    low = jnp.bfloat16
    first = Fetch(w_up_h, w_up, sems.at[0]).start()
    second = Fetch(w_down_h, w_down, sems.at[1]).start()
    tokens, width = stream.shape
    parts = w_up.shape[0]
    norm_forward(lambda rows: stream[rows, :], gain, shift, normed)

    def lower(index, total):
        rows = at_rows(index, ROWS)
        value = cotangent[rows, :].astype(jnp.float32) * live[rows, :]
        end_low[rows, :] = value.astype(low)
        return total + fold8(value)

    total = lax.fori_loop(0, tokens // ROWS, lower, jnp.zeros((8, width), jnp.float32))
    down_bias_out[...] = jnp.sum(total, axis=0, keepdims=True)
    first.wait()

    def emit_expand(columns, value):
        act, rate = gelu_pair(value + up_bias[:, columns])
        active[:, columns] = act.astype(low)
        slope[:, columns] = rate.astype(low)

    drain(project(normed, w_up, emit_expand, 256))
    second.wait()

    def emit_out(columns, value):
        end = stream[:, columns] + value + down_bias[:, columns]
        out[:, columns] = (end * live[...]).astype(out.dtype)

    drain(project(active, w_down, emit_out, 256))

    def emit_active(columns, value):
        grad = value * slope[:, columns].astype(jnp.float32)
        up_bias_out[:, columns] = jnp.sum(grad, axis=0, keepdims=True)
        expand_low[:, columns] = grad.astype(low)

    drain(project_back(end_low, w_down, emit_active, 256))

    drain(outer(active, end_low, down_grad_h, down_stage, sems.at[pl.ds(2, 2)]))
    drain(outer(normed, expand_low, up_grad_h, up_stage, sems.at[pl.ds(4, 2)]))

    def emit_normed(columns, value):
        normed_grad[:, columns] = value

    drain(project_back(expand_low, w_up, emit_normed, 256))

    def write(index, rows, value):
        down[rows, :] = value

    def upstream(rows):
        return cotangent[rows, :].astype(jnp.float32) * live[rows, :]

    norm_backward(lambda rows: stream[rows, :], gain, normed_grad, upstream, write, gain_out, shift_out)


def hidden_layer(stream, cotangent, live, gain, shift, up_bias, down_bias, w_up, w_down):
    tokens, width = stream.shape
    hidden = up_bias.shape[1]
    parts = w_up.shape[0]
    low, full = jnp.bfloat16, jnp.float32
    shape = jax.ShapeDtypeStruct
    return pl.pallas_call(
        hidden_kernel,
        out_shape=(
            shape((tokens, width), low),
            shape((tokens, width), full),
            shape(w_up.shape, low),
            shape(w_down.shape, low),
            shape((1, width), full),
            shape((1, width), full),
            shape((1, hidden), full),
            shape((1, width), full),
        ),
        in_specs=vmem(7) + hbm(2),
        out_specs=vmem(2) + hbm(2) + vmem(4),
        scratch_shapes=[
            pltpu.VMEM((tokens, width), low),
            pltpu.VMEM((tokens, width), low),
            pltpu.VMEM((tokens, hidden), low),
            pltpu.VMEM((tokens, hidden), low),
            pltpu.VMEM((tokens, hidden), low),
            pltpu.VMEM((tokens, width), full),
            pltpu.VMEM(w_up.shape, low),
            pltpu.VMEM(w_down.shape, low),
            pltpu.VMEM((2, parts, 256, w_up.shape[2]), low),
            pltpu.VMEM((2, parts, 256, w_down.shape[2]), low),
            pltpu.SemaphoreType.DMA((6,)),
        ],
        compiler_params=pltpu.CompilerParams(vmem_limit_bytes=VMEM_LIMIT),
        name="hidden_layer",
    )(stream, cotangent, live, gain, shift, up_bias, down_bias, w_up, w_down)

class Reduce:
    def __init__(self, place, order, partial_sum, rows, out, bufs, sems):
        self.place, self.order, self.rows = place, order, rows
        self.partial, self.out = partial_sum, out
        self.kept, self.from_core, self.from_third, self.from_second, self.from_first = bufs
        self.core_sems, self.third_sems, self.second_sems, self.first_sems = sems
        self.n = [place.size[axis] for axis in order]
        self.me = [place.at[axis] for axis in order]
        self.sent = []
        n1, n2, n3 = self.n
        self.pair = n3 == 2
        self.third_ticks = 0 if self.pair else n3
        self.ticks = 1 + self.third_ticks + n2 + (1 if n1 == 2 else n1)

    @staticmethod
    def scratch(order, sizes, rows, columns, dtype):
        size = dict(zip(("y", "z", "x"), sizes))
        n1, n2, n3 = [size[axis] for axis in order]
        left = (n2, n1) if n3 == 2 else tuple(size[a] for a in ("y", "z", "x") if a != order[2])
        slots = lambda count: 1 if count == 2 else count + 1
        return (
            [
                pltpu.VMEM(sizes + (rows, columns), dtype),
                pltpu.VMEM(sizes + (rows, columns), dtype),
                pltpu.VMEM((slots(n3),) + left + (rows, columns), dtype),
                pltpu.VMEM((slots(n2), n1, rows, columns), dtype),
                pltpu.VMEM((slots(n1), rows, columns), dtype),
            ],
            [
                pltpu.SemaphoreType.DMA((3,)),
                pltpu.SemaphoreType.DMA((2, n3 + 1, n2)),
                pltpu.SemaphoreType.DMA((2, n2 + 1)),
                pltpu.SemaphoreType.DMA((2, n1 + 1)),
            ],
        )

    def block(self, first, second, third):
        at = dict(zip(self.order, (first, second, third)))
        return self.kept.at[at["y"], at["z"], at["x"]]

    def core_copy(self):
        return pltpu.make_async_remote_copy(
            src_ref=self.partial.at[:, :, :, 1 - self.place.core, self.rows],
            dst_ref=self.from_core,
            send_sem=self.core_sems.at[0], recv_sem=self.core_sems.at[1],
            device_id=self.place.sibling(), device_id_type=MESH,
        )

    def own_copy(self):
        return pltpu.make_async_copy(
            self.partial.at[:, :, :, self.place.core, self.rows], self.kept, self.core_sems.at[2]
        )

    def add_rows(self, dst, src, index):
        rows = dst.shape[-2]

        def step(i):
            at = index + (at_rows(i, 16),)
            dst[at] = dst[at] + src[at]

        loop(rows // 16, step)

    def send(self, stage, slot_sem, src, dst, moved, recv_sem, condition=True):
        axis = self.order[stage]

        def copy():
            return pltpu.make_async_remote_copy(
                src_ref=src, dst_ref=dst, send_sem=slot_sem, recv_sem=recv_sem,
                device_id=self.place.device(**{axis: moved}), device_id_type=MESH,
            )

        when(condition, lambda: copy().start())
        self.sent.append((condition, copy))

    def arrived(self, sem, ref):
        pltpu.make_async_copy(ref, ref, sem).wait()

    def second_order(self):
        order = []
        for step in range(1, self.n[1] + 1):
            for index in (self.n[1] - step, step - 1):
                if index not in order:
                    order.append(index)
        return order

    def tick(self, now):
        n1, n2, n3 = self.n
        if now == 0:
            self.core_copy().start()
            self.own_copy().start()
            return
        if now == 1:
            self.own_copy().wait()
            self.arrived(self.core_sems.at[1], self.from_core)
            sizes = self.kept.shape[:3]

            def add(index):
                y, rest = index // (sizes[1] * sizes[2]), lax.rem(index, sizes[1] * sizes[2])
                at = (y, rest // sizes[2], lax.rem(rest, sizes[2]))
                self.add_rows(self.kept, self.from_core, at)

            loop(sizes[0] * sizes[1] * sizes[2], add)
            if self.pair:
                other = 1 - self.me[2]
                for second in self.second_order():
                    self.send(
                        2, self.third_sems.at[0, 0, second], self.block(slice(None), second, other),
                        self.from_third.at[0, second], other, self.third_sems.at[1, 0, second],
                    )
            return
        now = now - 2
        if not self.pair:
            if now < n3:
                self.line(2, now)
        now = now - self.third_ticks
        if 0 <= now < n2:
            self.line(1, now)
        now = now - n2
        if 0 <= now and now < (1 if n1 == 2 else n1):
            self.line(0, now)

    def stage_ref(self, stage, index):
        if stage == 2:
            return self.block(slice(None), slice(None), index)
        if stage == 1:
            return self.block(slice(None), index, self.me[2])
        return self.block(index, self.me[1], self.me[2])

    def buffers(self, stage):
        if stage == 2:
            return self.from_third, self.third_sems.at[0, :, 0], self.third_sems.at[1, :, 0]
        if stage == 1:
            return self.from_second, self.second_sems.at[0], self.second_sems.at[1]
        return self.from_first, self.first_sems.at[0], self.first_sems.at[1]

    def absorb(self, stage, index, buffer_slot):
        buffer, sems = (
            (self.from_third, lambda s: self.third_sems.at[1, s, 0]),
            (self.from_second, lambda s: self.second_sems.at[1, s]),
            (self.from_first, lambda s: self.first_sems.at[1, s]),
        )[2 - stage]
        self.arrived(sems(buffer_slot), buffer.at[buffer_slot])
        target = self.stage_ref(stage, index)
        source = buffer.at[buffer_slot]
        self.add_all(target, source)

    def add_all(self, target, source):
        lead = target.shape[:-2]
        count = 1
        for size in lead:
            count *= size

        def add(index):
            at, rest = (), index
            for size in reversed(lead):
                at = (lax.rem(rest, size),) + at
                rest = rest // size
            self.add_rows(target, source, at)

        if count == 1 and not lead:
            self.add_rows(target, source, ())
        else:
            loop(count, add)

    def third_ready(self, second):
        if not self.pair:
            return
        self.arrived(self.third_sems.at[1, 0, second], self.from_third.at[0, second])
        self.add_all(self.block(slice(None), second, self.me[2]), self.from_third.at[0, second])

    def line(self, stage, now):
        size, here = self.n[stage], self.me[stage]
        sems = (self.first_sems, self.second_sems, None)[stage]
        send_sem = lambda s: self.third_sems.at[0, s, 0] if stage == 2 else sems.at[0, s]
        recv_sem = lambda s: self.third_sems.at[1, s, 0] if stage == 2 else sems.at[1, s]
        buffer = (self.from_first, self.from_second, self.from_third)[stage]
        if size == 2:
            if stage == 1:
                if now == 0:
                    for second in range(2):
                        self.third_ready(second)
                    self.send(stage, send_sem(0), self.stage_ref(stage, 1 - here), buffer.at[0], 1 - here, recv_sem(0))
                if now == 1:
                    self.absorb(stage, here, 0)
                    self.start_first()
            if stage == 0:
                self.arrived(recv_sem(0), buffer.at[0])
                self.finish(buffer.at[0])
            return
        if now < size - 1:
            up = size - 1 - now + here
            goes_up = jnp.logical_and(here <= now, here < size - 1)

            def go_up():
                if stage == 1:
                    self.third_ready(up)
                pl.when(here > 0)(lambda: self.absorb(stage, up, up))

            up = jnp.minimum(up, size - 1)
            pl.when(goes_up)(go_up)
            self.send(stage, send_sem(up), self.stage_ref(stage, up), buffer.at[up], here + 1, recv_sem(up), goes_up)
            down = jnp.maximum(now + here - (size - 1), 0)
            goes_down = jnp.logical_and(size - 1 - here <= now, here > 0)

            def go_down():
                if stage == 1:
                    self.third_ready(down)
                pl.when(here < size - 1)(lambda: self.absorb(stage, down, down))

            pl.when(goes_down)(go_down)
            self.send(stage, send_sem(down), self.stage_ref(stage, down), buffer.at[self.down_slot(stage, down)],
                      here - 1, recv_sem(self.down_slot(stage, down)), goes_down)
            return
        if stage == 1:
            self.third_ready(here)
        pl.when(here > 0)(lambda: self.absorb(stage, here, here))
        pl.when(here < size - 1)(lambda: self.absorb(stage, here, size))
        if stage == 1:
            self.start_first()
        if stage == 0:
            self.finish(None)

    def down_slot(self, stage, target):
        here, size = self.me[stage], self.n[stage]
        return jnp.where(target == here - 1, size, target)

    def start_first(self):
        if self.n[0] == 2:
            other = 1 - self.me[0]
            self.send(0, self.first_sems.at[0, 0], self.stage_ref(0, other), self.from_first.at[0], other,
                      self.first_sems.at[1, 0])

    def finish(self, extra):
        own = self.stage_ref(0, self.me[0])

        def step(i):
            rows = at_rows(i, 16)
            value = own[rows, :].astype(jnp.float32)
            if extra is not None:
                value = value + extra[rows, :].astype(jnp.float32)
            self.out[pl.ds(pl.multiple_of(self.rows.start + i * 16, 16), 16), :] = value

        loop(own.shape[0] // 16, step)

    def finish_send(self):
        self.core_copy().wait_send()
        for condition, copy in self.sent:
            when(condition, lambda copy=copy: copy().wait_send())


def split_plan(heights, parts_of, orders_of):
    plan = []
    for index, height in enumerate(heights):
        parts = min(parts_of, height // 16)
        rows = height // parts
        for part in range(parts):
            plan.append((index, part * rows, rows, orders_of(index)[part]))
    return plan


def piece_events(pieces, offsets, skew):
    events = []
    for i, piece in enumerate(pieces):
        for e in range(piece.ticks + 1):
            own = offsets[piece.order[2]]
            when_at = own[e] if e < len(own) else own[-1] + e - len(own) + 1
            events.append((when_at + i * skew, i, e))
    events.sort()
    return [functools.partial(pieces[i].tick, e) for _, i, e in events]


LATE = (0, 1, 6, 7, 8, 9, 10)
OFFSETS = {"x": LATE, "y": LATE, "z": (0, 1, 2, 3, 4, 5, 6, 7, 8)}
PER_PIECE = 9


def weight_orders(index):
    third = ("x", "z", "y") if index % 2 == 0 else ("y", "z", "x")
    first = ("x", "y", "z") if index % 2 == 0 else ("y", "x", "z")
    return (("z", "x", "y"), ("z", "y", "x"), first, third)


def reduce_plan(partials, seq_count, dp_count, parts=4):
    sizes = (dp_count, 4, seq_count // 8)
    blocked, outs, scratch = [], [], []
    for p in partials:
        rows = p.shape[1] // seq_count
        blocked.append(p.reshape(sizes + (2, rows, p.shape[2])))
        outs.append(jax.ShapeDtypeStruct((rows, p.shape[2]), jnp.float32))
    plan = split_plan([o.shape[0] for o in outs], parts, weight_orders)
    for index, first, rows, order in plan:
        bufs, sems = Reduce.scratch(
            order, sizes, rows, outs[index].shape[1], partials[index].dtype
        )
        scratch += bufs + sems
    return plan, blocked, outs, scratch


def reduce_pieces(place, plan, partials, outs, scratch):
    pieces = []
    for number, (index, first, rows, order) in enumerate(plan):
        own = scratch[PER_PIECE * number : PER_PIECE * number + PER_PIECE]
        pieces.append(Reduce(place, order, partials[index], pl.ds(first, rows), outs[index], own[:5], own[5:]))
    return pieces


def reduce_kernel(seq_count, dp_count, plan, count, *refs):
    partials, outs, rest = refs[:count], refs[count : 2 * count], refs[2 * count :]
    place = Place(seq_count, dp_count)
    entry_barrier(place)
    pieces = reduce_pieces(place, plan, partials, outs, rest)
    for event in piece_events(pieces, OFFSETS, 0):
        event()
    for piece in pieces:
        piece.finish_send()


def reduce_all(partials, seq_count, dp_count, collective_id):
    plan, blocked, outs, scratch = reduce_plan(partials, seq_count, dp_count)
    return pl.pallas_call(
        functools.partial(reduce_kernel, seq_count, dp_count, plan, len(partials)),
        out_shape=outs,
        in_specs=hbm(len(partials)),
        out_specs=vmem(len(partials)),
        scratch_shapes=scratch,
        compiler_params=pltpu.CompilerParams(
            collective_id=collective_id, has_side_effects=True, vmem_limit_bytes=VMEM_LIMIT
        ),
        name="reduce_gradients",
    )(*blocked)


class Exchange:
    def __init__(self, place, src, dst, sems, micro, seq_count, forward):
        self.place, self.src, self.dst, self.sems = place, src, dst, sems
        self.micro, self.count, self.forward = micro, seq_count, forward
        self.each = src.shape[0] // (micro * seq_count)
        self.me = lax.axis_index("seq")

    def indices(self, peer):
        frames = self.count * self.each
        out = []
        for micro in range(self.micro):
            for f in range(self.each):
                by_frame = (micro * self.each + f) * self.count
                if self.forward:
                    out.append((by_frame + peer, micro * frames + self.me * self.each + f))
                else:
                    out.append((micro * frames + peer * self.each + f, by_frame + self.me))
        return out

    def greet(self):
        barrier = pltpu.get_barrier_semaphore()

        def one(step):
            peer = lax.rem(self.me + step + 1, self.count)
            pl.semaphore_signal(
                barrier, inc=1, device_id=(lax.axis_index("dp"), peer), device_id_type=MESH
            )

        loop(self.count - 1, one)
        return self.count - 1

    def start(self):
        for here, there in self.indices(self.me):
            pltpu.make_async_copy(self.src.at[here], self.dst.at[there], self.sems.at[2]).start()

        def one(step):
            peer = lax.rem(self.me + step + 1, self.count)
            for here, there in self.indices(peer):
                pltpu.make_async_remote_copy(
                    src_ref=self.src.at[here], dst_ref=self.dst.at[there],
                    send_sem=self.sems.at[0], recv_sem=self.sems.at[1],
                    device_id=(lax.axis_index("dp"), peer), device_id_type=MESH,
                ).start()

        loop(self.count - 1, one)

    def finish(self):
        own = self.micro * self.each
        most = self.dst.at[pl.ds(0, own * (self.count - 1))]
        pltpu.make_async_copy(most, most, self.sems.at[1]).wait()
        pltpu.make_async_copy(most, most, self.sems.at[0]).wait()
        few = self.dst.at[pl.ds(0, own)]
        pltpu.make_async_copy(few, few, self.sems.at[2]).wait()


def attend_backward_kernel(spatial, tokens, micro, seq_count, dp_count, plan, counts, ratio, *refs):
    fronts, count, outs_count = counts
    refs = list(refs)
    take = lambda n: [refs.pop(0) for _ in range(n)]
    if spatial:
        up, stream, extra, gain, shift = take(5)
    else:
        (up, stream, gain, shift), extra = take(4), None
    packed_h, probs_h, mixed, w_in_h, w_out_h = take(5)
    partials = take(count)
    arrived = None if spatial else take(1)[0]
    down, w_in_grad, w_out_grad, gain_out, shift_out = take(5) if spatial else [None] + take(4)
    sums = take(1)[0] if spatial else None
    outs = take(count)
    own = take(12)
    if not spatial:
        down = take(1)[0]
        change_sems = take(1)[0]
    place = Place(seq_count, dp_count)
    change = None if spatial else Exchange(place, down, arrived, change_sems, micro, seq_count, False)
    entry_barrier(place, change)
    pieces = reduce_pieces(place, plan, partials, outs, refs)
    work = attend_backward_work(
        spatial, tokens, up, stream, extra, gain, shift, packed_h, probs_h, mixed, w_in_h, w_out_h,
        down, w_in_grad, w_out_grad, gain_out, shift_out, sums, *own
    )

    def all_work():
        yield from work
        if change is not None:
            change.start()
            yield

    weave(all_work(), piece_events(pieces, OFFSETS, 0), ratio)
    if change is not None:
        change.finish()
    for piece in pieces:
        piece.finish_send()


def attend_backward(spatial, tokens, block, micro, seq_count, dp_count, partials, ratio, collective_id,
                    up, stream, extra, gain, shift, packed, probs, mixed, w_in, w_out):
    total, width = stream.shape
    low, full = jnp.bfloat16, jnp.float32
    shape = jax.ShapeDtypeStruct
    plan, blocked, sums_out, scratch = reduce_plan(partials, seq_count, dp_count)
    down = shape((total // block, block, width), low)
    outs = [
        down,
        shape(w_in.shape, low),
        shape(w_out.shape, low),
        shape((1, width), full),
        shape((1, width), full),
    ]
    specs = (vmem(1) if spatial else hbm(1)) + hbm(2) + vmem(2)
    if spatial:
        outs.append(shape((total // tokens, width), full))
        specs += vmem(1)
    front = (up, stream) + ((extra,) if spatial else ()) + (gain, shift)
    own = [
        pltpu.VMEM((total, width), low),
        pltpu.VMEM((total, width), low),
        pltpu.VMEM((total, width), low),
        pltpu.VMEM((total, 3 * width), low),
        pltpu.VMEM((total, width), full),
        pltpu.VMEM(packed.shape, low),
        pltpu.VMEM(probs.shape, low),
        pltpu.VMEM(w_in.shape, low),
        pltpu.VMEM(w_out.shape, low),
        pltpu.VMEM((2, dp_count, 128, w_in.shape[2]), low),
        pltpu.VMEM((2, dp_count, 128, w_out.shape[2]), low),
        pltpu.SemaphoreType.DMA((8,)),
    ]
    if not spatial:
        own += [pltpu.VMEM(down.shape, low), pltpu.SemaphoreType.DMA((3,))]
    result = pl.pallas_call(
        functools.partial(
            attend_backward_kernel, spatial, tokens, micro, seq_count, dp_count, plan,
            (len(front), len(partials), len(outs)), ratio,
        ),
        out_shape=tuple(outs + sums_out),
        in_specs=vmem(len(front)) + hbm(2) + vmem(1) + hbm(2) + hbm(len(partials)),
        out_specs=specs + vmem(len(partials)),
        scratch_shapes=own + scratch,
        compiler_params=pltpu.CompilerParams(
            collective_id=collective_id, has_side_effects=True, vmem_limit_bytes=VMEM_LIMIT
        ),
        name="space_backward" if spatial else "time_backward",
    )(*front, packed, probs, mixed, w_in, w_out, *blocked)
    return result[: len(outs)], result[len(outs) :]


ACTIONS = 8
FRAMES = 16


def body(
    frames_in,
    cotangent,
    lengths,
    actions,
    spatial_in,
    spatial_out,
    temporal_in,
    temporal_out,
    hidden_in,
    hidden_out,
    norm_gains,
    norm_shifts,
    bias_up,
    bias_down,
    action_table,
):
    seq_count, dp_count = lax.axis_size("seq"), lax.axis_size("dp")
    micro, frame_count, spatial, width = frames_in.shape
    tokens = micro * frame_count * spatial
    frames = seq_count * frame_count
    places = spatial // seq_count
    group = frames * places
    cut = norm_gains.shape[1]
    low, full = jnp.bfloat16, jnp.float32

    up_rows = bias_up.shape[0] // cut
    small = jnp.concatenate(
        [norm_gains, norm_shifts, action_table, bias_down[None], bias_up.reshape(up_rows, cut)], axis=0
    )
    used = small.shape[0]
    small = jnp.pad(small, ((0, 32 - used), (0, 128 - cut)))
    shards = [spatial_in, spatial_out, temporal_in, temporal_out, hidden_in, hidden_out, small]
    wholes = gather_all(shards, seq_count, dp_count, skew=0, collective_id=1)
    weights = [
        whole.reshape(dp_count, shard.shape[0] * seq_count, shard.shape[1])
        for whole, shard in zip(wholes[:6], shards)
    ]
    w_sin, w_sout, w_tin, w_tout, w_hin, w_hout = weights
    small = wholes[6][0].reshape(seq_count, 32, 128)[:, :, :cut].astype(full)
    rows = small[:, : used - up_rows].transpose(1, 0, 2).reshape(used - up_rows, width)
    gain, shift = [rows[i : i + 1] for i in range(3)], [rows[i : i + 1] for i in range(3, 6)]
    table, down_bias = rows[6:14], rows[14:15]
    up_bias = small[:, used - up_rows : used].reshape(1, -1)

    at = jnp.arange(group, dtype=jnp.int32)
    frame, place = at // places, at % places
    video, frame = frame // FRAMES, frame % FRAMES
    span = lengths[:, video]
    alive = frame[None] < span
    allowed = (
        (place[:, None] == place[None]) & (video[:, None] == video[None]) & (frame[:, None] <= frame[None])
    )[None] & alive[:, :, None]
    allowed = allowed.astype(full)
    live = alive.astype(full).reshape(tokens, 1)
    onehot = (actions.reshape(-1)[:, None] == jnp.arange(ACTIONS)[None, :]).astype(full)
    row_pair = jnp.dot(onehot, table, precision=lax.Precision.HIGHEST)

    def to_places(value):
        value = value.reshape(micro, frame_count, seq_count, places, width)
        value = lax.all_to_all(value, "seq", split_axis=2, concat_axis=2, tiled=True)
        return value.transpose(0, 2, 1, 3, 4).reshape(tokens, width)

    def to_frames(value):
        value = value.reshape(micro, seq_count, frame_count, places, width)
        value = lax.all_to_all(value, "seq", split_axis=1, concat_axis=1, tiled=True)
        return value.transpose(0, 2, 1, 3, 4).reshape(tokens, width)

    frames_flat = frames_in.reshape(tokens, width)
    end_grad = to_places(cotangent)
    stream_one, packed_one, probs_one, mixed_one = attend_forward(
        True, spatial, frames_flat, row_pair, gain[0], shift[0], w_sin, w_sout
    )
    stream_one = to_places(stream_one)
    stream_two, packed_two, probs_two, mixed_two = attend_forward(
        False, group, stream_one, allowed, gain[1], shift[1], w_tin, w_tout
    )
    out, two_grad, hin_grad, hout_grad, gain_three, shift_three, up_grad, down_grad = hidden_layer(
        stream_two, end_grad, live, gain[2], shift[2], up_bias, down_bias, w_hin, w_hout
    )
    layer_out = to_frames(out).reshape(frames_in.shape)
    (one_grad, tin_grad, tout_grad, gain_two, shift_two), hidden_sums = attend_backward(
        False, group, places, micro, seq_count, dp_count, [hin_grad, hout_grad], 0.5, 2,
        two_grad, stream_one, None, gain[1], shift[1], packed_two, probs_two, mixed_two, w_tin, w_tout,
    )
    one_grad = one_grad.reshape(tokens, width)
    (in_grad, sin_grad, sout_grad, gain_one, shift_one, sums), time_sums = attend_backward(
        True, spatial, 16, micro, seq_count, dp_count, [tin_grad, tout_grad], 0.5, 3,
        one_grad, frames_flat, row_pair, gain[0], shift[0], packed_one, probs_one, mixed_one, w_sin, w_sout,
    )
    table_grad = lax.dot_general(onehot, sums, (((0,), (0,)), ((), ())), precision=lax.Precision.HIGHEST)

    rows = jnp.concatenate(
        [gain_one, gain_two, gain_three, shift_one, shift_two, shift_three, table_grad, down_grad], axis=0
    )
    rows = rows.reshape(used - up_rows, seq_count, cut).transpose(1, 0, 2)
    rows = jnp.concatenate([rows, up_grad.reshape(seq_count, up_rows, cut)], axis=1)
    rows = jnp.pad(rows, ((0, 0), (0, 32 - used), (0, 128 - cut))).astype(low).reshape(1, seq_count * 32, 128)
    rows = jnp.broadcast_to(rows, (dp_count,) + rows.shape[1:])
    space_sums = reduce_all([sin_grad, sout_grad, rows], seq_count, dp_count, collective_id=4)
    small = space_sums[2][:, :cut]
    return (
        layer_out,
        in_grad.reshape(frames_in.shape),
        *space_sums[:2],
        *time_sums,
        *hidden_sums,
        small[0:3],
        small[3:6],
        small[15:used].reshape(-1),
        small[14],
        small[6:14],
    )


def solution(mesh):
    rows = P(None, ("dp", "seq"), None, None)
    matrix = P("seq", "dp")
    cut = P(None, "seq")
    in_specs = (rows, rows, P(None, "dp"), P(None, ("dp", "seq"))) + (matrix,) * 6 + (cut, cut, P("seq"), P("seq"), cut)
    out_specs = (rows, rows) + (matrix,) * 6 + (cut, cut, P("seq"), P("seq"), cut)
    return jax.shard_map(body, mesh=mesh, in_specs=in_specs, out_specs=out_specs, check_vma=False)
```

```python
import functools
import jax
import jax.numpy as jnp
from jax import lax
from jax.experimental import pallas as pl
from jax.experimental.pallas import tpu as pltpu
from jax.sharding import PartitionSpec as P

MESH = pl.DeviceIdType.MESH


class Place:
    def __init__(self, seq_count, dp_count):
        self.size = {"z": 4, "x": seq_count // 8, "y": dp_count}
        seq = lax.axis_index("seq")
        self.core = lax.rem(seq, 2)
        self.at = {
            "z": seq // (2 * self.size["x"]),
            "x": lax.rem(seq // 2, self.size["x"]),
            "y": lax.axis_index("dp"),
        }

    def device(self, core=None, **moved):
        at = dict(self.at, **moved)
        core = self.core if core is None else core
        return (at["y"], (at["z"] * self.size["x"] + at["x"]) * 2 + core)

    def sibling(self):
        return self.device(core=1 - self.core)


def when(condition, action):
    if condition is True:
        action()
    elif condition is not False:
        pl.when(condition)(action)


def entry_barrier(place, change=None):
    barrier = pltpu.get_barrier_semaphore()

    def greet(device):
        pl.semaphore_signal(barrier, inc=1, device_id=device, device_id_type=MESH)

    count = 1
    if change is not None:
        count = count + change.greet()
    greet(place.sibling())
    for axis in ("x", "y", "z"):
        here, size = place.at[axis], place.size[axis]
        if size == 2:
            greet(place.device(**{axis: 1 - here}))
            count = count + 1
            continue
        pl.when(here > 0)(lambda axis=axis, here=here: greet(place.device(**{axis: here - 1})))
        pl.when(here < size - 1)(lambda axis=axis, here=here: greet(place.device(**{axis: here + 1})))
        count = count + (here > 0).astype(jnp.int32) + (here < size - 1).astype(jnp.int32)
    pl.semaphore_wait(barrier, count)


def line_steps(here, size, distance):
    if size == 2:
        return [(1 - here, True, False, 0)]
    return [
        (here - distance, here - distance >= 0, here < size - 1, 1),
        (here + distance, here + distance < size, here > 0, -1),
    ]


class Gather:
    def __init__(self, place, order, shard, whole, rows, sems):
        self.place, self.order = place, order
        self.shard, self.whole, self.rows = shard, whole, rows
        self.n = [place.size[axis] for axis in order]
        self.me = [place.at[axis] for axis in order]
        self.recv, self.send, self.sib_send, self.sib_recv, self.own_sem = sems
        self.sent = []
        n1, n2, n3 = self.n
        self.ticks = n1 - 1 + n2 + max(n3 - 1, 1)

    @staticmethod
    def sem_shapes(n):
        n1, n2, n3 = n
        count = n1 + n2 + n2 * n3
        return (
            pltpu.SemaphoreType.DMA((count,)),
            pltpu.SemaphoreType.DMA((2, count)),
            pltpu.SemaphoreType.DMA((n2, n3)),
            pltpu.SemaphoreType.DMA((n2, n3)),
            pltpu.SemaphoreType.DMA((1,)),
        )

    def block(self, first, second, third, core=None):
        at = dict(zip(self.order, (first, second, third)))
        core = self.place.core if core is None else core
        return self.whole.at[at["y"], at["z"], at["x"], core, self.rows]

    def own(self):
        return pltpu.make_async_copy(
            self.shard.at[self.rows], self.block(*self.me), self.own_sem.at[0]
        )

    def pass_on(self, stage, slot, src, dst, direction, condition):
        axis, here = self.order[stage], self.me[stage]
        target = self.place.device(**{axis: here + direction})
        sem = self.send.at[(direction + 1) // 2, slot]

        def copy():
            return pltpu.make_async_remote_copy(
                src_ref=src, dst_ref=dst, send_sem=sem, recv_sem=self.recv.at[slot],
                device_id=target, device_id_type=MESH,
            )

        when(condition, lambda: copy().start())
        self.sent.append((condition, copy))

    def spread(self, stage, slot, src, dst):
        here, size = self.me[stage], self.n[stage]
        if size == 2:
            axis = self.order[stage]
            target = self.place.device(**{axis: 1 - here})

            def copy():
                return pltpu.make_async_remote_copy(
                    src_ref=src, dst_ref=dst, send_sem=self.send.at[0, slot],
                    recv_sem=self.recv.at[slot], device_id=target, device_id_type=MESH,
                )

            copy().start()
            self.sent.append((True, copy))
            return
        self.pass_on(stage, slot, src, dst, 1, here < size - 1)
        self.pass_on(stage, slot, src, dst, -1, here > 0)

    def arrive(self, slot, ref):
        pltpu.make_async_copy(ref, ref, self.recv.at[slot]).wait()

    def to_sibling(self, second, third):
        ref = self.block(slice(None), second, third)

        def copy():
            return pltpu.make_async_remote_copy(
                src_ref=ref, dst_ref=ref, send_sem=self.sib_send.at[second, third],
                recv_sem=self.sib_recv.at[second, third],
                device_id=self.place.sibling(), device_id_type=MESH,
            )

        return copy

    def hand(self, second, third, condition=True):
        copy = self.to_sibling(second, third)
        when(condition, lambda: copy().start())

    def tick(self, now):
        n1, n2, n3 = self.n
        me1, me2, me3 = self.me
        if now == 0:
            self.own().start()
            src = self.shard.at[self.rows]
            self.spread(0, me1, src, self.block(*self.me))
        if 1 <= now <= n1 - 1:
            for index, here, go, way in line_steps(me1, n1, now):
                self.step_one(index, here, go, way)
        base = n1 - 1
        if now == base:
            self.own().wait()
            self.group_ready(me2)
            ref = self.block(slice(None), me2, me3)
            self.spread(1, n1 + me2, ref, ref)
        for distance in range(1, n2):
            if now == base + distance:
                for index, here, go, way in line_steps(me2, n2, distance):
                    self.step_two(index, here, go, way)
        for far in range(1, n3):
            for distance in range(0, n2):
                if now == base + distance + far:
                    choices = [(me2, True)] if distance == 0 else [
                        (index, here) for index, here, _, _ in line_steps(me2, n2, distance)
                    ]
                    for second, there in choices:
                        for index, here, go, way in line_steps(me3, n3, far):
                            self.step_three(second, there, index, here, go, way)

    def step_one(self, index, here, go, way):
        ref = self.block(index, *self.me[1:])
        both = here if go is True or go is False else jnp.logical_and(here, go)

        when(here, lambda: self.arrive(index, ref))
        if go is not False:
            self.pass_on(0, index, ref, ref, way, both)

    def group_ready(self, second, condition=True):
        self.hand(second, self.me[2], condition)
        ref = self.block(slice(None), second, self.me[2])
        slot = self.n[0] + self.n[1] + second * self.n[2] + self.me[2]
        if condition is True:
            self.spread(2, slot, ref, ref)
            return
        here, size = self.me[2], self.n[2]
        if size == 2:
            axis = self.order[2]
            target = self.place.device(**{axis: 1 - here})

            def copy():
                return pltpu.make_async_remote_copy(
                    src_ref=ref, dst_ref=ref, send_sem=self.send.at[0, slot],
                    recv_sem=self.recv.at[slot], device_id=target, device_id_type=MESH,
                )

            when(condition, lambda: copy().start())
            self.sent.append((condition, copy))
            return
        self.pass_on(2, slot, ref, ref, 1, jnp.logical_and(condition, here < size - 1))
        self.pass_on(2, slot, ref, ref, -1, jnp.logical_and(condition, here > 0))

    def step_two(self, index, here, go, way):
        slot = self.n[0] + index
        ref = self.block(slice(None), index, self.me[2])
        when(here, lambda: self.arrive(slot, ref))
        if go is not False:
            both = here if go is True else jnp.logical_and(here, go)
            self.pass_on(1, slot, ref, ref, way, both)
        self.group_ready(index, here)

    def step_three(self, second, there, index, here, go, way):
        slot = self.n[0] + self.n[1] + second * self.n[2] + index
        ref = self.block(slice(None), second, index)
        here = here if there is True else (there if here is True else jnp.logical_and(here, there))
        when(here, lambda: self.arrive(slot, ref))
        if go is not False:
            both = here if go is True else (go if here is True else jnp.logical_and(here, go))
            self.pass_on(2, slot, ref, ref, way, both)
        self.hand(second, index, here)

    def finish_recv(self):
        other = 1 - self.place.core
        for second in range(self.n[1]):
            for third in range(self.n[2]):
                ref = self.block(slice(None), second, third, core=other)
                pltpu.make_async_copy(ref, ref, self.sib_recv.at[second, third]).wait()

    def finish_send(self):
        for condition, copy in self.sent:
            when(condition, lambda copy=copy: copy().wait_send())
        for second in range(self.n[1]):
            for third in range(self.n[2]):
                self.to_sibling(second, third)().wait_send()


def split_plan(heights, parts_of, orders_of):
    plan = []
    for index, height in enumerate(heights):
        parts = min(parts_of, height // 16)
        rows = height // parts
        for part in range(parts):
            plan.append((index, part * rows, rows, orders_of(index)[part]))
    return plan


def gather_orders(index):
    if index % 2 == 0:
        return (("x", "z", "y"), ("y", "z", "x"))
    return (("z", "x", "y"), ("z", "y", "x"))


PER_GATHER = 5


def gather_plan(shards, seq_count, dp_count, parts=2):
    size = {"z": 4, "x": seq_count // 8, "y": dp_count}
    plan = split_plan([s.shape[0] for s in shards], parts, gather_orders)
    scratch = []
    for _, _, _, order in plan:
        scratch += list(Gather.sem_shapes([size[a] for a in order]))
    outs = [jax.ShapeDtypeStruct((dp_count, 4, size["x"], 2) + s.shape, s.dtype) for s in shards]
    return plan, outs, scratch


def gather_pieces(place, plan, shards, wholes, scratch):
    pieces = []
    for number, (index, first, rows, order) in enumerate(plan):
        pieces.append(
            Gather(place, order, shards[index], wholes[index], pl.ds(first, rows),
                   scratch[PER_GATHER * number : PER_GATHER * number + PER_GATHER])
        )
    return pieces

D_EPS = 1e-05
NEG = -1e30
HEADS = 16
HDIM = 64
SCALE = HDIM ** (-0.5)
NT = (((1,), (1,)), ((), ()))
TN = (((0,), (0,)), ((), ()))
ROWS = 32
VMEM_LIMIT = 63 * 1024 * 1024


def dot(left, right, dims=(((1,), (0,)), ((), ()))):
    return lax.dot_general(left, right, dims, preferred_element_type=jnp.float32)


def tile_of(size, largest=512):
    return max(t for t in (128, 256, 384, 512, 1024) if t <= largest and size % t == 0)


def loop(count, action):
    def step(index, carry):
        action(index)
        return carry

    lax.fori_loop(0, count, step, 0)


def at_rows(index, size):
    return pl.ds(pl.multiple_of(index * size, size), size)


def moments(value):
    width = value.shape[-1]
    centre = jnp.sum(value, axis=-1, keepdims=True) * (1.0 / width)
    offset = value - centre
    spread = jnp.sum(offset * offset, axis=-1, keepdims=True) * (1.0 / width)
    return offset, lax.rsqrt(spread + D_EPS)


def norm_forward(read, gain, shift, out):
    def step(index):
        rows = at_rows(index, ROWS)
        offset, rate = moments(read(rows))
        out[rows, :] = (offset * rate * gain[...] + shift[...]).astype(jnp.bfloat16)

    loop(out.shape[0] // ROWS, step)


def fold8(value):
    return jnp.sum(value.reshape(-1, 8, value.shape[-1]), axis=0)


def norm_backward(read, gain, grad, upstream, write, gain_out, shift_out):
    tokens, width = grad.shape

    def step(index, carry):
        gain_sum, shift_sum = carry
        rows = at_rows(index, ROWS)
        offset, rate = moments(read(rows))
        unit = offset * rate
        dy = grad[rows, :]
        gain_sum = gain_sum + fold8(dy * unit)
        shift_sum = shift_sum + fold8(dy)
        scaled = dy * gain[...]
        mean = jnp.sum(scaled, axis=-1, keepdims=True) * (1.0 / width)
        slope = jnp.sum(scaled * unit, axis=-1, keepdims=True) * (1.0 / width)
        write(index, rows, upstream(rows) + rate * (scaled - mean - unit * slope))
        return gain_sum, shift_sum

    zero = jnp.zeros((8, width), jnp.float32)
    gain_sum, shift_sum = lax.fori_loop(0, tokens // ROWS, step, (zero, zero))
    gain_out[...] = jnp.sum(gain_sum, axis=0, keepdims=True)
    shift_out[...] = jnp.sum(shift_sum, axis=0, keepdims=True)


def chunks(count, step, units):
    units = max(u for u in range(1, min(units, count) + 1) if count % u == 0)
    each = count // units
    for unit in range(units):
        loop(each, lambda index, unit=unit: step(unit * each + index))
        yield


def drain(work):
    for _ in work:
        pass


def project(rows, weight, emit, tile_max=512, units=1):
    parts, _, size = weight.shape
    tile = tile_of(size, tile_max)
    for part in range(parts):

        def step(index, part=part):
            inner = at_rows(index, tile)
            columns = pl.ds(pl.multiple_of(part * size + index * tile, 128), tile)
            emit(columns, dot(rows[...], weight[part, :, inner]))

        yield from chunks(size // tile, step, units)


def project_back(grad, weight, emit, tile_max=512, units=1):
    parts, depth, size = weight.shape
    tile = tile_of(depth, tile_max)

    def step(index):
        inner = at_rows(index, tile)
        total = None
        for part in range(parts):
            term = dot(grad[:, part * size : (part + 1) * size], weight[part, inner, :], NT)
            total = term if total is None else total + term
        emit(inner, total)

    yield from chunks(depth // tile, step, units)


def outer(rows, grad, out, stage, sems, units=1):
    parts, _, across, _, size_r, size = out.shape
    chips = stage.shape[2]
    tile = chips * 2 * size_r

    def leave(index, slot):
        first = index * chips
        return pltpu.make_async_copy(
            stage.at[slot], out.at[:, first // across, pl.ds(lax.rem(first, across), chips)], sems.at[slot]
        )

    def step(index):
        slot = lax.rem(index, 2)
        pl.when(index >= 2)(lambda: leave(index - 2, slot).wait())
        left = rows[:, at_rows(index, tile)]
        for part in range(parts):
            value = dot(left, grad[:, part * size : (part + 1) * size], TN)
            stage[slot, part] = value.reshape(chips, 2, size_r, size).astype(out.dtype)
        leave(index, slot).start()

    count = rows.shape[1] // tile
    yield from chunks(count, step, units)
    leave(count - 2, (count - 2) % 2).wait()
    leave(count - 1, (count - 1) % 2).wait()


def head_mask(shape, axis, head):
    lane = lax.broadcasted_iota(jnp.int32, shape, axis)
    return (lane // HDIM) == head


def pick(value, head):
    return jnp.where(head_mask(value.shape, 1, head), value, jnp.zeros_like(value))


def pick_rows(value, head):
    return jnp.where(head_mask(value.shape, 0, head), value, jnp.zeros_like(value))


def pair_slices(index, width, tokens):
    pairs = width // 128
    micro, pair = index // pairs, lax.rem(index, pairs)
    rows = pl.ds(pl.multiple_of(micro * tokens, tokens), tokens)
    return micro, rows, [
        pl.ds(pl.multiple_of(part * width + pair * 128, 128), 128) for part in range(3)
    ]


def attention_forward(packed, allowed, probs, mixed, tokens, units=1):
    width = mixed.shape[1]

    def step(index):
        micro, rows, (q_at, k_at, v_at) = pair_slices(index, width, tokens)
        queries = packed[rows, q_at] * jnp.bfloat16(SCALE)
        keys, values = packed[rows, k_at], packed[rows, v_at]
        values_t = values.astype(jnp.float32).T.astype(jnp.bfloat16)
        total = None
        for head in range(2):
            scores = dot(keys, pick(queries, head), NT)
            if allowed is not None:
                scores = jnp.where(allowed[micro] > 0, scores, NEG)
            raised = jnp.exp(scores - jnp.max(scores, axis=0, keepdims=True))
            prob = raised * (1.0 / jnp.sum(raised, axis=0, keepdims=True))
            prob = prob.astype(jnp.bfloat16)
            probs[2 * index + head] = prob
            term = dot(pick_rows(values_t, head), prob)
            total = term if total is None else total + term
        mixed[rows, q_at] = total.T.astype(jnp.bfloat16)

    yield from chunks(mixed.shape[0] // tokens * (width // 128), step, units)


def attention_backward(packed, probs, grad, packed_grad, tokens, units=1):
    width = grad.shape[1]

    def step(index):
        _, rows, (q_at, k_at, v_at) = pair_slices(index, width, tokens)
        queries, keys, values = packed[rows, q_at], packed[rows, k_at], packed[rows, v_at]
        upstream = grad[rows, q_at]
        keys_t = keys.astype(jnp.float32).T.astype(jnp.bfloat16)
        query_grad = key_grad = value_grad = None
        for head in range(2):
            low = probs[2 * index + head]
            prob = low.astype(jnp.float32)
            up = pick(upstream, head)
            prob_grad = dot(values, up, NT)
            inner = jnp.sum(prob * prob_grad, axis=0, keepdims=True)
            score_grad = (prob * (prob_grad - inner) * SCALE).astype(jnp.bfloat16)
            terms = (
                dot(pick_rows(keys_t, head), score_grad),
                dot(score_grad, pick(queries, head)),
                dot(low, up),
            )
            if head == 0:
                query_grad, key_grad, value_grad = terms
            else:
                query_grad = query_grad + terms[0]
                key_grad = key_grad + terms[1]
                value_grad = value_grad + terms[2]
        packed_grad[rows, q_at] = query_grad.T.astype(jnp.bfloat16)
        packed_grad[rows, k_at] = key_grad.astype(jnp.bfloat16)
        packed_grad[rows, v_at] = value_grad.astype(jnp.bfloat16)

    yield from chunks(grad.shape[0] // tokens * (width // 128), step, units)


class Fetch:
    def __init__(self, src, dst, sem):
        self.copy = pltpu.make_async_copy(src, dst, sem)

    def start(self):
        self.copy.start()
        return self

    def wait(self):
        self.copy.wait()


def spatial_reader(frames, row_pair, tokens):
    def read(rows):
        micro = rows.start // tokens
        return frames[rows, :].astype(jnp.float32) + row_pair[pl.ds(micro, 1), :]

    return read


def attend_forward_work(read, base, allowed, gain, shift, v_in, v_out, ready_in, ready_out, put,
                        packed, probs, mixed, normed, tokens):
    norm_forward(read, gain, shift, normed)
    ready_in()
    yield

    def emit(columns, value):
        packed[:, columns] = value.astype(jnp.bfloat16)

    yield from project(normed, v_in, emit, units=3)
    yield from attention_forward(packed, allowed, probs, mixed, tokens, units=8)
    ready_out()

    def emit_out(columns, value):
        put(columns, base(columns) + value)

    yield from project(mixed, v_out, emit_out, units=2)


def vmem(count):
    return [pl.BlockSpec(memory_space=pltpu.VMEM)] * count


def hbm(count):
    return [pl.BlockSpec(memory_space=pltpu.HBM)] * count


def attend_backward_work(spatial, tokens, up, stream, extra, gain, shift, packed_h, probs_h, mixed, w_in_h, w_out_h,
                         down, w_in_grad, w_out_grad, gain_out, shift_out, sums,
                         up_low, mixed_grad, packed_grad, normed_grad, packed, probs, w_in, w_out,
                         in_stage, out_stage, sems):
    read = spatial_reader(stream, extra, tokens) if spatial else (lambda rows: stream[rows, :].astype(jnp.float32))
    fetches = [
        Fetch(src, dst, sems.at[i]).start()
        for i, (src, dst) in enumerate(
            ((w_out_h, w_out), (packed_h, packed), (probs_h, probs), (w_in_h, w_in))
        )
    ]

    def lower(index):
        rows = at_rows(index, ROWS)
        up_low[rows, :] = up[rows, :].astype(jnp.bfloat16)

    loop(up.shape[0] // ROWS, lower)
    yield
    fetches[0].wait()

    def emit_mixed(columns, value):
        mixed_grad[:, columns] = value.astype(jnp.bfloat16)

    yield from project_back(up_low, w_out, emit_mixed, units=2)
    yield from outer(mixed, up_low, w_out_grad, out_stage, sems.at[pl.ds(4, 2)], units=2)
    normed = up_low
    norm_forward(read, gain, shift, normed)
    yield
    fetches[1].wait()
    fetches[2].wait()
    yield from attention_backward(packed, probs, mixed_grad, packed_grad, tokens, units=8)
    fetches[3].wait()
    yield from outer(normed, packed_grad, w_in_grad, in_stage, sems.at[pl.ds(6, 2)], units=4)

    def emit_normed(columns, value):
        normed_grad[:, columns] = value

    yield from project_back(packed_grad, w_in, emit_normed, 256, units=4)
    block = down.shape[1]

    def put(index, value):
        down[pl.ds(index * (ROWS // block), ROWS // block)] = value.reshape(-1, block, value.shape[1]).astype(down.dtype)

    if spatial:
        sums[...] = jnp.zeros_like(sums)

        def write(index, rows, value):
            put(index, value)
            micro = rows.start // tokens
            sums[pl.ds(micro, 1), :] += jnp.sum(fold8(value), axis=0, keepdims=True)
    else:

        def write(index, rows, value):
            put(index, value)

    norm_backward(
        read, gain, normed_grad, lambda rows: up[rows, :].astype(jnp.float32), write, gain_out, shift_out
    )
    yield


END = object()


def weave(work, ticks, units, last=()):
    held = -1
    for now, events in enumerate(ticks):
        for event in events:
            event()
        for _ in range(units[min(now, len(units) - 1)]):
            if held > now:
                break
            step = next(work, END)
            held = -1 if step is END or step is None else last[step]
            if held <= now:
                held = -1
    drain(work)


GELU_A = 0.7978845608028654
GELU_B = 0.044715


def gelu_pair(value):
    square = value * value
    bent = jnp.tanh(GELU_A * value * (1.0 + GELU_B * square))
    half = 0.5 * (1.0 + bent)
    slope = half + 0.5 * value * (1.0 - bent * bent) * (GELU_A * (1.0 + 3.0 * GELU_B * square))
    return value * half, slope


def hidden_kernel(micro, seq_count, dp_count, stream, live, gain, shift, up_bias, down_bias, cotangent_h, w_up_h, w_down_h,
                  layer_out, down, up_grad_h, down_grad_h, gain_out, shift_out, up_bias_out, down_bias_out,
                  normed, end_low, active, slope, expand_low, normed_grad, w_up, w_down, up_stage, down_stage,
                  cotangent, out, sems, end_sems, home_sems):
    low = jnp.bfloat16
    place = Place(seq_count, dp_count)
    end = Exchange(place, cotangent_h, cotangent, end_sems, micro, seq_count, True)
    home = Exchange(place, out, layer_out, home_sems, micro, seq_count, False)
    exchange_barrier(end)
    end.start()
    block = out.shape[1]
    first = Fetch(w_up_h, w_up, sems.at[0]).start()
    second = Fetch(w_down_h, w_down, sems.at[1]).start()
    tokens, width = stream.shape
    parts = w_up.shape[0]
    norm_forward(lambda rows: stream[rows, :], gain, shift, normed)

    first.wait()

    def emit_expand(columns, value):
        act, rate = gelu_pair(value + up_bias[:, columns])
        active[:, columns] = act.astype(low)
        slope[:, columns] = rate.astype(low)

    drain(project(normed, w_up, emit_expand, 256))
    second.wait()

    def emit_out(columns, value):
        ended = stream[:, columns] + value + down_bias[:, columns]
        out[:, :, columns] = (ended * live[...]).astype(low).reshape(tokens // block, block, -1)

    drain(project(active, w_down, emit_out, 256))
    home.start()
    end.finish()

    def upstream(rows):
        part = cotangent[pl.ds(rows.start // block, ROWS // block)].astype(jnp.float32).reshape(ROWS, width)
        return part * live[rows, :]

    def lower(index, total):
        rows = at_rows(index, ROWS)
        value = upstream(rows)
        end_low[rows, :] = value.astype(low)
        return total + fold8(value)

    total = lax.fori_loop(0, tokens // ROWS, lower, jnp.zeros((8, width), jnp.float32))
    down_bias_out[...] = jnp.sum(total, axis=0, keepdims=True)

    def emit_active(columns, value):
        grad = value * slope[:, columns].astype(jnp.float32)
        up_bias_out[:, columns] = jnp.sum(grad, axis=0, keepdims=True)
        expand_low[:, columns] = grad.astype(low)

    drain(project_back(end_low, w_down, emit_active, 256))

    drain(outer(active, end_low, down_grad_h, down_stage, sems.at[pl.ds(2, 2)]))
    drain(outer(normed, expand_low, up_grad_h, up_stage, sems.at[pl.ds(4, 2)]))

    def emit_normed(columns, value):
        normed_grad[:, columns] = value

    drain(project_back(expand_low, w_up, emit_normed, 256))

    def write(index, rows, value):
        down[rows, :] = value

    norm_backward(lambda rows: stream[rows, :], gain, normed_grad, upstream, write, gain_out, shift_out)
    home.finish()


def blocks_of(weight, seq_count):
    parts, depth, size = weight.shape
    return jax.ShapeDtypeStruct((parts, 4, seq_count // 8, 2, depth // seq_count, size), jnp.bfloat16)


def stage_of(blocks):
    chips = max(1, 64 // blocks.shape[4])
    return pltpu.VMEM((2, blocks.shape[0], chips) + blocks.shape[3:], jnp.bfloat16)


def hidden_layer(micro, seq_count, dp_count, stream, live, gain, shift, up_bias, down_bias, cotangent, w_up, w_down):
    tokens, width = stream.shape
    hidden = up_bias.shape[1]
    parts = w_up.shape[0]
    low, full = jnp.bfloat16, jnp.float32
    shape = jax.ShapeDtypeStruct
    up_blocks, down_blocks = blocks_of(w_up, seq_count), blocks_of(w_down, seq_count)
    return pl.pallas_call(
        functools.partial(hidden_kernel, micro, seq_count, dp_count),
        out_shape=(
            shape(cotangent.shape, low),
            shape((tokens, width), full),
            up_blocks,
            down_blocks,
            shape((1, width), full),
            shape((1, width), full),
            shape((1, hidden), full),
            shape((1, width), full),
        ),
        in_specs=vmem(6) + hbm(3),
        out_specs=hbm(1) + vmem(1) + hbm(2) + vmem(4),
        scratch_shapes=[
            pltpu.VMEM((tokens, width), low),
            pltpu.VMEM((tokens, width), low),
            pltpu.VMEM((tokens, hidden), low),
            pltpu.VMEM((tokens, hidden), low),
            pltpu.VMEM((tokens, hidden), low),
            pltpu.VMEM((tokens, width), full),
            pltpu.VMEM(w_up.shape, low),
            pltpu.VMEM(w_down.shape, low),
            stage_of(up_blocks),
            stage_of(down_blocks),
            pltpu.VMEM(cotangent.shape, low),
            pltpu.VMEM(cotangent.shape, low),
            pltpu.SemaphoreType.DMA((6,)),
            pltpu.SemaphoreType.DMA((3,)),
            pltpu.SemaphoreType.DMA((3,)),
        ],
        compiler_params=pltpu.CompilerParams(
            collective_id=4, has_side_effects=True, vmem_limit_bytes=VMEM_LIMIT
        ),
        name="hidden_layer",
    )(stream, live, gain, shift, up_bias, down_bias, cotangent, w_up, w_down)

class Reduce:
    def __init__(self, place, order, partial_sum, rows, out, bufs, sems):
        self.place, self.order, self.rows = place, order, rows
        self.partial, self.out = partial_sum, out
        self.kept, self.from_core, self.from_third, self.from_second, self.from_first = bufs
        self.core_sems, self.third_sems, self.second_sems, self.first_sems = sems
        self.n = [place.size[axis] for axis in order]
        self.me = [place.at[axis] for axis in order]
        self.sent = []
        n1, n2, n3 = self.n
        self.pair = n3 == 2
        self.third_ticks = 0 if self.pair else n3
        self.ticks = 1 + self.third_ticks + n2 + (1 if n1 == 2 else n1)

    @staticmethod
    def scratch(order, sizes, rows, columns, dtype):
        size = dict(zip(("y", "z", "x"), sizes))
        n1, n2, n3 = [size[axis] for axis in order]
        left = (n2, n1) if n3 == 2 else tuple(size[a] for a in ("y", "z", "x") if a != order[2])
        slots = lambda count: 1 if count == 2 else count + 1
        return (
            [
                pltpu.VMEM(sizes + (rows, columns), dtype),
                pltpu.VMEM(sizes + (rows, columns), dtype),
                pltpu.VMEM((slots(n3),) + left + (rows, columns), dtype),
                pltpu.VMEM((slots(n2), n1, rows, columns), dtype),
                pltpu.VMEM((slots(n1), rows, columns), dtype),
            ],
            [
                pltpu.SemaphoreType.DMA((3,)),
                pltpu.SemaphoreType.DMA((2, n3 + 1, n2)),
                pltpu.SemaphoreType.DMA((2, n2 + 1)),
                pltpu.SemaphoreType.DMA((2, n1 + 1)),
            ],
        )

    def block(self, first, second, third):
        at = dict(zip(self.order, (first, second, third)))
        return self.kept.at[at["y"], at["z"], at["x"]]

    def core_copy(self):
        return pltpu.make_async_remote_copy(
            src_ref=self.partial.at[:, :, :, 1 - self.place.core, self.rows],
            dst_ref=self.from_core,
            send_sem=self.core_sems.at[0], recv_sem=self.core_sems.at[1],
            device_id=self.place.sibling(), device_id_type=MESH,
        )

    def own_copy(self):
        return pltpu.make_async_copy(
            self.partial.at[:, :, :, self.place.core, self.rows], self.kept, self.core_sems.at[2]
        )

    def add_rows(self, dst, src, index):
        rows = dst.shape[-2]

        def step(i):
            at = index + (at_rows(i, 16),)
            dst[at] = dst[at] + src[at]

        loop(rows // 16, step)

    def send(self, stage, slot_sem, src, dst, moved, recv_sem, condition=True):
        axis = self.order[stage]

        def copy():
            return pltpu.make_async_remote_copy(
                src_ref=src, dst_ref=dst, send_sem=slot_sem, recv_sem=recv_sem,
                device_id=self.place.device(**{axis: moved}), device_id_type=MESH,
            )

        when(condition, lambda: copy().start())
        self.sent.append((condition, copy))

    def arrived(self, sem, ref):
        pltpu.make_async_copy(ref, ref, sem).wait()

    def second_order(self):
        order = []
        for step in range(1, self.n[1] + 1):
            for index in (self.n[1] - step, step - 1):
                if index not in order:
                    order.append(index)
        return order

    def tick(self, now):
        n1, n2, n3 = self.n
        if now == 0:
            self.core_copy().start()
            self.own_copy().start()
            return
        if now == 1:
            self.own_copy().wait()
            self.arrived(self.core_sems.at[1], self.from_core)
            sizes = self.kept.shape[:3]

            def add(index):
                y, rest = index // (sizes[1] * sizes[2]), lax.rem(index, sizes[1] * sizes[2])
                at = (y, rest // sizes[2], lax.rem(rest, sizes[2]))
                self.add_rows(self.kept, self.from_core, at)

            loop(sizes[0] * sizes[1] * sizes[2], add)
            if self.pair:
                other = 1 - self.me[2]
                for second in self.second_order():
                    self.send(
                        2, self.third_sems.at[0, 0, second], self.block(slice(None), second, other),
                        self.from_third.at[0, second], other, self.third_sems.at[1, 0, second],
                    )
            return
        now = now - 2
        if not self.pair:
            if now < n3:
                self.line(2, now)
        now = now - self.third_ticks
        if 0 <= now < n2:
            self.line(1, now)
        now = now - n2
        if 0 <= now and now < (1 if n1 == 2 else n1):
            self.line(0, now)

    def stage_ref(self, stage, index):
        if stage == 2:
            return self.block(slice(None), slice(None), index)
        if stage == 1:
            return self.block(slice(None), index, self.me[2])
        return self.block(index, self.me[1], self.me[2])

    def buffers(self, stage):
        if stage == 2:
            return self.from_third, self.third_sems.at[0, :, 0], self.third_sems.at[1, :, 0]
        if stage == 1:
            return self.from_second, self.second_sems.at[0], self.second_sems.at[1]
        return self.from_first, self.first_sems.at[0], self.first_sems.at[1]

    def absorb(self, stage, index, buffer_slot):
        buffer, sems = (
            (self.from_third, lambda s: self.third_sems.at[1, s, 0]),
            (self.from_second, lambda s: self.second_sems.at[1, s]),
            (self.from_first, lambda s: self.first_sems.at[1, s]),
        )[2 - stage]
        self.arrived(sems(buffer_slot), buffer.at[buffer_slot])
        target = self.stage_ref(stage, index)
        source = buffer.at[buffer_slot]
        self.add_all(target, source)

    def add_all(self, target, source):
        lead = target.shape[:-2]
        count = 1
        for size in lead:
            count *= size

        def add(index):
            at, rest = (), index
            for size in reversed(lead):
                at = (lax.rem(rest, size),) + at
                rest = rest // size
            self.add_rows(target, source, at)

        if count == 1 and not lead:
            self.add_rows(target, source, ())
        else:
            loop(count, add)

    def third_ready(self, second):
        if not self.pair:
            return
        self.arrived(self.third_sems.at[1, 0, second], self.from_third.at[0, second])
        self.add_all(self.block(slice(None), second, self.me[2]), self.from_third.at[0, second])

    def line(self, stage, now):
        size, here = self.n[stage], self.me[stage]
        sems = (self.first_sems, self.second_sems, None)[stage]
        send_sem = lambda s: self.third_sems.at[0, s, 0] if stage == 2 else sems.at[0, s]
        recv_sem = lambda s: self.third_sems.at[1, s, 0] if stage == 2 else sems.at[1, s]
        buffer = (self.from_first, self.from_second, self.from_third)[stage]
        if size == 2:
            if stage == 1:
                if now == 0:
                    for second in range(2):
                        self.third_ready(second)
                    self.send(stage, send_sem(0), self.stage_ref(stage, 1 - here), buffer.at[0], 1 - here, recv_sem(0))
                if now == 1:
                    self.absorb(stage, here, 0)
                    self.start_first()
            if stage == 0:
                self.arrived(recv_sem(0), buffer.at[0])
                self.finish(buffer.at[0])
            return
        if now < size - 1:
            up = size - 1 - now + here
            goes_up = jnp.logical_and(here <= now, here < size - 1)

            def go_up():
                if stage == 1:
                    self.third_ready(up)
                pl.when(here > 0)(lambda: self.absorb(stage, up, up))

            up = jnp.minimum(up, size - 1)
            pl.when(goes_up)(go_up)
            self.send(stage, send_sem(up), self.stage_ref(stage, up), buffer.at[up], here + 1, recv_sem(up), goes_up)
            down = jnp.maximum(now + here - (size - 1), 0)
            goes_down = jnp.logical_and(size - 1 - here <= now, here > 0)

            def go_down():
                if stage == 1:
                    self.third_ready(down)
                pl.when(here < size - 1)(lambda: self.absorb(stage, down, down))

            pl.when(goes_down)(go_down)
            self.send(stage, send_sem(down), self.stage_ref(stage, down), buffer.at[self.down_slot(stage, down)],
                      here - 1, recv_sem(self.down_slot(stage, down)), goes_down)
            return
        if stage == 1:
            self.third_ready(here)
        pl.when(here > 0)(lambda: self.absorb(stage, here, here))
        pl.when(here < size - 1)(lambda: self.absorb(stage, here, size))
        if stage == 1:
            self.start_first()
        if stage == 0:
            self.finish(None)

    def down_slot(self, stage, target):
        here, size = self.me[stage], self.n[stage]
        return jnp.where(target == here - 1, size, target)

    def start_first(self):
        if self.n[0] == 2:
            other = 1 - self.me[0]
            self.send(0, self.first_sems.at[0, 0], self.stage_ref(0, other), self.from_first.at[0], other,
                      self.first_sems.at[1, 0])

    def finish(self, extra):
        own = self.stage_ref(0, self.me[0])

        def step(i):
            rows = at_rows(i, 16)
            value = own[rows, :].astype(jnp.float32)
            if extra is not None:
                value = value + extra[rows, :].astype(jnp.float32)
            self.out[pl.ds(pl.multiple_of(self.rows.start + i * 16, 16), 16), :] = value

        loop(own.shape[0] // 16, step)

    def finish_send(self):
        self.core_copy().wait_send()
        for condition, copy in self.sent:
            when(condition, lambda copy=copy: copy().wait_send())


def by_time(timed):
    times = sorted({entry[0] for entry in timed})
    return [[entry[-1] for entry in timed if entry[0] == time] for time in times]


def piece_ticks(pieces, offsets):
    timed = []
    for piece in pieces:
        for e in range(piece.ticks + 1):
            own = offsets[piece.order[2]]
            when_at = own[e] if e < len(own) else own[-1] + e - len(own) + 1
            timed.append((when_at, functools.partial(piece.tick, e)))
    return by_time(timed)


LATE = (0, 1, 4, 5, 6, 7, 8)
OFFSETS = {"x": LATE, "y": LATE, "z": (0, 1, 1, 2, 3, 4, 5, 6, 7)}
PER_PIECE = 9


def weight_orders(index):
    third = ("x", "z", "y") if index % 2 == 0 else ("y", "z", "x")
    first = ("x", "y", "z") if index % 2 == 0 else ("y", "x", "z")
    return (("z", "x", "y"), ("z", "y", "x"), first, third)


def reduce_plan(blocked, parts=4):
    outs = [jax.ShapeDtypeStruct(p.shape[4:], jnp.float32) for p in blocked]
    plan = split_plan([o.shape[0] for o in outs], parts, weight_orders)
    scratch = []
    for index, first, rows, order in plan:
        bufs, sems = Reduce.scratch(order, blocked[index].shape[:3], rows, outs[index].shape[1], blocked[index].dtype)
        scratch += bufs + sems
    return plan, outs, scratch


def reduce_pieces(place, plan, partials, outs, scratch):
    pieces = []
    for number, (index, first, rows, order) in enumerate(plan):
        own = scratch[PER_PIECE * number : PER_PIECE * number + PER_PIECE]
        pieces.append(Reduce(place, order, partials[index], pl.ds(first, rows), outs[index], own[:5], own[5:]))
    return pieces


class Exchange:
    def __init__(self, place, src, dst, sems, micro, seq_count, forward):
        self.place, self.src, self.dst, self.sems = place, src, dst, sems
        self.micro, self.count, self.forward = micro, seq_count, forward
        self.each = src.shape[0] // (micro * seq_count)
        self.me = lax.axis_index("seq")

    def indices(self, peer):
        frames = self.count * self.each
        out = []
        for micro in range(self.micro):
            for f in range(self.each):
                by_frame = (micro * self.each + f) * self.count
                if self.forward:
                    out.append((by_frame + peer, micro * frames + self.me * self.each + f))
                else:
                    out.append((micro * frames + peer * self.each + f, by_frame + self.me))
        return out

    def greet(self):
        barrier = pltpu.get_barrier_semaphore()

        def one(step):
            peer = lax.rem(self.me + step + 1, self.count)
            pl.semaphore_signal(
                barrier, inc=1, device_id=(lax.axis_index("dp"), peer), device_id_type=MESH
            )

        loop(self.count - 1, one)
        return self.count - 1

    def start(self):
        for here, there in self.indices(self.me):
            pltpu.make_async_copy(self.src.at[here], self.dst.at[there], self.sems.at[2]).start()

        def one(step):
            peer = lax.rem(self.me + step + 1, self.count)
            for here, there in self.indices(peer):
                pltpu.make_async_remote_copy(
                    src_ref=self.src.at[here], dst_ref=self.dst.at[there],
                    send_sem=self.sems.at[0], recv_sem=self.sems.at[1],
                    device_id=(lax.axis_index("dp"), peer), device_id_type=MESH,
                ).start()

        loop(self.count - 1, one)

    def finish(self):
        own = self.micro * self.each
        most = self.dst.at[pl.ds(0, own * (self.count - 1))]
        pltpu.make_async_copy(most, most, self.sems.at[1]).wait()
        pltpu.make_async_copy(most, most, self.sems.at[0]).wait()
        few = self.dst.at[pl.ds(0, own)]
        pltpu.make_async_copy(few, few, self.sems.at[2]).wait()


def exchange_barrier(change):
    pl.semaphore_wait(pltpu.get_barrier_semaphore(), change.greet())

class Taker:
    def __init__(self, refs):
        self.refs = list(refs)

    def __call__(self, count):
        taken, self.refs = self.refs[:count], self.refs[count:]
        return taken


def batch_ticks(pieces, batches, stagger):
    timed = []
    for piece, batch in zip(pieces, batches):
        for e in range(piece.ticks + 1):
            timed.append((e + stagger[batch], batch, functools.partial(piece.tick, e)))
    timed.sort(key=lambda entry: entry[:2])
    times = sorted({entry[0] for entry in timed})
    last = {batch: max(times.index(entry[0]) for entry in timed if entry[1] == batch) for batch in set(batches)}
    return by_time(timed), last


def forward_kernel(tokens, group, micro, seq_count, dp_count, plan, count, tuning, *refs):
    batches, stagger, units = tuning
    take = Taker(refs)
    frames, onehot, allowed = take(3)
    shards = take(count)
    wholes = take(count)
    stream_out, stream_two = take(2)
    kept_one, kept_two = take(3), take(3)
    small, table_rows, v_small, source, landed, normed, v_in, v_out, sems, one_sems = take(10)
    place = Place(seq_count, dp_count)
    one = Exchange(place, source, landed, one_sems, micro, seq_count, True)
    entry_barrier(place, one)
    pieces = gather_pieces(place, plan, shards, wholes, take.refs)
    owners = [index for index, _, _, _ in plan]
    ticks, last = batch_ticks(pieces, [batches[index] for index in owners], stagger)
    across = seq_count // 8
    total, width = frames.shape
    cut = width // seq_count
    block = source.shape[1]
    low, full = jnp.bfloat16, jnp.float32

    def arrived(*indices):
        for piece, owner in zip(pieces, owners):
            if owner in indices:
                piece.finish_recv()

    def fetch(index, into, sem):
        rows = shards[index].shape[0]

        def copy(shard):
            src = wholes[index].at[:, shard // (2 * across), lax.rem(shard // 2, across), lax.rem(shard, 2)]
            pltpu.make_async_copy(src, into.at[:, at_rows(shard, rows)], sem).start()

        loop(seq_count, copy)
        return lambda: pltpu.make_async_copy(into, into, sem).wait()

    def space_read(rows):
        return frames[rows, :].astype(full) + table_rows[pl.ds(rows.start // tokens, 1), :]

    def space_base(columns):
        rows = frames[:, columns].astype(full).reshape(total // tokens, tokens, -1)
        return (rows + table_rows[:, columns][:, None, :]).reshape(total, -1)

    def space_put(columns, value):
        source[:, :, columns] = value.astype(low).reshape(total // block, block, -1)

    def time_read(rows):
        return landed[pl.ds(rows.start // block, ROWS // block)].astype(full).reshape(ROWS, width)

    def time_base(columns):
        return landed[:, :, columns].astype(full).reshape(total, -1)

    def time_put(columns, value):
        stream_two[:, columns] = value

    def work():
        yield 0
        arrived(0, 1, 2)
        ready_in, ready_out = fetch(1, v_in, sems.at[0]), fetch(2, v_out, sems.at[1])
        Fetch(wholes[0].at[0], v_small, sems.at[2]).start().wait()
        small[...] = jnp.zeros_like(small)
        for shard in range(seq_count):
            tile = pl.ds(shard * cut // 128 * 128, 128)
            piece = v_small[shard // (2 * across), shard // 2 % across, shard % 2]
            small[:, tile] = small[:, tile] + piece.astype(full)
        rows = onehot[:, 0:1] * small[6:7, :]
        for action in range(1, ACTIONS):
            rows = rows + onehot[:, action : action + 1] * small[6 + action : 7 + action, :]
        table_rows[...] = rows
        yield
        yield from attend_forward_work(
            space_read, space_base, None, small.at[0:1], small.at[3:4], v_in, v_out, ready_in, ready_out,
            space_put, *kept_one, normed, tokens,
        )
        one.start()
        yield 1
        arrived(3, 4)
        ready_in, ready_out = fetch(3, v_in, sems.at[0]), fetch(4, v_out, sems.at[1])
        yield
        one.finish()
        yield
        yield from attend_forward_work(
            time_read, time_base, allowed, small.at[1:2], small.at[4:5], v_in, v_out, ready_in, ready_out,
            time_put, *kept_two, normed, group,
        )

    weave(work(), ticks, units, last)
    leave = Fetch(landed, stream_out, sems.at[3]).start()
    arrived(*range(5, count))
    for piece in pieces:
        piece.finish_send()
    leave.wait()


def forward(frames, onehot, allowed, shards, tokens, group, micro, seq_count, dp_count, block, tuning):
    total, width = frames.shape
    low, full = jnp.bfloat16, jnp.float32
    shape = jax.ShapeDtypeStruct
    plan, wholes, scratch = gather_plan(shards, seq_count, dp_count)
    heads = width // HDIM
    kept = [
        [shape((total, 3 * width), low), shape((total // size * heads, size, size), low), shape((total, width), low)]
        for size in (tokens, group)
    ]
    blocks = (total // block, block, width)
    count = len(shards)
    result = pl.pallas_call(
        functools.partial(forward_kernel, tokens, group, micro, seq_count, dp_count, plan, count, tuning),
        out_shape=tuple(wholes + [shape(blocks, low), shape((total, width), full)] + kept[0] + kept[1]),
        in_specs=vmem(3) + hbm(count),
        out_specs=hbm(count + 1) + vmem(7),
        scratch_shapes=[
            pltpu.VMEM((32, width), full),
            pltpu.VMEM((total // tokens, width), full),
            pltpu.VMEM(wholes[0].shape[1:], low),
            pltpu.VMEM(blocks, low),
            pltpu.VMEM(blocks, low),
            pltpu.VMEM((total, width), low),
            pltpu.VMEM((dp_count, width, 3 * width // dp_count), low),
            pltpu.VMEM((dp_count, width, width // dp_count), low),
            pltpu.SemaphoreType.DMA((4,)),
            pltpu.SemaphoreType.DMA((3,)),
        ] + scratch,
        compiler_params=pltpu.CompilerParams(
            collective_id=1, has_side_effects=True, vmem_limit_bytes=VMEM_LIMIT
        ),
        name="forward",
    )(frames, onehot, allowed, *shards)
    wholes, rest = result[:count], result[count:]
    return wholes, rest[0], rest[1], rest[2:5], rest[5:8]


def backward_scratch(total, width, packed, probs, w_in, w_out, in_blocks, out_blocks):
    low, full = jnp.bfloat16, jnp.float32
    return [
        pltpu.VMEM((total, width), low),
        pltpu.VMEM((total, width), low),
        pltpu.VMEM((total, 3 * width), low),
        pltpu.VMEM((total, width), full),
        pltpu.VMEM(packed.shape, low),
        pltpu.VMEM(probs.shape, low),
        pltpu.VMEM(w_in.shape, low),
        pltpu.VMEM(w_out.shape, low),
        stage_of(in_blocks),
        stage_of(out_blocks),
        pltpu.SemaphoreType.DMA((8,)),
    ]


def time_backward_kernel(tokens, micro, seq_count, dp_count, plan, count, ratio, *refs):
    take = Taker(refs)
    up, stream, gain, shift, packed_h, probs_h, mixed, w_in_h, w_out_h = take(9)
    partials = take(count)
    arrived, w_in_grad, w_out_grad, gain_out, shift_out = take(5)
    outs = take(count)
    own = take(11)
    down, change_sems = take(2)
    place = Place(seq_count, dp_count)
    change = Exchange(place, down, arrived, change_sems, micro, seq_count, False)
    entry_barrier(place, change)
    pieces = reduce_pieces(place, plan, partials, outs, take.refs)

    def work():
        yield from attend_backward_work(
            False, tokens, up, stream, None, gain, shift, packed_h, probs_h, mixed, w_in_h, w_out_h,
            down, w_in_grad, w_out_grad, gain_out, shift_out, None, *own
        )
        change.start()

    weave(work(), piece_ticks(pieces, OFFSETS), ratio)
    change.finish()
    for piece in pieces:
        piece.finish_send()


def time_backward(tokens, block, micro, seq_count, dp_count, partials, ratio,
                  up, stream, gain, shift, packed, probs, mixed, w_in, w_out):
    total, width = stream.shape
    low, full = jnp.bfloat16, jnp.float32
    shape = jax.ShapeDtypeStruct
    plan, sums_out, scratch = reduce_plan(partials)
    blocks = (total // block, block, width)
    in_blocks, out_blocks = blocks_of(w_in, seq_count), blocks_of(w_out, seq_count)
    outs = [
        shape(blocks, low), in_blocks, out_blocks, shape((1, width), full), shape((1, width), full)
    ]
    got = pl.pallas_call(
        functools.partial(time_backward_kernel, tokens, micro, seq_count, dp_count, plan, len(partials), ratio),
        out_shape=tuple(outs + sums_out),
        in_specs=vmem(4) + hbm(2) + vmem(1) + hbm(2 + len(partials)),
        out_specs=hbm(3) + vmem(2 + len(partials)),
        scratch_shapes=backward_scratch(total, width, packed, probs, w_in, w_out, in_blocks, out_blocks)
        + [pltpu.VMEM(blocks, low), pltpu.SemaphoreType.DMA((3,))]
        + scratch,
        compiler_params=pltpu.CompilerParams(
            collective_id=2, has_side_effects=True, vmem_limit_bytes=VMEM_LIMIT
        ),
        name="time_backward",
    )(up, stream, gain, shift, packed, probs, mixed, w_in, w_out, *partials)
    return got[:5], got[5:]


def space_backward_kernel(tokens, seq_count, dp_count, plans, counts, units, *refs):
    take = Taker(refs)
    up, stream, extra, gain, shift, packed_h, probs_h, mixed, w_in_h, w_out_h = take(10)
    onehot, gain_two, gain_three, shift_two, shift_three, up_bias, down_bias = take(7)
    partials = take(counts[0])
    down, w_in_grad, w_out_grad = take(3)
    outs = take(counts[0])
    last_outs = take(3)
    own = take(11)
    gain_out, shift_out, sums, rows, small_part = take(5)
    place = Place(seq_count, dp_count)
    entry_barrier(place)
    scratch = take(counts[1])
    pieces = reduce_pieces(place, plans[0], partials, outs, scratch)
    ends = reduce_pieces(place, plans[1], (w_in_grad, w_out_grad, small_part), last_outs, take.refs)
    width, hidden = stream.shape[1], up_bias.shape[1]
    low = jnp.bfloat16

    def small_rows():
        top = [gain_out, gain_two, gain_three, shift_out, shift_two, shift_three]
        rows[...] = jnp.zeros_like(rows)
        for at, row in enumerate(top):
            rows[at : at + 1, :] = row[...]
        for action in range(ACTIONS):
            total = onehot[0:1, action : action + 1] * sums[0:1, :]
            for frame in range(1, sums.shape[0]):
                total = total + onehot[frame : frame + 1, action : action + 1] * sums[frame : frame + 1, :]
            rows[6 + action : 7 + action, :] = total
        rows[14:15, :] = down_bias[...]
        across = seq_count // 8
        lane_row = lax.broadcasted_iota(jnp.int32, (16, 128), 0)
        for shard in range(seq_count):
            tile = shard * (width // seq_count) // 128 * 128
            first = rows[:, tile : tile + 128].astype(low)
            second = jnp.zeros((16, 128), jnp.float32)
            each = hidden // seq_count
            for part in range(each // 128):
                start = shard * each + part * 128
                second = jnp.where(lane_row == part, up_bias[:, start : start + 128], second)
            for part in range(dp_count):
                at = (part, shard // (2 * across), shard // 2 % across, shard % 2)
                small_part[at + (slice(0, 16),)] = first
                small_part[at + (slice(16, 32),)] = second.astype(low)

    def work():
        yield from attend_backward_work(
            True, tokens, up, stream, extra, gain, shift, packed_h, probs_h, mixed, w_in_h, w_out_h,
            down, w_in_grad, w_out_grad, gain_out, shift_out, sums, *own
        )
        small_rows()
        yield

    weave(work(), piece_ticks(pieces, OFFSETS), units)
    for events in piece_ticks(ends, OFFSETS):
        for event in events:
            event()
    for piece in pieces + ends:
        piece.finish_send()


def space_backward(tokens, seq_count, dp_count, partials, units,
                   up, stream, extra, gain, shift, packed, probs, mixed, w_in, w_out,
                   onehot, gain_two, gain_three, shift_two, shift_three, up_bias, down_bias):
    total, width = stream.shape
    low, full = jnp.bfloat16, jnp.float32
    shape = jax.ShapeDtypeStruct
    in_blocks, out_blocks = blocks_of(w_in, seq_count), blocks_of(w_out, seq_count)
    small = shape(in_blocks.shape[:4] + (32, 128), low)
    plan, sums_out, scratch = reduce_plan(partials)
    end_plan, end_out, end_scratch = reduce_plan([in_blocks, out_blocks, small])
    outs = [shape((total // 16, 16, width), low), in_blocks, out_blocks]
    count = len(partials)
    got = pl.pallas_call(
        functools.partial(
            space_backward_kernel, tokens, seq_count, dp_count, (plan, end_plan), (count, len(scratch)), units
        ),
        out_shape=tuple(outs + sums_out + end_out),
        in_specs=vmem(5) + hbm(2) + vmem(1) + hbm(2) + vmem(7) + hbm(count),
        out_specs=vmem(1) + hbm(2) + vmem(count + 3),
        scratch_shapes=backward_scratch(total, width, packed, probs, w_in, w_out, in_blocks, out_blocks)
        + [
            pltpu.VMEM((1, width), full),
            pltpu.VMEM((1, width), full),
            pltpu.VMEM((total // tokens, width), full),
            pltpu.VMEM((16, width), full),
            pltpu.VMEM(small.shape, low),
        ]
        + scratch + end_scratch,
        compiler_params=pltpu.CompilerParams(
            collective_id=3, has_side_effects=True, vmem_limit_bytes=VMEM_LIMIT
        ),
        name="space_backward",
    )(up, stream, extra, gain, shift, packed, probs, mixed, w_in, w_out,
      onehot, gain_two, gain_three, shift_two, shift_three, up_bias, down_bias, *partials)
    return got[0], got[3 : 3 + count], got[3 + count :]

ACTIONS = 8
FRAMES = 16
FORWARD = ((0, 0, 0, 1, 1, 2, 2), (0, 3, 6), (6,))
TIME_UNITS = (7, 6, 6, 4)
SPACE_UNITS = (6, 4, 4, 4, 4, 2)


def body(
    frames_in,
    cotangent,
    lengths,
    actions,
    spatial_in,
    spatial_out,
    temporal_in,
    temporal_out,
    hidden_in,
    hidden_out,
    norm_gains,
    norm_shifts,
    bias_up,
    bias_down,
    action_table,
):
    seq_count, dp_count = lax.axis_size("seq"), lax.axis_size("dp")
    micro, frame_count, spatial, width = frames_in.shape
    tokens = micro * frame_count * spatial
    frames = seq_count * frame_count
    places = spatial // seq_count
    group = frames * places
    cut = norm_gains.shape[1]
    low, full = jnp.bfloat16, jnp.float32

    up_rows = bias_up.shape[0] // cut
    small = jnp.concatenate(
        [norm_gains, norm_shifts, action_table, bias_down[None], bias_up.reshape(up_rows, cut)], axis=0
    )
    used = small.shape[0]
    small = jnp.pad(small, ((0, 32 - used), (0, 0)))
    lane = lax.rem(lax.axis_index("seq") * cut, 128)
    small = lax.dynamic_update_slice(jnp.zeros((32, 128), low), small, (0, lane))
    shards = [small, spatial_in, spatial_out, temporal_in, temporal_out, hidden_in, hidden_out]

    at = jnp.arange(group, dtype=jnp.int32)
    frame, place = at // places, at % places
    video, frame = frame // FRAMES, frame % FRAMES
    span = lengths[:, video]
    alive = frame[None] < span
    allowed = (
        (place[:, None] == place[None]) & (video[:, None] == video[None]) & (frame[:, None] <= frame[None])
    )[None] & alive[:, :, None]
    allowed = allowed.astype(full)
    live = alive.astype(full).reshape(tokens, 1)
    onehot = (actions.reshape(-1)[:, None] == jnp.arange(ACTIONS)[None, :]).astype(full)

    frames_flat = frames_in.reshape(tokens, width)
    blocks = (tokens // places, places, width)
    wholes, stream_one, stream_two, kept_one, kept_two = forward(
        frames_flat, onehot, allowed, shards, spatial, group, micro, seq_count, dp_count,
        places, FORWARD,
    )
    w_sin, w_sout, w_tin, w_tout, w_hin, w_hout = [
        whole.reshape(dp_count, shard.shape[0] * seq_count, shard.shape[1])
        for whole, shard in zip(wholes[1:], shards[1:])
    ]
    small = wholes[0][0].reshape(seq_count // (128 // cut), 128 // cut, 32, 128).astype(full).sum(axis=1)
    rows = small.transpose(1, 0, 2).reshape(32, width)
    gain, shift = [rows[i : i + 1] for i in range(3)], [rows[i : i + 1] for i in range(3, 6)]
    table, down_bias = rows[6:14], rows[14:15]
    up_bias = rows[used - up_rows : used].reshape(up_rows, seq_count, cut).transpose(1, 0, 2).reshape(1, -1)
    row_pair = jnp.dot(onehot, table, precision=lax.Precision.HIGHEST)
    stream_one = stream_one.reshape(tokens, width)
    layer_out, two_grad, hin_grad, hout_grad, gain_three, shift_three, up_grad, down_grad = hidden_layer(
        micro, seq_count, dp_count, stream_two, live, gain[2], shift[2], up_bias, down_bias, cotangent.reshape(blocks),
        w_hin, w_hout,
    )
    (one_grad, tin_grad, tout_grad, gain_two, shift_two), hidden_sums = time_backward(
        group, places, micro, seq_count, dp_count, [hin_grad, hout_grad], TIME_UNITS,
        two_grad, stream_one, gain[1], shift[1], *kept_two, w_tin, w_tout,
    )
    in_grad, time_sums, (*space_sums, small) = space_backward(
        spatial, seq_count, dp_count, [tin_grad, tout_grad], SPACE_UNITS,
        one_grad.reshape(tokens, width), frames_flat, row_pair, gain[0], shift[0], *kept_one, w_sin, w_sout,
        onehot, gain_two, gain_three, shift_two, shift_three, up_grad, down_grad,
    )
    up_sum = small[16 : 16 + bias_up.shape[0] // 128].reshape(-1)
    small = lax.dynamic_slice(small, (0, lane), (16, cut))
    return (
        layer_out.reshape(frames_in.shape),
        in_grad.reshape(frames_in.shape),
        *space_sums,
        *time_sums,
        *hidden_sums,
        small[0:3],
        small[3:6],
        up_sum,
        small[14],
        small[6:14],
    )


def solution(mesh):
    rows = P(None, ("dp", "seq"), None, None)
    matrix = P("seq", "dp")
    cut = P(None, "seq")
    in_specs = (rows, rows, P(None, "dp"), P(None, ("dp", "seq"))) + (matrix,) * 6 + (cut, cut, P("seq"), P("seq"), cut)
    out_specs = (rows, rows) + (matrix,) * 6 + (cut, cut, P("seq"), P("seq"), cut)
    return jax.shard_map(body, mesh=mesh, in_specs=in_specs, out_specs=out_specs, check_vma=False)
```

```python
import functools
import jax
import jax.numpy as jnp
from jax import lax
from jax.experimental import pallas as pl
from jax.experimental.pallas import tpu as pltpu
from jax.sharding import PartitionSpec as P

MESH = pl.DeviceIdType.MESH


class Place:
    def __init__(self, seq_count, dp_count):
        self.size = {"z": 4, "x": seq_count // 8, "y": dp_count}
        seq = lax.axis_index("seq")
        self.core = lax.rem(seq, 2)
        self.at = {
            "z": seq // (2 * self.size["x"]),
            "x": lax.rem(seq // 2, self.size["x"]),
            "y": lax.axis_index("dp"),
        }

    def device(self, core=None, **moved):
        at = dict(self.at, **moved)
        core = self.core if core is None else core
        return (at["y"], (at["z"] * self.size["x"] + at["x"]) * 2 + core)

    def sibling(self):
        return self.device(core=1 - self.core)


def when(condition, action):
    if condition is True:
        action()
    elif condition is not False:
        pl.when(condition)(action)


def entry_barrier(place, change=None):
    barrier = pltpu.get_barrier_semaphore()

    def greet(device):
        pl.semaphore_signal(barrier, inc=1, device_id=device, device_id_type=MESH)

    count = 1
    if change is not None:
        count = count + change.greet()
    greet(place.sibling())
    for axis in ("x", "y", "z"):
        here, size = place.at[axis], place.size[axis]
        if size == 2:
            greet(place.device(**{axis: 1 - here}))
            count = count + 1
            continue
        pl.when(here > 0)(lambda axis=axis, here=here: greet(place.device(**{axis: here - 1})))
        pl.when(here < size - 1)(lambda axis=axis, here=here: greet(place.device(**{axis: here + 1})))
        count = count + (here > 0).astype(jnp.int32) + (here < size - 1).astype(jnp.int32)
    pl.semaphore_wait(barrier, count)


def line_steps(here, size, distance):
    if size == 2:
        return [(1 - here, True, False, 0)]
    return [
        (here - distance, here - distance >= 0, here < size - 1, 1),
        (here + distance, here + distance < size, here > 0, -1),
    ]


class Gather:
    def __init__(self, place, order, shard, whole, rows, sems):
        self.place, self.order = place, order
        self.shard, self.whole, self.rows = shard, whole, rows
        self.n = [place.size[axis] for axis in order]
        self.me = [place.at[axis] for axis in order]
        self.recv, self.send, self.sib_send, self.sib_recv, self.own_sem = sems
        self.sent = []
        n1, n2, n3 = self.n
        self.ticks = n1 - 1 + n2 + max(n3 - 1, 1)

    @staticmethod
    def sem_shapes(n):
        n1, n2, n3 = n
        count = n1 + n2 + n2 * n3
        return (
            pltpu.SemaphoreType.DMA((count,)),
            pltpu.SemaphoreType.DMA((2, count)),
            pltpu.SemaphoreType.DMA((n2, n3)),
            pltpu.SemaphoreType.DMA((n2, n3)),
            pltpu.SemaphoreType.DMA((1,)),
        )

    def block(self, first, second, third, core=None):
        at = dict(zip(self.order, (first, second, third)))
        core = self.place.core if core is None else core
        return self.whole.at[at["y"], at["z"], at["x"], core, self.rows]

    def own(self):
        return pltpu.make_async_copy(
            self.shard.at[self.rows], self.block(*self.me), self.own_sem.at[0]
        )

    def pass_on(self, stage, slot, src, dst, direction, condition):
        axis, here = self.order[stage], self.me[stage]
        target = self.place.device(**{axis: here + direction})
        sem = self.send.at[(direction + 1) // 2, slot]

        def copy():
            return pltpu.make_async_remote_copy(
                src_ref=src, dst_ref=dst, send_sem=sem, recv_sem=self.recv.at[slot],
                device_id=target, device_id_type=MESH,
            )

        when(condition, lambda: copy().start())
        self.sent.append((condition, copy))

    def spread(self, stage, slot, src, dst):
        here, size = self.me[stage], self.n[stage]
        if size == 2:
            axis = self.order[stage]
            target = self.place.device(**{axis: 1 - here})

            def copy():
                return pltpu.make_async_remote_copy(
                    src_ref=src, dst_ref=dst, send_sem=self.send.at[0, slot],
                    recv_sem=self.recv.at[slot], device_id=target, device_id_type=MESH,
                )

            copy().start()
            self.sent.append((True, copy))
            return
        self.pass_on(stage, slot, src, dst, 1, here < size - 1)
        self.pass_on(stage, slot, src, dst, -1, here > 0)

    def arrive(self, slot, ref):
        pltpu.make_async_copy(ref, ref, self.recv.at[slot]).wait()

    def to_sibling(self, second, third):
        ref = self.block(slice(None), second, third)

        def copy():
            return pltpu.make_async_remote_copy(
                src_ref=ref, dst_ref=ref, send_sem=self.sib_send.at[second, third],
                recv_sem=self.sib_recv.at[second, third],
                device_id=self.place.sibling(), device_id_type=MESH,
            )

        return copy

    def hand(self, second, third, condition=True):
        copy = self.to_sibling(second, third)
        when(condition, lambda: copy().start())

    def tick(self, now):
        n1, n2, n3 = self.n
        me1, me2, me3 = self.me
        if now == 0:
            self.own().start()
            src = self.shard.at[self.rows]
            self.spread(0, me1, src, self.block(*self.me))
        if 1 <= now <= n1 - 1:
            for index, here, go, way in line_steps(me1, n1, now):
                self.step_one(index, here, go, way)
        base = n1 - 1
        if now == base:
            self.own().wait()
            self.group_ready(me2)
            ref = self.block(slice(None), me2, me3)
            self.spread(1, n1 + me2, ref, ref)
        for distance in range(1, n2):
            if now == base + distance:
                for index, here, go, way in line_steps(me2, n2, distance):
                    self.step_two(index, here, go, way)
        for far in range(1, n3):
            for distance in range(0, n2):
                if now == base + distance + far:
                    choices = [(me2, True)] if distance == 0 else [
                        (index, here) for index, here, _, _ in line_steps(me2, n2, distance)
                    ]
                    for second, there in choices:
                        for index, here, go, way in line_steps(me3, n3, far):
                            self.step_three(second, there, index, here, go, way)

    def step_one(self, index, here, go, way):
        ref = self.block(index, *self.me[1:])
        both = here if go is True or go is False else jnp.logical_and(here, go)

        when(here, lambda: self.arrive(index, ref))
        if go is not False:
            self.pass_on(0, index, ref, ref, way, both)

    def group_ready(self, second, condition=True):
        self.hand(second, self.me[2], condition)
        ref = self.block(slice(None), second, self.me[2])
        slot = self.n[0] + self.n[1] + second * self.n[2] + self.me[2]
        if condition is True:
            self.spread(2, slot, ref, ref)
            return
        here, size = self.me[2], self.n[2]
        if size == 2:
            axis = self.order[2]
            target = self.place.device(**{axis: 1 - here})

            def copy():
                return pltpu.make_async_remote_copy(
                    src_ref=ref, dst_ref=ref, send_sem=self.send.at[0, slot],
                    recv_sem=self.recv.at[slot], device_id=target, device_id_type=MESH,
                )

            when(condition, lambda: copy().start())
            self.sent.append((condition, copy))
            return
        self.pass_on(2, slot, ref, ref, 1, jnp.logical_and(condition, here < size - 1))
        self.pass_on(2, slot, ref, ref, -1, jnp.logical_and(condition, here > 0))

    def step_two(self, index, here, go, way):
        slot = self.n[0] + index
        ref = self.block(slice(None), index, self.me[2])
        when(here, lambda: self.arrive(slot, ref))
        if go is not False:
            both = here if go is True else jnp.logical_and(here, go)
            self.pass_on(1, slot, ref, ref, way, both)
        self.group_ready(index, here)

    def step_three(self, second, there, index, here, go, way):
        slot = self.n[0] + self.n[1] + second * self.n[2] + index
        ref = self.block(slice(None), second, index)
        here = here if there is True else (there if here is True else jnp.logical_and(here, there))
        when(here, lambda: self.arrive(slot, ref))
        if go is not False:
            both = here if go is True else (go if here is True else jnp.logical_and(here, go))
            self.pass_on(2, slot, ref, ref, way, both)
        self.hand(second, index, here)

    def finish_recv(self):
        other = 1 - self.place.core
        for second in range(self.n[1]):
            for third in range(self.n[2]):
                ref = self.block(slice(None), second, third, core=other)
                pltpu.make_async_copy(ref, ref, self.sib_recv.at[second, third]).wait()

    def finish_send(self):
        for condition, copy in self.sent:
            when(condition, lambda copy=copy: copy().wait_send())
        for second in range(self.n[1]):
            for third in range(self.n[2]):
                self.to_sibling(second, third)().wait_send()


def split_plan(heights, parts_of, orders_of):
    plan = []
    for index, height in enumerate(heights):
        parts = min(parts_of, height // 16)
        rows = height // parts
        for part in range(parts):
            plan.append((index, part * rows, rows, orders_of(index)[part]))
    return plan


def gather_orders(index):
    if index % 2 == 0:
        return (("x", "z", "y"), ("y", "z", "x"))
    return (("z", "x", "y"), ("z", "y", "x"))


PER_GATHER = 5


def gather_plan(shards, seq_count, dp_count, parts=2):
    size = {"z": 4, "x": seq_count // 8, "y": dp_count}
    plan = split_plan([s.shape[0] for s in shards], parts, gather_orders)
    scratch = []
    for _, _, _, order in plan:
        scratch += list(Gather.sem_shapes([size[a] for a in order]))
    outs = [jax.ShapeDtypeStruct((dp_count, 4, size["x"], 2) + s.shape, s.dtype) for s in shards]
    return plan, outs, scratch


def gather_pieces(place, plan, shards, wholes, scratch):
    pieces = []
    for number, (index, first, rows, order) in enumerate(plan):
        pieces.append(
            Gather(place, order, shards[index], wholes[index], pl.ds(first, rows),
                   scratch[PER_GATHER * number : PER_GATHER * number + PER_GATHER])
        )
    return pieces

D_EPS = 1e-05
NEG = -1e30
HEADS = 16
HDIM = 64
SCALE = HDIM ** (-0.5)
NT = (((1,), (1,)), ((), ()))
TN = (((0,), (0,)), ((), ()))
ROWS = 32
VMEM_LIMIT = 63 * 1024 * 1024


def dot(left, right, dims=(((1,), (0,)), ((), ()))):
    return lax.dot_general(left, right, dims, preferred_element_type=jnp.float32)


def tile_of(size, largest=512):
    return max(t for t in (128, 256, 384, 512, 1024) if t <= largest and size % t == 0)


def loop(count, action):
    def step(index, carry):
        action(index)
        return carry

    lax.fori_loop(0, count, step, 0)


def at_rows(index, size):
    return pl.ds(pl.multiple_of(index * size, size), size)


def moments(value):
    width = value.shape[-1]
    centre = jnp.sum(value, axis=-1, keepdims=True) * (1.0 / width)
    offset = value - centre
    spread = jnp.sum(offset * offset, axis=-1, keepdims=True) * (1.0 / width)
    return offset, lax.rsqrt(spread + D_EPS)


def norm_forward(read, gain, shift, out):
    def step(index):
        rows = at_rows(index, ROWS)
        offset, rate = moments(read(rows))
        out[rows, :] = (offset * rate * gain[...] + shift[...]).astype(jnp.bfloat16)

    loop(out.shape[0] // ROWS, step)


def fold8(value):
    return jnp.sum(value.reshape(-1, 8, value.shape[-1]), axis=0)


def norm_backward(read, gain, grad, upstream, write, gain_out, shift_out):
    tokens, width = grad.shape

    def step(index, carry):
        gain_sum, shift_sum = carry
        rows = at_rows(index, ROWS)
        offset, rate = moments(read(rows))
        unit = offset * rate
        dy = grad[rows, :]
        gain_sum = gain_sum + fold8(dy * unit)
        shift_sum = shift_sum + fold8(dy)
        scaled = dy * gain[...]
        mean = jnp.sum(scaled, axis=-1, keepdims=True) * (1.0 / width)
        slope = jnp.sum(scaled * unit, axis=-1, keepdims=True) * (1.0 / width)
        write(index, rows, upstream(rows) + rate * (scaled - mean - unit * slope))
        return gain_sum, shift_sum

    zero = jnp.zeros((8, width), jnp.float32)
    gain_sum, shift_sum = lax.fori_loop(0, tokens // ROWS, step, (zero, zero))
    gain_out[...] = jnp.sum(gain_sum, axis=0, keepdims=True)
    shift_out[...] = jnp.sum(shift_sum, axis=0, keepdims=True)


def chunks(count, step, units):
    units = max(u for u in range(1, min(units, count) + 1) if count % u == 0)
    each = count // units
    for unit in range(units):
        loop(each, lambda index, unit=unit: step(unit * each + index))
        yield


def drain(work):
    for _ in work:
        pass


def project(rows, weight, emit, tile_max=512, units=1):
    parts, _, size = weight.shape
    tile = tile_of(size, tile_max)
    for part in range(parts):

        def step(index, part=part):
            inner = at_rows(index, tile)
            columns = pl.ds(pl.multiple_of(part * size + index * tile, 128), tile)
            emit(columns, dot(rows[...], weight[part, :, inner]))

        yield from chunks(size // tile, step, units)


def project_back(grad, weight, emit, tile_max=512, units=1):
    parts, depth, size = weight.shape
    tile = tile_of(depth, tile_max)

    def step(index):
        inner = at_rows(index, tile)
        total = None
        for part in range(parts):
            term = dot(grad[:, part * size : (part + 1) * size], weight[part, inner, :], NT)
            total = term if total is None else total + term
        emit(inner, total)

    yield from chunks(depth // tile, step, units)


def outer(rows, grad, out, stage, sems, units=1):
    parts, _, across, _, size_r, size = out.shape
    chips = stage.shape[2]
    tile = chips * 2 * size_r

    def leave(index, slot):
        first = index * chips
        return pltpu.make_async_copy(
            stage.at[slot], out.at[:, first // across, pl.ds(lax.rem(first, across), chips)], sems.at[slot]
        )

    def step(index):
        slot = lax.rem(index, 2)
        pl.when(index >= 2)(lambda: leave(index - 2, slot).wait())
        left = rows[:, at_rows(index, tile)]
        for part in range(parts):
            value = dot(left, grad[:, part * size : (part + 1) * size], TN)
            stage[slot, part] = value.reshape(chips, 2, size_r, size).astype(out.dtype)
        leave(index, slot).start()

    count = rows.shape[1] // tile
    yield from chunks(count, step, units)
    leave(count - 2, (count - 2) % 2).wait()
    leave(count - 1, (count - 1) % 2).wait()


def head_mask(shape, axis, head):
    lane = lax.broadcasted_iota(jnp.int32, shape, axis)
    return (lane // HDIM) == head


def pick(value, head):
    return jnp.where(head_mask(value.shape, 1, head), value, jnp.zeros_like(value))


def pick_rows(value, head):
    return jnp.where(head_mask(value.shape, 0, head), value, jnp.zeros_like(value))


def pair_slices(index, width, tokens):
    pairs = width // 128
    micro, pair = index // pairs, lax.rem(index, pairs)
    rows = pl.ds(pl.multiple_of(micro * tokens, tokens), tokens)
    return micro, rows, [
        pl.ds(pl.multiple_of(part * width + pair * 128, 128), 128) for part in range(3)
    ]


def attention_forward(packed, allowed, probs, mixed, tokens, units=1):
    width = mixed.shape[1]

    def step(index):
        micro, rows, (q_at, k_at, v_at) = pair_slices(index, width, tokens)
        queries = packed[rows, q_at] * jnp.bfloat16(SCALE)
        keys, values = packed[rows, k_at], packed[rows, v_at]
        values_t = values.astype(jnp.float32).T.astype(jnp.bfloat16)
        total = None
        for head in range(2):
            scores = dot(keys, pick(queries, head), NT)
            if allowed is not None:
                scores = jnp.where(allowed[micro] > 0, scores, NEG)
            raised = jnp.exp(scores - jnp.max(scores, axis=0, keepdims=True))
            prob = raised * (1.0 / jnp.sum(raised, axis=0, keepdims=True))
            prob = prob.astype(jnp.bfloat16)
            probs[2 * index + head] = prob
            term = dot(pick_rows(values_t, head), prob)
            total = term if total is None else total + term
        mixed[rows, q_at] = total.T.astype(jnp.bfloat16)

    yield from chunks(mixed.shape[0] // tokens * (width // 128), step, units)


def attention_backward(packed, probs, grad, packed_grad, tokens, units=1):
    width = grad.shape[1]

    def step(index):
        _, rows, (q_at, k_at, v_at) = pair_slices(index, width, tokens)
        queries, keys, values = packed[rows, q_at], packed[rows, k_at], packed[rows, v_at]
        upstream = grad[rows, q_at]
        keys_t = keys.astype(jnp.float32).T.astype(jnp.bfloat16)
        query_grad = key_grad = value_grad = None
        for head in range(2):
            low = probs[2 * index + head]
            prob = low.astype(jnp.float32)
            up = pick(upstream, head)
            prob_grad = dot(values, up, NT)
            inner = jnp.sum(prob * prob_grad, axis=0, keepdims=True)
            score_grad = (prob * (prob_grad - inner) * SCALE).astype(jnp.bfloat16)
            terms = (
                dot(pick_rows(keys_t, head), score_grad),
                dot(score_grad, pick(queries, head)),
                dot(low, up),
            )
            if head == 0:
                query_grad, key_grad, value_grad = terms
            else:
                query_grad = query_grad + terms[0]
                key_grad = key_grad + terms[1]
                value_grad = value_grad + terms[2]
        packed_grad[rows, q_at] = query_grad.T.astype(jnp.bfloat16)
        packed_grad[rows, k_at] = key_grad.astype(jnp.bfloat16)
        packed_grad[rows, v_at] = value_grad.astype(jnp.bfloat16)

    yield from chunks(grad.shape[0] // tokens * (width // 128), step, units)


class Fetch:
    def __init__(self, src, dst, sem):
        self.copy = pltpu.make_async_copy(src, dst, sem)

    def start(self):
        self.copy.start()
        return self

    def wait(self):
        self.copy.wait()


def spatial_reader(frames, row_pair, tokens):
    def read(rows):
        micro = rows.start // tokens
        return frames[rows, :].astype(jnp.float32) + row_pair[pl.ds(micro, 1), :]

    return read


def attend_forward_work(read, base, allowed, gain, shift, v_in, v_out, ready_in, ready_out, put,
                        packed, probs, mixed, normed, tokens):
    norm_forward(read, gain, shift, normed)
    ready_in()
    yield

    def emit(columns, value):
        packed[:, columns] = value.astype(jnp.bfloat16)

    yield from project(normed, v_in, emit, units=3)
    yield from attention_forward(packed, allowed, probs, mixed, tokens, units=8)
    ready_out()

    def emit_out(columns, value):
        put(columns, base(columns) + value)

    yield from project(mixed, v_out, emit_out, units=2)


def vmem(count):
    return [pl.BlockSpec(memory_space=pltpu.VMEM)] * count


def hbm(count):
    return [pl.BlockSpec(memory_space=pltpu.HBM)] * count


def attend_backward_work(spatial, tokens, up, stream, extra, gain, shift, packed_h, probs_h, mixed, w_in_h, w_out_h,
                         down, w_in_grad, w_out_grad, gain_out, shift_out, sums,
                         up_low, mixed_grad, packed_grad, normed_grad, packed, probs, w_in, w_out,
                         in_stage, out_stage, sems, have_grads=None, have_normed=None):
    read = spatial_reader(stream, extra, tokens) if spatial else (lambda rows: stream[rows, :].astype(jnp.float32))
    fetches = [
        Fetch(src, dst, sems.at[i]).start()
        for i, (src, dst) in enumerate(
            ((w_out_h, w_out), (packed_h, packed), (probs_h, probs), (w_in_h, w_in))
        )
    ]

    def lower(index):
        rows = at_rows(index, ROWS)
        up_low[rows, :] = up[rows, :].astype(jnp.bfloat16)

    loop(up.shape[0] // ROWS, lower)
    yield
    fetches[0].wait()

    def emit_mixed(columns, value):
        mixed_grad[:, columns] = value.astype(jnp.bfloat16)

    yield from project_back(up_low, w_out, emit_mixed, units=2)
    yield from outer(mixed, up_low, w_out_grad, out_stage, sems.at[pl.ds(4, 2)], units=2)
    normed = up_low
    norm_forward(read, gain, shift, normed)
    yield
    fetches[1].wait()
    fetches[2].wait()
    yield from attention_backward(packed, probs, mixed_grad, packed_grad, tokens, units=8)
    fetches[3].wait()
    yield from outer(normed, packed_grad, w_in_grad, in_stage, sems.at[pl.ds(6, 2)], units=4)
    if have_grads is not None:
        have_grads()

    def emit_normed(columns, value):
        normed_grad[:, columns] = value

    yield from project_back(packed_grad, w_in, emit_normed, 256, units=4)
    if have_normed is not None:
        have_normed()
    block = down.shape[1]

    def put(index, value):
        down[pl.ds(index * (ROWS // block), ROWS // block)] = value.reshape(-1, block, value.shape[1]).astype(down.dtype)

    if spatial:
        sums[...] = jnp.zeros_like(sums)

        def write(index, rows, value):
            put(index, value)
            micro = rows.start // tokens
            sums[pl.ds(micro, 1), :] += jnp.sum(fold8(value), axis=0, keepdims=True)
    else:

        def write(index, rows, value):
            put(index, value)

    norm_backward(
        read, gain, normed_grad, lambda rows: up[rows, :].astype(jnp.float32), write, gain_out, shift_out
    )
    yield


END = object()


def weave(work, ticks, units, last=()):
    held = -1
    for now, events in enumerate(ticks):
        for event in events:
            event()
        for _ in range(units[min(now, len(units) - 1)]):
            if held > now:
                break
            step = next(work, END)
            held = -1 if step is END or step is None else last[step]
            if held <= now:
                held = -1
    drain(work)


GELU_A = 0.7978845608028654
GELU_B = 0.044715


def gelu_pair(value):
    square = value * value
    bent = jnp.tanh(GELU_A * value * (1.0 + GELU_B * square))
    half = 0.5 * (1.0 + bent)
    slope = half + 0.5 * value * (1.0 - bent * bent) * (GELU_A * (1.0 + 3.0 * GELU_B * square))
    return value * half, slope


def hidden_kernel(micro, seq_count, dp_count, stream, live, gain, shift, up_bias, down_bias, cotangent_h, w_up_h, w_down_h,
                  layer_out, down, up_grad_h, down_grad_h, gain_out, shift_out, up_bias_out, down_bias_out,
                  normed, end_low, active, slope, expand_low, normed_grad, w_up, w_down, up_stage, down_stage,
                  cotangent, out, sems, end_sems, home_sems):
    low = jnp.bfloat16
    place = Place(seq_count, dp_count)
    end = Exchange(place, cotangent_h, cotangent, end_sems, micro, seq_count, True)
    home = Exchange(place, out, layer_out, home_sems, micro, seq_count, False)
    exchange_barrier(end)
    end.start()
    block = out.shape[1]
    first = Fetch(w_up_h, w_up, sems.at[0]).start()
    second = Fetch(w_down_h, w_down, sems.at[1]).start()
    tokens, width = stream.shape
    parts = w_up.shape[0]
    norm_forward(lambda rows: stream[rows, :], gain, shift, normed)

    first.wait()

    def emit_expand(columns, value):
        act, rate = gelu_pair(value + up_bias[:, columns])
        active[:, columns] = act.astype(low)
        slope[:, columns] = rate.astype(low)

    drain(project(normed, w_up, emit_expand, 256))
    second.wait()

    def emit_out(columns, value):
        ended = stream[:, columns] + value + down_bias[:, columns]
        out[:, :, columns] = (ended * live[...]).astype(low).reshape(tokens // block, block, -1)

    drain(project(active, w_down, emit_out, 256))
    home.start()
    end.finish()

    def upstream(rows):
        part = cotangent[pl.ds(rows.start // block, ROWS // block)].astype(jnp.float32).reshape(ROWS, width)
        return part * live[rows, :]

    def lower(index, total):
        rows = at_rows(index, ROWS)
        value = upstream(rows)
        end_low[rows, :] = value.astype(low)
        return total + fold8(value)

    total = lax.fori_loop(0, tokens // ROWS, lower, jnp.zeros((8, width), jnp.float32))
    down_bias_out[...] = jnp.sum(total, axis=0, keepdims=True)

    def emit_active(columns, value):
        grad = value * slope[:, columns].astype(jnp.float32)
        up_bias_out[:, columns] = jnp.sum(grad, axis=0, keepdims=True)
        expand_low[:, columns] = grad.astype(low)

    drain(project_back(end_low, w_down, emit_active, 256))

    drain(outer(active, end_low, down_grad_h, down_stage, sems.at[pl.ds(2, 2)]))
    drain(outer(normed, expand_low, up_grad_h, up_stage, sems.at[pl.ds(4, 2)]))

    def emit_normed(columns, value):
        normed_grad[:, columns] = value

    drain(project_back(expand_low, w_up, emit_normed, 256))

    def write(index, rows, value):
        down[rows, :] = value

    norm_backward(lambda rows: stream[rows, :], gain, normed_grad, upstream, write, gain_out, shift_out)
    home.finish()


def blocks_of(weight, seq_count):
    parts, depth, size = weight.shape
    return jax.ShapeDtypeStruct((parts, 4, seq_count // 8, 2, depth // seq_count, size), jnp.bfloat16)


def stage_of(blocks):
    chips = max(1, 64 // blocks.shape[4])
    return pltpu.VMEM((2, blocks.shape[0], chips) + blocks.shape[3:], jnp.bfloat16)


def hidden_layer(micro, seq_count, dp_count, stream, live, gain, shift, up_bias, down_bias, cotangent, w_up, w_down):
    tokens, width = stream.shape
    hidden = up_bias.shape[1]
    parts = w_up.shape[0]
    low, full = jnp.bfloat16, jnp.float32
    shape = jax.ShapeDtypeStruct
    up_blocks, down_blocks = blocks_of(w_up, seq_count), blocks_of(w_down, seq_count)
    return pl.pallas_call(
        functools.partial(hidden_kernel, micro, seq_count, dp_count),
        out_shape=(
            shape(cotangent.shape, low),
            shape((tokens, width), full),
            up_blocks,
            down_blocks,
            shape((1, width), full),
            shape((1, width), full),
            shape((1, hidden), full),
            shape((1, width), full),
        ),
        in_specs=vmem(6) + hbm(3),
        out_specs=hbm(1) + vmem(1) + hbm(2) + vmem(4),
        scratch_shapes=[
            pltpu.VMEM((tokens, width), low),
            pltpu.VMEM((tokens, width), low),
            pltpu.VMEM((tokens, hidden), low),
            pltpu.VMEM((tokens, hidden), low),
            pltpu.VMEM((tokens, hidden), low),
            pltpu.VMEM((tokens, width), full),
            pltpu.VMEM(w_up.shape, low),
            pltpu.VMEM(w_down.shape, low),
            stage_of(up_blocks),
            stage_of(down_blocks),
            pltpu.VMEM(cotangent.shape, low),
            pltpu.VMEM(cotangent.shape, low),
            pltpu.SemaphoreType.DMA((6,)),
            pltpu.SemaphoreType.DMA((3,)),
            pltpu.SemaphoreType.DMA((3,)),
        ],
        compiler_params=pltpu.CompilerParams(
            collective_id=4, has_side_effects=True, vmem_limit_bytes=VMEM_LIMIT
        ),
        name="hidden_layer",
    )(stream, live, gain, shift, up_bias, down_bias, cotangent, w_up, w_down)

class Reduce:
    def __init__(self, place, order, partial_sum, rows, out, bufs, sems):
        self.place, self.order, self.rows = place, order, rows
        self.partial, self.out = partial_sum, out
        self.kept, self.from_core, self.from_third, self.from_second, self.from_first = bufs
        self.core_sems, self.third_sems, self.second_sems, self.first_sems = sems
        self.n = [place.size[axis] for axis in order]
        self.me = [place.at[axis] for axis in order]
        self.sent = []
        n1, n2, n3 = self.n
        self.pair = n3 == 2
        self.third_ticks = 0 if self.pair else n3
        self.ticks = 1 + self.third_ticks + n2 + (1 if n1 == 2 else n1)

    @staticmethod
    def scratch(order, sizes, rows, columns, dtype):
        size = dict(zip(("y", "z", "x"), sizes))
        n1, n2, n3 = [size[axis] for axis in order]
        left = (n2, n1) if n3 == 2 else tuple(size[a] for a in ("y", "z", "x") if a != order[2])
        slots = lambda count: 1 if count == 2 else count + 1
        return (
            [
                pltpu.VMEM(sizes + (rows, columns), dtype),
                pltpu.VMEM(sizes + (rows, columns), dtype),
                pltpu.VMEM((slots(n3),) + left + (rows, columns), dtype),
                pltpu.VMEM((slots(n2), n1, rows, columns), dtype),
                pltpu.VMEM((slots(n1), rows, columns), dtype),
            ],
            [
                pltpu.SemaphoreType.DMA((3,)),
                pltpu.SemaphoreType.DMA((2, n3 + 1, n2)),
                pltpu.SemaphoreType.DMA((2, n2 + 1)),
                pltpu.SemaphoreType.DMA((2, n1 + 1)),
            ],
        )

    def block(self, first, second, third):
        at = dict(zip(self.order, (first, second, third)))
        return self.kept.at[at["y"], at["z"], at["x"]]

    def core_copy(self):
        return pltpu.make_async_remote_copy(
            src_ref=self.partial.at[:, :, :, 1 - self.place.core, self.rows],
            dst_ref=self.from_core,
            send_sem=self.core_sems.at[0], recv_sem=self.core_sems.at[1],
            device_id=self.place.sibling(), device_id_type=MESH,
        )

    def own_copy(self):
        return pltpu.make_async_copy(
            self.partial.at[:, :, :, self.place.core, self.rows], self.kept, self.core_sems.at[2]
        )

    def add_rows(self, dst, src, index):
        rows = dst.shape[-2]

        def step(i):
            at = index + (at_rows(i, 16),)
            dst[at] = dst[at] + src[at]

        loop(rows // 16, step)

    def send(self, stage, slot_sem, src, dst, moved, recv_sem, condition=True):
        axis = self.order[stage]

        def copy():
            return pltpu.make_async_remote_copy(
                src_ref=src, dst_ref=dst, send_sem=slot_sem, recv_sem=recv_sem,
                device_id=self.place.device(**{axis: moved}), device_id_type=MESH,
            )

        when(condition, lambda: copy().start())
        self.sent.append((condition, copy))

    def arrived(self, sem, ref):
        pltpu.make_async_copy(ref, ref, sem).wait()

    def second_order(self):
        order = []
        for step in range(1, self.n[1] + 1):
            for index in (self.n[1] - step, step - 1):
                if index not in order:
                    order.append(index)
        return order

    def tick(self, now):
        n1, n2, n3 = self.n
        if now == 0:
            self.core_copy().start()
            self.own_copy().start()
            return
        if now == 1:
            self.own_copy().wait()
            self.arrived(self.core_sems.at[1], self.from_core)
            sizes = self.kept.shape[:3]

            def add(index):
                y, rest = index // (sizes[1] * sizes[2]), lax.rem(index, sizes[1] * sizes[2])
                at = (y, rest // sizes[2], lax.rem(rest, sizes[2]))
                self.add_rows(self.kept, self.from_core, at)

            loop(sizes[0] * sizes[1] * sizes[2], add)
            if self.pair:
                other = 1 - self.me[2]
                for second in self.second_order():
                    self.send(
                        2, self.third_sems.at[0, 0, second], self.block(slice(None), second, other),
                        self.from_third.at[0, second], other, self.third_sems.at[1, 0, second],
                    )
            return
        now = now - 2
        if not self.pair:
            if now < n3:
                self.line(2, now)
        now = now - self.third_ticks
        if 0 <= now < n2:
            self.line(1, now)
        now = now - n2
        if 0 <= now and now < (1 if n1 == 2 else n1):
            self.line(0, now)

    def stage_ref(self, stage, index):
        if stage == 2:
            return self.block(slice(None), slice(None), index)
        if stage == 1:
            return self.block(slice(None), index, self.me[2])
        return self.block(index, self.me[1], self.me[2])

    def buffers(self, stage):
        if stage == 2:
            return self.from_third, self.third_sems.at[0, :, 0], self.third_sems.at[1, :, 0]
        if stage == 1:
            return self.from_second, self.second_sems.at[0], self.second_sems.at[1]
        return self.from_first, self.first_sems.at[0], self.first_sems.at[1]

    def absorb(self, stage, index, buffer_slot):
        buffer, sems = (
            (self.from_third, lambda s: self.third_sems.at[1, s, 0]),
            (self.from_second, lambda s: self.second_sems.at[1, s]),
            (self.from_first, lambda s: self.first_sems.at[1, s]),
        )[2 - stage]
        self.arrived(sems(buffer_slot), buffer.at[buffer_slot])
        target = self.stage_ref(stage, index)
        source = buffer.at[buffer_slot]
        self.add_all(target, source)

    def add_all(self, target, source):
        lead = target.shape[:-2]
        count = 1
        for size in lead:
            count *= size

        def add(index):
            at, rest = (), index
            for size in reversed(lead):
                at = (lax.rem(rest, size),) + at
                rest = rest // size
            self.add_rows(target, source, at)

        if count == 1 and not lead:
            self.add_rows(target, source, ())
        else:
            loop(count, add)

    def third_ready(self, second):
        if not self.pair:
            return
        self.arrived(self.third_sems.at[1, 0, second], self.from_third.at[0, second])
        self.add_all(self.block(slice(None), second, self.me[2]), self.from_third.at[0, second])

    def line(self, stage, now):
        size, here = self.n[stage], self.me[stage]
        sems = (self.first_sems, self.second_sems, None)[stage]
        send_sem = lambda s: self.third_sems.at[0, s, 0] if stage == 2 else sems.at[0, s]
        recv_sem = lambda s: self.third_sems.at[1, s, 0] if stage == 2 else sems.at[1, s]
        buffer = (self.from_first, self.from_second, self.from_third)[stage]
        if size == 2:
            if stage == 1:
                if now == 0:
                    for second in range(2):
                        self.third_ready(second)
                    self.send(stage, send_sem(0), self.stage_ref(stage, 1 - here), buffer.at[0], 1 - here, recv_sem(0))
                if now == 1:
                    self.absorb(stage, here, 0)
                    self.start_first()
            if stage == 0:
                self.arrived(recv_sem(0), buffer.at[0])
                self.finish(buffer.at[0])
            return
        if now < size - 1:
            up = size - 1 - now + here
            goes_up = jnp.logical_and(here <= now, here < size - 1)

            def go_up():
                if stage == 1:
                    self.third_ready(up)
                pl.when(here > 0)(lambda: self.absorb(stage, up, up))

            up = jnp.minimum(up, size - 1)
            pl.when(goes_up)(go_up)
            self.send(stage, send_sem(up), self.stage_ref(stage, up), buffer.at[up], here + 1, recv_sem(up), goes_up)
            down = jnp.maximum(now + here - (size - 1), 0)
            goes_down = jnp.logical_and(size - 1 - here <= now, here > 0)

            def go_down():
                if stage == 1:
                    self.third_ready(down)
                pl.when(here < size - 1)(lambda: self.absorb(stage, down, down))

            pl.when(goes_down)(go_down)
            self.send(stage, send_sem(down), self.stage_ref(stage, down), buffer.at[self.down_slot(stage, down)],
                      here - 1, recv_sem(self.down_slot(stage, down)), goes_down)
            return
        if stage == 1:
            self.third_ready(here)
        pl.when(here > 0)(lambda: self.absorb(stage, here, here))
        pl.when(here < size - 1)(lambda: self.absorb(stage, here, size))
        if stage == 1:
            self.start_first()
        if stage == 0:
            self.finish(None)

    def down_slot(self, stage, target):
        here, size = self.me[stage], self.n[stage]
        return jnp.where(target == here - 1, size, target)

    def start_first(self):
        if self.n[0] == 2:
            other = 1 - self.me[0]
            self.send(0, self.first_sems.at[0, 0], self.stage_ref(0, other), self.from_first.at[0], other,
                      self.first_sems.at[1, 0])

    def finish(self, extra):
        own = self.stage_ref(0, self.me[0])

        def step(i):
            rows = at_rows(i, 16)
            value = own[rows, :].astype(jnp.float32)
            if extra is not None:
                value = value + extra[rows, :].astype(jnp.float32)
            self.out[pl.ds(pl.multiple_of(self.rows.start + i * 16, 16), 16), :] = value

        loop(own.shape[0] // 16, step)

    def finish_send(self):
        self.core_copy().wait_send()
        for condition, copy in self.sent:
            when(condition, lambda copy=copy: copy().wait_send())


def by_time(timed):
    times = sorted({entry[0] for entry in timed})
    return [[entry[-1] for entry in timed if entry[0] == time] for time in times]


def piece_ticks(pieces, offsets, begun=()):
    timed = []
    for piece in pieces:
        for e in range(2 if piece in begun else 0, piece.ticks + 1):
            own = offsets[piece.order[2]]
            when_at = own[e] if e < len(own) else own[-1] + e - len(own) + 1
            timed.append((when_at, functools.partial(piece.tick, e)))
    return by_time(timed)


LATE = (0, 1, 4, 5, 6, 7, 8)
OFFSETS = {"x": LATE, "y": LATE, "z": (0, 1, 1, 2, 3, 4, 5, 6, 7)}
END_OFFSETS = OFFSETS
PER_PIECE = 9


def weight_orders(index):
    third = ("x", "z", "y") if index % 2 == 0 else ("y", "z", "x")
    first = ("x", "y", "z") if index % 2 == 0 else ("y", "x", "z")
    return (("z", "x", "y"), ("z", "y", "x"), first, third)


def reduce_plan(blocked, parts=4):
    outs = [jax.ShapeDtypeStruct(p.shape[4:], jnp.float32) for p in blocked]
    plan = split_plan([o.shape[0] for o in outs], parts, weight_orders)
    scratch = []
    for index, first, rows, order in plan:
        bufs, sems = Reduce.scratch(order, blocked[index].shape[:3], rows, outs[index].shape[1], blocked[index].dtype)
        scratch += bufs + sems
    return plan, outs, scratch


def reduce_pieces(place, plan, partials, outs, scratch):
    pieces = []
    for number, (index, first, rows, order) in enumerate(plan):
        own = scratch[PER_PIECE * number : PER_PIECE * number + PER_PIECE]
        pieces.append(Reduce(place, order, partials[index], pl.ds(first, rows), outs[index], own[:5], own[5:]))
    return pieces


class Exchange:
    def __init__(self, place, src, dst, sems, micro, seq_count, forward):
        self.place, self.src, self.dst, self.sems = place, src, dst, sems
        self.micro, self.count, self.forward = micro, seq_count, forward
        self.each = src.shape[0] // (micro * seq_count)
        self.me = lax.axis_index("seq")

    def indices(self, peer):
        frames = self.count * self.each
        out = []
        for micro in range(self.micro):
            for f in range(self.each):
                by_frame = (micro * self.each + f) * self.count
                if self.forward:
                    out.append((by_frame + peer, micro * frames + self.me * self.each + f))
                else:
                    out.append((micro * frames + peer * self.each + f, by_frame + self.me))
        return out

    def greet(self):
        barrier = pltpu.get_barrier_semaphore()

        def one(step):
            peer = lax.rem(self.me + step + 1, self.count)
            pl.semaphore_signal(
                barrier, inc=1, device_id=(lax.axis_index("dp"), peer), device_id_type=MESH
            )

        loop(self.count - 1, one)
        return self.count - 1

    def start(self):
        for here, there in self.indices(self.me):
            pltpu.make_async_copy(self.src.at[here], self.dst.at[there], self.sems.at[2]).start()

        def one(step):
            peer = lax.rem(self.me + step + 1, self.count)
            for here, there in self.indices(peer):
                pltpu.make_async_remote_copy(
                    src_ref=self.src.at[here], dst_ref=self.dst.at[there],
                    send_sem=self.sems.at[0], recv_sem=self.sems.at[1],
                    device_id=(lax.axis_index("dp"), peer), device_id_type=MESH,
                ).start()

        loop(self.count - 1, one)

    def finish(self):
        own = self.micro * self.each
        most = self.dst.at[pl.ds(0, own * (self.count - 1))]
        pltpu.make_async_copy(most, most, self.sems.at[1]).wait()
        pltpu.make_async_copy(most, most, self.sems.at[0]).wait()
        few = self.dst.at[pl.ds(0, own)]
        pltpu.make_async_copy(few, few, self.sems.at[2]).wait()


def exchange_barrier(change):
    pl.semaphore_wait(pltpu.get_barrier_semaphore(), change.greet())

class Taker:
    def __init__(self, refs):
        self.refs = list(refs)

    def __call__(self, count):
        taken, self.refs = self.refs[:count], self.refs[count:]
        return taken


def batch_ticks(pieces, batches, stagger):
    timed = []
    for piece, batch in zip(pieces, batches):
        for e in range(piece.ticks + 1):
            timed.append((e + stagger[batch], batch, functools.partial(piece.tick, e)))
    timed.sort(key=lambda entry: entry[:2])
    times = sorted({entry[0] for entry in timed})
    last = {batch: max(times.index(entry[0]) for entry in timed if entry[1] == batch) for batch in set(batches)}
    return by_time(timed), last


def forward_kernel(tokens, group, micro, seq_count, dp_count, plan, count, tuning, *refs):
    batches, stagger, units = tuning
    take = Taker(refs)
    frames, onehot, allowed = take(3)
    shards = take(count)
    wholes = take(count)
    stream_out, stream_two = take(2)
    kept_one, kept_two = take(3), take(3)
    small, table_rows, v_small, source, landed, normed, v_in, v_out, sems, one_sems = take(10)
    place = Place(seq_count, dp_count)
    one = Exchange(place, source, landed, one_sems, micro, seq_count, True)
    entry_barrier(place, one)
    pieces = gather_pieces(place, plan, shards, wholes, take.refs)
    owners = [index for index, _, _, _ in plan]
    ticks, last = batch_ticks(pieces, [batches[index] for index in owners], stagger)
    across = seq_count // 8
    total, width = frames.shape
    cut = width // seq_count
    block = source.shape[1]
    low, full = jnp.bfloat16, jnp.float32

    def arrived(*indices):
        for piece, owner in zip(pieces, owners):
            if owner in indices:
                piece.finish_recv()

    def fetch(index, into, sem):
        rows = shards[index].shape[0]

        def copy(shard):
            src = wholes[index].at[:, shard // (2 * across), lax.rem(shard // 2, across), lax.rem(shard, 2)]
            pltpu.make_async_copy(src, into.at[:, at_rows(shard, rows)], sem).start()

        loop(seq_count, copy)
        return lambda: pltpu.make_async_copy(into, into, sem).wait()

    def space_read(rows):
        return frames[rows, :].astype(full) + table_rows[pl.ds(rows.start // tokens, 1), :]

    def space_base(columns):
        rows = frames[:, columns].astype(full).reshape(total // tokens, tokens, -1)
        return (rows + table_rows[:, columns][:, None, :]).reshape(total, -1)

    def space_put(columns, value):
        source[:, :, columns] = value.astype(low).reshape(total // block, block, -1)

    def time_read(rows):
        return landed[pl.ds(rows.start // block, ROWS // block)].astype(full).reshape(ROWS, width)

    def time_base(columns):
        return landed[:, :, columns].astype(full).reshape(total, -1)

    def time_put(columns, value):
        stream_two[:, columns] = value

    def work():
        yield 0
        arrived(0, 1, 2)
        ready_in, ready_out = fetch(1, v_in, sems.at[0]), fetch(2, v_out, sems.at[1])
        Fetch(wholes[0].at[0], v_small, sems.at[2]).start().wait()
        small[...] = jnp.zeros_like(small)
        for shard in range(seq_count):
            tile = pl.ds(shard * cut // 128 * 128, 128)
            piece = v_small[shard // (2 * across), shard // 2 % across, shard % 2]
            small[:, tile] = small[:, tile] + piece.astype(full)
        rows = onehot[:, 0:1] * small[6:7, :]
        for action in range(1, ACTIONS):
            rows = rows + onehot[:, action : action + 1] * small[6 + action : 7 + action, :]
        table_rows[...] = rows
        yield
        yield from attend_forward_work(
            space_read, space_base, None, small.at[0:1], small.at[3:4], v_in, v_out, ready_in, ready_out,
            space_put, *kept_one, normed, tokens,
        )
        one.start()
        yield 1
        arrived(3, 4)
        ready_in, ready_out = fetch(3, v_in, sems.at[0]), fetch(4, v_out, sems.at[1])
        yield
        one.finish()
        yield
        yield from attend_forward_work(
            time_read, time_base, allowed, small.at[1:2], small.at[4:5], v_in, v_out, ready_in, ready_out,
            time_put, *kept_two, normed, group,
        )

    weave(work(), ticks, units, last)
    leave = Fetch(landed, stream_out, sems.at[3]).start()
    arrived(*range(5, count))
    for piece in pieces:
        piece.finish_send()
    leave.wait()


def forward(frames, onehot, allowed, shards, tokens, group, micro, seq_count, dp_count, block, tuning):
    total, width = frames.shape
    low, full = jnp.bfloat16, jnp.float32
    shape = jax.ShapeDtypeStruct
    plan, wholes, scratch = gather_plan(shards, seq_count, dp_count)
    heads = width // HDIM
    kept = [
        [shape((total, 3 * width), low), shape((total // size * heads, size, size), low), shape((total, width), low)]
        for size in (tokens, group)
    ]
    blocks = (total // block, block, width)
    count = len(shards)
    result = pl.pallas_call(
        functools.partial(forward_kernel, tokens, group, micro, seq_count, dp_count, plan, count, tuning),
        out_shape=tuple(wholes + [shape(blocks, low), shape((total, width), full)] + kept[0] + kept[1]),
        in_specs=vmem(3) + hbm(count),
        out_specs=hbm(count + 1) + vmem(7),
        scratch_shapes=[
            pltpu.VMEM((32, width), full),
            pltpu.VMEM((total // tokens, width), full),
            pltpu.VMEM(wholes[0].shape[1:], low),
            pltpu.VMEM(blocks, low),
            pltpu.VMEM(blocks, low),
            pltpu.VMEM((total, width), low),
            pltpu.VMEM((dp_count, width, 3 * width // dp_count), low),
            pltpu.VMEM((dp_count, width, width // dp_count), low),
            pltpu.SemaphoreType.DMA((4,)),
            pltpu.SemaphoreType.DMA((3,)),
        ] + scratch,
        compiler_params=pltpu.CompilerParams(
            collective_id=1, has_side_effects=True, vmem_limit_bytes=VMEM_LIMIT
        ),
        name="forward",
    )(frames, onehot, allowed, *shards)
    wholes, rest = result[:count], result[count:]
    return wholes, rest[0], rest[1], rest[2:5], rest[5:8]


def backward_scratch(total, width, packed, probs, w_in, w_out, in_blocks, out_blocks):
    low, full = jnp.bfloat16, jnp.float32
    return [
        pltpu.VMEM((total, width), low),
        pltpu.VMEM((total, width), low),
        pltpu.VMEM((total, 3 * width), low),
        pltpu.VMEM((total, width), full),
        pltpu.VMEM(packed.shape, low),
        pltpu.VMEM(probs.shape, low),
        pltpu.VMEM(w_in.shape, low),
        pltpu.VMEM(w_out.shape, low),
        stage_of(in_blocks),
        stage_of(out_blocks),
        pltpu.SemaphoreType.DMA((8,)),
    ]


def time_backward_kernel(tokens, micro, seq_count, dp_count, plan, count, ratio, *refs):
    take = Taker(refs)
    up, stream, gain, shift, packed_h, probs_h, mixed, w_in_h, w_out_h = take(9)
    partials = take(count)
    arrived, w_in_grad, w_out_grad, gain_out, shift_out = take(5)
    outs = take(count)
    own = take(11)
    down, change_sems = take(2)
    place = Place(seq_count, dp_count)
    change = Exchange(place, down, arrived, change_sems, micro, seq_count, False)
    entry_barrier(place, change)
    pieces = reduce_pieces(place, plan, partials, outs, take.refs)

    def work():
        yield from attend_backward_work(
            False, tokens, up, stream, None, gain, shift, packed_h, probs_h, mixed, w_in_h, w_out_h,
            down, w_in_grad, w_out_grad, gain_out, shift_out, None, *own
        )
        change.start()

    weave(work(), piece_ticks(pieces, OFFSETS), ratio)
    change.finish()
    for piece in pieces:
        piece.finish_send()


def time_backward(tokens, block, micro, seq_count, dp_count, partials, ratio,
                  up, stream, gain, shift, packed, probs, mixed, w_in, w_out):
    total, width = stream.shape
    low, full = jnp.bfloat16, jnp.float32
    shape = jax.ShapeDtypeStruct
    plan, sums_out, scratch = reduce_plan(partials)
    blocks = (total // block, block, width)
    in_blocks, out_blocks = blocks_of(w_in, seq_count), blocks_of(w_out, seq_count)
    outs = [
        shape(blocks, low), in_blocks, out_blocks, shape((1, width), full), shape((1, width), full)
    ]
    got = pl.pallas_call(
        functools.partial(time_backward_kernel, tokens, micro, seq_count, dp_count, plan, len(partials), ratio),
        out_shape=tuple(outs + sums_out),
        in_specs=vmem(4) + hbm(2) + vmem(1) + hbm(2 + len(partials)),
        out_specs=hbm(3) + vmem(2 + len(partials)),
        scratch_shapes=backward_scratch(total, width, packed, probs, w_in, w_out, in_blocks, out_blocks)
        + [pltpu.VMEM(blocks, low), pltpu.SemaphoreType.DMA((3,))]
        + scratch,
        compiler_params=pltpu.CompilerParams(
            collective_id=2, has_side_effects=True, vmem_limit_bytes=VMEM_LIMIT
        ),
        name="time_backward",
    )(up, stream, gain, shift, packed, probs, mixed, w_in, w_out, *partials)
    return got[:5], got[5:]


def space_backward_kernel(tokens, seq_count, dp_count, plans, counts, units, *refs):
    take = Taker(refs)
    up, stream, extra, gain, shift, packed_h, probs_h, mixed, w_in_h, w_out_h = take(10)
    onehot, gain_two, gain_three, shift_two, shift_three, up_bias, down_bias = take(7)
    partials = take(counts[0])
    down, w_in_grad, w_out_grad = take(3)
    outs = take(counts[0])
    last_outs = take(3)
    own = take(11)
    gain_out, shift_out, sums, rows, small_part = take(5)
    place = Place(seq_count, dp_count)
    entry_barrier(place)
    scratch = take(counts[1])
    pieces = reduce_pieces(place, plans[0], partials, outs, scratch)
    ends = reduce_pieces(place, plans[1], (w_in_grad, w_out_grad, small_part), last_outs, take.refs)
    width, hidden = stream.shape[1], up_bias.shape[1]
    low = jnp.bfloat16

    def small_rows():
        top = [gain_out, gain_two, gain_three, shift_out, shift_two, shift_three]
        rows[...] = jnp.zeros_like(rows)
        for at, row in enumerate(top):
            rows[at : at + 1, :] = row[...]
        for action in range(ACTIONS):
            total = onehot[0:1, action : action + 1] * sums[0:1, :]
            for frame in range(1, sums.shape[0]):
                total = total + onehot[frame : frame + 1, action : action + 1] * sums[frame : frame + 1, :]
            rows[6 + action : 7 + action, :] = total
        rows[14:15, :] = down_bias[...]
        across = seq_count // 8
        lane_row = lax.broadcasted_iota(jnp.int32, (16, 128), 0)
        for shard in range(seq_count):
            tile = shard * (width // seq_count) // 128 * 128
            first = rows[:, tile : tile + 128].astype(low)
            second = jnp.zeros((16, 128), jnp.float32)
            each = hidden // seq_count
            for part in range(each // 128):
                start = shard * each + part * 128
                second = jnp.where(lane_row == part, up_bias[:, start : start + 128], second)
            for part in range(dp_count):
                at = (part, shard // (2 * across), shard // 2 % across, shard % 2)
                small_part[at + (slice(0, 16),)] = first
                small_part[at + (slice(16, 32),)] = second.astype(low)

    matrices = [piece for piece, (index, _, _, _) in zip(ends, plans[1]) if index < 2]

    def early(event):
        for piece in matrices:
            piece.tick(event)

    def work():
        yield from attend_backward_work(
            True, tokens, up, stream, extra, gain, shift, packed_h, probs_h, mixed, w_in_h, w_out_h,
            down, w_in_grad, w_out_grad, gain_out, shift_out, sums, *own,
            have_grads=lambda: early(0), have_normed=lambda: early(1),
        )
        small_rows()
        yield

    weave(work(), piece_ticks(pieces, OFFSETS), units)
    for events in piece_ticks(ends, END_OFFSETS, matrices):
        for event in events:
            event()
    for piece in pieces + ends:
        piece.finish_send()


def space_backward(tokens, seq_count, dp_count, partials, units,
                   up, stream, extra, gain, shift, packed, probs, mixed, w_in, w_out,
                   onehot, gain_two, gain_three, shift_two, shift_three, up_bias, down_bias):
    total, width = stream.shape
    low, full = jnp.bfloat16, jnp.float32
    shape = jax.ShapeDtypeStruct
    in_blocks, out_blocks = blocks_of(w_in, seq_count), blocks_of(w_out, seq_count)
    small = shape(in_blocks.shape[:4] + (32, 128), low)
    plan, sums_out, scratch = reduce_plan(partials)
    end_plan, end_out, end_scratch = reduce_plan([in_blocks, out_blocks, small])
    outs = [shape((total // 16, 16, width), low), in_blocks, out_blocks]
    count = len(partials)
    got = pl.pallas_call(
        functools.partial(
            space_backward_kernel, tokens, seq_count, dp_count, (plan, end_plan), (count, len(scratch)), units
        ),
        out_shape=tuple(outs + sums_out + end_out),
        in_specs=vmem(5) + hbm(2) + vmem(1) + hbm(2) + vmem(7) + hbm(count),
        out_specs=vmem(1) + hbm(2) + vmem(count + 3),
        scratch_shapes=backward_scratch(total, width, packed, probs, w_in, w_out, in_blocks, out_blocks)
        + [
            pltpu.VMEM((1, width), full),
            pltpu.VMEM((1, width), full),
            pltpu.VMEM((total // tokens, width), full),
            pltpu.VMEM((16, width), full),
            pltpu.VMEM(small.shape, low),
        ]
        + scratch + end_scratch,
        compiler_params=pltpu.CompilerParams(
            collective_id=3, has_side_effects=True, vmem_limit_bytes=VMEM_LIMIT
        ),
        name="space_backward",
    )(up, stream, extra, gain, shift, packed, probs, mixed, w_in, w_out,
      onehot, gain_two, gain_three, shift_two, shift_three, up_bias, down_bias, *partials)
    return got[0], got[3 : 3 + count], got[3 + count :]

ACTIONS = 8
FRAMES = 16
FORWARD = ((0, 0, 0, 1, 1, 2, 2), (0, 3, 6), (14,))
TIME_UNITS = (7, 6, 6, 4)
SPACE_UNITS = (6, 4, 4, 4, 4, 2)


def body(
    frames_in,
    cotangent,
    lengths,
    actions,
    spatial_in,
    spatial_out,
    temporal_in,
    temporal_out,
    hidden_in,
    hidden_out,
    norm_gains,
    norm_shifts,
    bias_up,
    bias_down,
    action_table,
):
    seq_count, dp_count = lax.axis_size("seq"), lax.axis_size("dp")
    micro, frame_count, spatial, width = frames_in.shape
    tokens = micro * frame_count * spatial
    frames = seq_count * frame_count
    places = spatial // seq_count
    group = frames * places
    cut = norm_gains.shape[1]
    low, full = jnp.bfloat16, jnp.float32

    up_rows = bias_up.shape[0] // cut
    small = jnp.concatenate(
        [norm_gains, norm_shifts, action_table, bias_down[None], bias_up.reshape(up_rows, cut)], axis=0
    )
    used = small.shape[0]
    small = jnp.pad(small, ((0, 32 - used), (0, 0)))
    lane = lax.rem(lax.axis_index("seq") * cut, 128)
    small = lax.dynamic_update_slice(jnp.zeros((32, 128), low), small, (0, lane))
    shards = [small, spatial_in, spatial_out, temporal_in, temporal_out, hidden_in, hidden_out]

    at = jnp.arange(group, dtype=jnp.int32)
    frame, place = at // places, at % places
    video, frame = frame // FRAMES, frame % FRAMES
    span = lengths[:, video]
    alive = frame[None] < span
    allowed = (
        (place[:, None] == place[None]) & (video[:, None] == video[None]) & (frame[:, None] <= frame[None])
    )[None] & alive[:, :, None]
    allowed = allowed.astype(full)
    live = alive.astype(full).reshape(tokens, 1)
    onehot = (actions.reshape(-1)[:, None] == jnp.arange(ACTIONS)[None, :]).astype(full)

    frames_flat = frames_in.reshape(tokens, width)
    blocks = (tokens // places, places, width)
    wholes, stream_one, stream_two, kept_one, kept_two = forward(
        frames_flat, onehot, allowed, shards, spatial, group, micro, seq_count, dp_count,
        places, FORWARD,
    )
    w_sin, w_sout, w_tin, w_tout, w_hin, w_hout = [
        whole.reshape(dp_count, shard.shape[0] * seq_count, shard.shape[1])
        for whole, shard in zip(wholes[1:], shards[1:])
    ]
    small = wholes[0][0].reshape(seq_count // (128 // cut), 128 // cut, 32, 128).astype(full).sum(axis=1)
    rows = small.transpose(1, 0, 2).reshape(32, width)
    gain, shift = [rows[i : i + 1] for i in range(3)], [rows[i : i + 1] for i in range(3, 6)]
    table, down_bias = rows[6:14], rows[14:15]
    up_bias = rows[used - up_rows : used].reshape(up_rows, seq_count, cut).transpose(1, 0, 2).reshape(1, -1)
    row_pair = jnp.dot(onehot, table, precision=lax.Precision.HIGHEST)
    stream_one = stream_one.reshape(tokens, width)
    layer_out, two_grad, hin_grad, hout_grad, gain_three, shift_three, up_grad, down_grad = hidden_layer(
        micro, seq_count, dp_count, stream_two, live, gain[2], shift[2], up_bias, down_bias, cotangent.reshape(blocks),
        w_hin, w_hout,
    )
    (one_grad, tin_grad, tout_grad, gain_two, shift_two), hidden_sums = time_backward(
        group, places, micro, seq_count, dp_count, [hin_grad, hout_grad], TIME_UNITS,
        two_grad, stream_one, gain[1], shift[1], *kept_two, w_tin, w_tout,
    )
    in_grad, time_sums, (*space_sums, small) = space_backward(
        spatial, seq_count, dp_count, [tin_grad, tout_grad], SPACE_UNITS,
        one_grad.reshape(tokens, width), frames_flat, row_pair, gain[0], shift[0], *kept_one, w_sin, w_sout,
        onehot, gain_two, gain_three, shift_two, shift_three, up_grad, down_grad,
    )
    up_sum = small[16 : 16 + bias_up.shape[0] // 128].reshape(-1)
    small = lax.dynamic_slice(small, (0, lane), (16, cut))
    return (
        layer_out.reshape(frames_in.shape),
        in_grad.reshape(frames_in.shape),
        *space_sums,
        *time_sums,
        *hidden_sums,
        small[0:3],
        small[3:6],
        up_sum,
        small[14],
        small[6:14],
    )


def solution(mesh):
    rows = P(None, ("dp", "seq"), None, None)
    matrix = P("seq", "dp")
    cut = P(None, "seq")
    in_specs = (rows, rows, P(None, "dp"), P(None, ("dp", "seq"))) + (matrix,) * 6 + (cut, cut, P("seq"), P("seq"), cut)
    out_specs = (rows, rows) + (matrix,) * 6 + (cut, cut, P("seq"), P("seq"), cut)
    return jax.shard_map(body, mesh=mesh, in_specs=in_specs, out_specs=out_specs, check_vma=False)
```

```python
import functools
import jax
import jax.numpy as jnp
from jax import lax
from jax.experimental import pallas as pl
from jax.experimental.pallas import tpu as pltpu
from jax.sharding import PartitionSpec as P

MESH = pl.DeviceIdType.MESH


class Place:
    def __init__(self, seq_count, dp_count):
        self.size = {"z": 4, "x": seq_count // 8, "y": dp_count}
        seq = lax.axis_index("seq")
        self.core = lax.rem(seq, 2)
        self.at = {
            "z": seq // (2 * self.size["x"]),
            "x": lax.rem(seq // 2, self.size["x"]),
            "y": lax.axis_index("dp"),
        }

    def device(self, core=None, **moved):
        at = dict(self.at, **moved)
        core = self.core if core is None else core
        return (at["y"], (at["z"] * self.size["x"] + at["x"]) * 2 + core)

    def sibling(self):
        return self.device(core=1 - self.core)


def when(condition, action):
    if condition is True:
        action()
    elif condition is not False:
        pl.when(condition)(action)


def entry_barrier(place, change=None):
    barrier = pltpu.get_barrier_semaphore()

    def greet(device):
        pl.semaphore_signal(barrier, inc=1, device_id=device, device_id_type=MESH)

    count = 1
    if change is not None:
        count = count + change.greet()
    greet(place.sibling())
    for axis in ("x", "y", "z"):
        here, size = place.at[axis], place.size[axis]
        if size == 2:
            greet(place.device(**{axis: 1 - here}))
            count = count + 1
            continue
        pl.when(here > 0)(lambda axis=axis, here=here: greet(place.device(**{axis: here - 1})))
        pl.when(here < size - 1)(lambda axis=axis, here=here: greet(place.device(**{axis: here + 1})))
        count = count + (here > 0).astype(jnp.int32) + (here < size - 1).astype(jnp.int32)
    pl.semaphore_wait(barrier, count)


def line_steps(here, size, distance):
    if size == 2:
        return [(1 - here, True, False, 0)]
    return [
        (here - distance, here - distance >= 0, here < size - 1, 1),
        (here + distance, here + distance < size, here > 0, -1),
    ]


class Gather:
    def __init__(self, place, order, shard, whole, rows, sems):
        self.place, self.order = place, order
        self.shard, self.whole, self.rows = shard, whole, rows
        self.n = [place.size[axis] for axis in order]
        self.me = [place.at[axis] for axis in order]
        self.recv, self.send, self.sib_send, self.sib_recv, self.own_sem = sems
        self.sent = []
        n1, n2, n3 = self.n
        self.ticks = n1 - 1 + n2 + max(n3 - 1, 1)

    @staticmethod
    def sem_shapes(n):
        n1, n2, n3 = n
        count = n1 + n2 + n2 * n3
        return (
            pltpu.SemaphoreType.DMA((count,)),
            pltpu.SemaphoreType.DMA((2, count)),
            pltpu.SemaphoreType.DMA((n2, n3)),
            pltpu.SemaphoreType.DMA((n2, n3)),
            pltpu.SemaphoreType.DMA((1,)),
        )

    def block(self, first, second, third, core=None):
        at = dict(zip(self.order, (first, second, third)))
        core = self.place.core if core is None else core
        return self.whole.at[at["y"], at["z"], at["x"], core, self.rows]

    def own(self):
        return pltpu.make_async_copy(
            self.shard.at[self.rows], self.block(*self.me), self.own_sem.at[0]
        )

    def pass_on(self, stage, slot, src, dst, direction, condition):
        axis, here = self.order[stage], self.me[stage]
        target = self.place.device(**{axis: here + direction})
        sem = self.send.at[(direction + 1) // 2, slot]

        def copy():
            return pltpu.make_async_remote_copy(
                src_ref=src, dst_ref=dst, send_sem=sem, recv_sem=self.recv.at[slot],
                device_id=target, device_id_type=MESH,
            )

        when(condition, lambda: copy().start())
        self.sent.append((condition, copy))

    def spread(self, stage, slot, src, dst):
        here, size = self.me[stage], self.n[stage]
        if size == 2:
            axis = self.order[stage]
            target = self.place.device(**{axis: 1 - here})

            def copy():
                return pltpu.make_async_remote_copy(
                    src_ref=src, dst_ref=dst, send_sem=self.send.at[0, slot],
                    recv_sem=self.recv.at[slot], device_id=target, device_id_type=MESH,
                )

            copy().start()
            self.sent.append((True, copy))
            return
        self.pass_on(stage, slot, src, dst, 1, here < size - 1)
        self.pass_on(stage, slot, src, dst, -1, here > 0)

    def arrive(self, slot, ref):
        pltpu.make_async_copy(ref, ref, self.recv.at[slot]).wait()

    def to_sibling(self, second, third):
        ref = self.block(slice(None), second, third)

        def copy():
            return pltpu.make_async_remote_copy(
                src_ref=ref, dst_ref=ref, send_sem=self.sib_send.at[second, third],
                recv_sem=self.sib_recv.at[second, third],
                device_id=self.place.sibling(), device_id_type=MESH,
            )

        return copy

    def hand(self, second, third, condition=True):
        copy = self.to_sibling(second, third)
        when(condition, lambda: copy().start())

    def tick(self, now):
        n1, n2, n3 = self.n
        me1, me2, me3 = self.me
        if now == 0:
            self.own().start()
            src = self.shard.at[self.rows]
            self.spread(0, me1, src, self.block(*self.me))
        if 1 <= now <= n1 - 1:
            for index, here, go, way in line_steps(me1, n1, now):
                self.step_one(index, here, go, way)
        base = n1 - 1
        if now == base:
            self.own().wait()
            self.group_ready(me2)
            ref = self.block(slice(None), me2, me3)
            self.spread(1, n1 + me2, ref, ref)
        for distance in range(1, n2):
            if now == base + distance:
                for index, here, go, way in line_steps(me2, n2, distance):
                    self.step_two(index, here, go, way)
        for far in range(1, n3):
            for distance in range(0, n2):
                if now == base + distance + far:
                    choices = [(me2, True)] if distance == 0 else [
                        (index, here) for index, here, _, _ in line_steps(me2, n2, distance)
                    ]
                    for second, there in choices:
                        for index, here, go, way in line_steps(me3, n3, far):
                            self.step_three(second, there, index, here, go, way)

    def step_one(self, index, here, go, way):
        ref = self.block(index, *self.me[1:])
        both = here if go is True or go is False else jnp.logical_and(here, go)

        when(here, lambda: self.arrive(index, ref))
        if go is not False:
            self.pass_on(0, index, ref, ref, way, both)

    def group_ready(self, second, condition=True):
        self.hand(second, self.me[2], condition)
        ref = self.block(slice(None), second, self.me[2])
        slot = self.n[0] + self.n[1] + second * self.n[2] + self.me[2]
        if condition is True:
            self.spread(2, slot, ref, ref)
            return
        here, size = self.me[2], self.n[2]
        if size == 2:
            axis = self.order[2]
            target = self.place.device(**{axis: 1 - here})

            def copy():
                return pltpu.make_async_remote_copy(
                    src_ref=ref, dst_ref=ref, send_sem=self.send.at[0, slot],
                    recv_sem=self.recv.at[slot], device_id=target, device_id_type=MESH,
                )

            when(condition, lambda: copy().start())
            self.sent.append((condition, copy))
            return
        self.pass_on(2, slot, ref, ref, 1, jnp.logical_and(condition, here < size - 1))
        self.pass_on(2, slot, ref, ref, -1, jnp.logical_and(condition, here > 0))

    def step_two(self, index, here, go, way):
        slot = self.n[0] + index
        ref = self.block(slice(None), index, self.me[2])
        when(here, lambda: self.arrive(slot, ref))
        if go is not False:
            both = here if go is True else jnp.logical_and(here, go)
            self.pass_on(1, slot, ref, ref, way, both)
        self.group_ready(index, here)

    def step_three(self, second, there, index, here, go, way):
        slot = self.n[0] + self.n[1] + second * self.n[2] + index
        ref = self.block(slice(None), second, index)
        here = here if there is True else (there if here is True else jnp.logical_and(here, there))
        when(here, lambda: self.arrive(slot, ref))
        if go is not False:
            both = here if go is True else (go if here is True else jnp.logical_and(here, go))
            self.pass_on(2, slot, ref, ref, way, both)
        self.hand(second, index, here)

    def finish_recv(self):
        other = 1 - self.place.core
        for second in range(self.n[1]):
            for third in range(self.n[2]):
                ref = self.block(slice(None), second, third, core=other)
                pltpu.make_async_copy(ref, ref, self.sib_recv.at[second, third]).wait()

    def finish_send(self):
        for condition, copy in self.sent:
            when(condition, lambda copy=copy: copy().wait_send())
        for second in range(self.n[1]):
            for third in range(self.n[2]):
                self.to_sibling(second, third)().wait_send()


def split_plan(heights, parts_of, orders_of):
    plan = []
    for index, height in enumerate(heights):
        parts = min(parts_of, height // 16)
        rows = height // parts
        for part in range(parts):
            plan.append((index, part * rows, rows, orders_of(index)[part]))
    return plan


def gather_orders(index):
    if index % 2 == 0:
        return (("x", "z", "y"), ("y", "z", "x"))
    return (("z", "x", "y"), ("z", "y", "x"))


PER_GATHER = 5


def gather_plan(shards, seq_count, dp_count, parts=2):
    size = {"z": 4, "x": seq_count // 8, "y": dp_count}
    plan = split_plan([s.shape[0] for s in shards], parts, gather_orders)
    scratch = []
    for _, _, _, order in plan:
        scratch += list(Gather.sem_shapes([size[a] for a in order]))
    outs = [jax.ShapeDtypeStruct((dp_count, 4, size["x"], 2) + s.shape, s.dtype) for s in shards]
    return plan, outs, scratch


def gather_pieces(place, plan, shards, wholes, scratch):
    pieces = []
    for number, (index, first, rows, order) in enumerate(plan):
        pieces.append(
            Gather(place, order, shards[index], wholes[index], pl.ds(first, rows),
                   scratch[PER_GATHER * number : PER_GATHER * number + PER_GATHER])
        )
    return pieces

D_EPS = 1e-05
NEG = -1e30
HEADS = 16
HDIM = 64
SCALE = HDIM ** (-0.5)
NT = (((1,), (1,)), ((), ()))
TN = (((0,), (0,)), ((), ()))
ROWS = 32
VMEM_LIMIT = 63 * 1024 * 1024


def dot(left, right, dims=(((1,), (0,)), ((), ()))):
    return lax.dot_general(left, right, dims, preferred_element_type=jnp.float32)


def tile_of(size, largest=512):
    return max(t for t in (128, 256, 384, 512, 1024) if t <= largest and size % t == 0)


def loop(count, action):
    def step(index, carry):
        action(index)
        return carry

    lax.fori_loop(0, count, step, 0)


def at_rows(index, size):
    return pl.ds(pl.multiple_of(index * size, size), size)


def moments(value):
    width = value.shape[-1]
    centre = jnp.sum(value, axis=-1, keepdims=True) * (1.0 / width)
    offset = value - centre
    spread = jnp.sum(offset * offset, axis=-1, keepdims=True) * (1.0 / width)
    return offset, lax.rsqrt(spread + D_EPS)


def norm_forward(read, gain, shift, out):
    def step(index):
        rows = at_rows(index, ROWS)
        offset, rate = moments(read(rows))
        out[rows, :] = (offset * rate * gain[...] + shift[...]).astype(jnp.bfloat16)

    loop(out.shape[0] // ROWS, step)


def fold8(value):
    return jnp.sum(value.reshape(-1, 8, value.shape[-1]), axis=0)


def norm_backward(read, gain, grad, upstream, write, gain_out, shift_out):
    tokens, width = grad.shape

    def step(index, carry):
        gain_sum, shift_sum = carry
        rows = at_rows(index, ROWS)
        offset, rate = moments(read(rows))
        unit = offset * rate
        dy = grad[rows, :]
        gain_sum = gain_sum + fold8(dy * unit)
        shift_sum = shift_sum + fold8(dy)
        scaled = dy * gain[...]
        mean = jnp.sum(scaled, axis=-1, keepdims=True) * (1.0 / width)
        slope = jnp.sum(scaled * unit, axis=-1, keepdims=True) * (1.0 / width)
        write(index, rows, upstream(rows) + rate * (scaled - mean - unit * slope))
        return gain_sum, shift_sum

    zero = jnp.zeros((8, width), jnp.float32)
    gain_sum, shift_sum = lax.fori_loop(0, tokens // ROWS, step, (zero, zero))
    gain_out[...] = jnp.sum(gain_sum, axis=0, keepdims=True)
    shift_out[...] = jnp.sum(shift_sum, axis=0, keepdims=True)


def chunks(count, step, units):
    units = max(u for u in range(1, min(units, count) + 1) if count % u == 0)
    each = count // units
    for unit in range(units):
        loop(each, lambda index, unit=unit: step(unit * each + index))
        yield


def drain(work):
    for _ in work:
        pass


def project(rows, weight, emit, tile_max=512, units=1):
    parts, _, size = weight.shape
    tile = tile_of(size, tile_max)
    for part in range(parts):

        def step(index, part=part):
            inner = at_rows(index, tile)
            columns = pl.ds(pl.multiple_of(part * size + index * tile, 128), tile)
            emit(columns, dot(rows[...], weight[part, :, inner]))

        yield from chunks(size // tile, step, units)


def project_back(grad, weight, emit, tile_max=512, units=1):
    parts, depth, size = weight.shape
    tile = tile_of(depth, tile_max)

    def step(index):
        inner = at_rows(index, tile)
        total = None
        for part in range(parts):
            term = dot(grad[:, part * size : (part + 1) * size], weight[part, inner, :], NT)
            total = term if total is None else total + term
        emit(inner, total)

    yield from chunks(depth // tile, step, units)


def outer(rows, grad, out, stage, sems, units=1):
    parts, _, across, _, size_r, size = out.shape
    chips = stage.shape[2]
    tile = chips * 2 * size_r

    def leave(index, slot):
        first = index * chips
        return pltpu.make_async_copy(
            stage.at[slot], out.at[:, first // across, pl.ds(lax.rem(first, across), chips)], sems.at[slot]
        )

    def step(index):
        slot = lax.rem(index, 2)
        pl.when(index >= 2)(lambda: leave(index - 2, slot).wait())
        left = rows[:, at_rows(index, tile)]
        for part in range(parts):
            value = dot(left, grad[:, part * size : (part + 1) * size], TN)
            stage[slot, part] = value.reshape(chips, 2, size_r, size).astype(out.dtype)
        leave(index, slot).start()

    count = rows.shape[1] // tile
    yield from chunks(count, step, units)
    leave(count - 2, (count - 2) % 2).wait()
    leave(count - 1, (count - 1) % 2).wait()


def head_mask(shape, axis, head):
    lane = lax.broadcasted_iota(jnp.int32, shape, axis)
    return (lane // HDIM) == head


def pick(value, head):
    return jnp.where(head_mask(value.shape, 1, head), value, jnp.zeros_like(value))


def pick_rows(value, head):
    return jnp.where(head_mask(value.shape, 0, head), value, jnp.zeros_like(value))


def pair_slices(index, width, tokens):
    pairs = width // 128
    micro, pair = index // pairs, lax.rem(index, pairs)
    rows = pl.ds(pl.multiple_of(micro * tokens, tokens), tokens)
    return micro, rows, [
        pl.ds(pl.multiple_of(part * width + pair * 128, 128), 128) for part in range(3)
    ]


def attention_forward(packed, allowed, probs, mixed, tokens, units=1):
    width = mixed.shape[1]

    def step(index):
        micro, rows, (q_at, k_at, v_at) = pair_slices(index, width, tokens)
        queries = packed[rows, q_at] * jnp.bfloat16(SCALE)
        keys, values = packed[rows, k_at], packed[rows, v_at]
        values_t = values.astype(jnp.float32).T.astype(jnp.bfloat16)
        total = None
        for head in range(2):
            scores = dot(keys, pick(queries, head), NT)
            if allowed is not None:
                scores = jnp.where(allowed[micro] > 0, scores, NEG)
            raised = jnp.exp(scores - jnp.max(scores, axis=0, keepdims=True))
            prob = raised * (1.0 / jnp.sum(raised, axis=0, keepdims=True))
            prob = prob.astype(jnp.bfloat16)
            probs[2 * index + head] = prob
            term = dot(pick_rows(values_t, head), prob)
            total = term if total is None else total + term
        mixed[rows, q_at] = total.T.astype(jnp.bfloat16)

    yield from chunks(mixed.shape[0] // tokens * (width // 128), step, units)


def attention_backward(packed, probs, grad, packed_grad, tokens, units=1):
    width = grad.shape[1]

    def step(index):
        _, rows, (q_at, k_at, v_at) = pair_slices(index, width, tokens)
        queries, keys, values = packed[rows, q_at], packed[rows, k_at], packed[rows, v_at]
        upstream = grad[rows, q_at]
        keys_t = keys.astype(jnp.float32).T.astype(jnp.bfloat16)
        query_grad = key_grad = value_grad = None
        for head in range(2):
            low = probs[2 * index + head]
            prob = low.astype(jnp.float32)
            up = pick(upstream, head)
            prob_grad = dot(values, up, NT)
            inner = jnp.sum(prob * prob_grad, axis=0, keepdims=True)
            score_grad = (prob * (prob_grad - inner) * SCALE).astype(jnp.bfloat16)
            terms = (
                dot(pick_rows(keys_t, head), score_grad),
                dot(score_grad, pick(queries, head)),
                dot(low, up),
            )
            if head == 0:
                query_grad, key_grad, value_grad = terms
            else:
                query_grad = query_grad + terms[0]
                key_grad = key_grad + terms[1]
                value_grad = value_grad + terms[2]
        packed_grad[rows, q_at] = query_grad.T.astype(jnp.bfloat16)
        packed_grad[rows, k_at] = key_grad.astype(jnp.bfloat16)
        packed_grad[rows, v_at] = value_grad.astype(jnp.bfloat16)

    yield from chunks(grad.shape[0] // tokens * (width // 128), step, units)


class Fetch:
    def __init__(self, src, dst, sem):
        self.copy = pltpu.make_async_copy(src, dst, sem)

    def start(self):
        self.copy.start()
        return self

    def wait(self):
        self.copy.wait()


def spatial_reader(frames, row_pair, tokens):
    def read(rows):
        micro = rows.start // tokens
        return frames[rows, :].astype(jnp.float32) + row_pair[pl.ds(micro, 1), :]

    return read


def attend_forward_work(read, base, allowed, gain, shift, v_in, v_out, ready_in, ready_out, put,
                        packed, probs, mixed, normed, tokens):
    norm_forward(read, gain, shift, normed)
    ready_in()
    yield

    def emit(columns, value):
        packed[:, columns] = value.astype(jnp.bfloat16)

    yield from project(normed, v_in, emit, units=3)
    yield from attention_forward(packed, allowed, probs, mixed, tokens, units=8)
    ready_out()

    def emit_out(columns, value):
        put(columns, base(columns) + value)

    yield from project(mixed, v_out, emit_out, units=2)


def vmem(count):
    return [pl.BlockSpec(memory_space=pltpu.VMEM)] * count


def hbm(count):
    return [pl.BlockSpec(memory_space=pltpu.HBM)] * count


def attend_backward_work(spatial, tokens, up, stream, extra, gain, shift, packed_h, probs_h, mixed, w_in_h, w_out_h,
                         down, w_in_grad, w_out_grad, gain_out, shift_out, sums,
                         up_low, mixed_grad, packed_grad, normed_grad, packed, probs, w_in, w_out,
                         in_stage, out_stage, sems, have_grads=None, have_normed=None):
    read = spatial_reader(stream, extra, tokens) if spatial else (lambda rows: stream[rows, :].astype(jnp.float32))
    fetches = [
        Fetch(src, dst, sems.at[i]).start()
        for i, (src, dst) in enumerate(
            ((w_out_h, w_out), (packed_h, packed), (probs_h, probs), (w_in_h, w_in))
        )
    ]

    def lower(index):
        rows = at_rows(index, ROWS)
        up_low[rows, :] = up[rows, :].astype(jnp.bfloat16)

    loop(up.shape[0] // ROWS, lower)
    yield
    fetches[0].wait()

    def emit_mixed(columns, value):
        mixed_grad[:, columns] = value.astype(jnp.bfloat16)

    yield from project_back(up_low, w_out, emit_mixed, units=2)
    yield from outer(mixed, up_low, w_out_grad, out_stage, sems.at[pl.ds(4, 2)], units=2)
    normed = up_low
    norm_forward(read, gain, shift, normed)
    yield
    fetches[1].wait()
    fetches[2].wait()
    yield from attention_backward(packed, probs, mixed_grad, packed_grad, tokens, units=8)
    fetches[3].wait()
    yield from outer(normed, packed_grad, w_in_grad, in_stage, sems.at[pl.ds(6, 2)], units=4)
    if have_grads is not None:
        have_grads()

    def emit_normed(columns, value):
        normed_grad[:, columns] = value

    yield from project_back(packed_grad, w_in, emit_normed, 256, units=4)
    if have_normed is not None:
        have_normed()
    block = down.shape[1]

    def put(index, value):
        down[pl.ds(index * (ROWS // block), ROWS // block)] = value.reshape(-1, block, value.shape[1]).astype(down.dtype)

    if spatial:
        sums[...] = jnp.zeros_like(sums)

        def write(index, rows, value):
            put(index, value)
            micro = rows.start // tokens
            sums[pl.ds(micro, 1), :] += jnp.sum(fold8(value), axis=0, keepdims=True)
    else:

        def write(index, rows, value):
            put(index, value)

    norm_backward(
        read, gain, normed_grad, lambda rows: up[rows, :].astype(jnp.float32), write, gain_out, shift_out
    )
    yield


END = object()


def weave(work, ticks, units, last=()):
    held = -1
    for now, events in enumerate(ticks):
        for event in events:
            event()
        for _ in range(units[min(now, len(units) - 1)]):
            if held > now:
                break
            step = next(work, END)
            held = -1 if step is END or step is None else last[step]
            if held <= now:
                held = -1
    drain(work)


GELU_A = 0.7978845608028654
GELU_B = 0.044715


def gelu_pair(value):
    square = value * value
    bent = jnp.tanh(GELU_A * value * (1.0 + GELU_B * square))
    half = 0.5 * (1.0 + bent)
    slope = half + 0.5 * value * (1.0 - bent * bent) * (GELU_A * (1.0 + 3.0 * GELU_B * square))
    return value * half, slope


def hidden_kernel(micro, seq_count, dp_count, stream, live, gain, shift, up_bias, down_bias, cotangent_h, w_up_h, w_down_h,
                  layer_out, down, up_grad_h, down_grad_h, gain_out, shift_out, up_bias_out, down_bias_out,
                  normed, end_low, active, slope, expand_low, normed_grad, w_up, w_down, up_stage, down_stage,
                  cotangent, out, sems, end_sems, home_sems):
    low = jnp.bfloat16
    place = Place(seq_count, dp_count)
    end = Exchange(place, cotangent_h, cotangent, end_sems, micro, seq_count, True)
    home = Exchange(place, out, layer_out, home_sems, micro, seq_count, False)
    exchange_barrier(end)
    end.start()
    block = out.shape[1]
    first = Fetch(w_up_h, w_up, sems.at[0]).start()
    second = Fetch(w_down_h, w_down, sems.at[1]).start()
    tokens, width = stream.shape
    parts = w_up.shape[0]
    norm_forward(lambda rows: stream[rows, :], gain, shift, normed)

    first.wait()

    def emit_expand(columns, value):
        act, rate = gelu_pair(value + up_bias[:, columns])
        active[:, columns] = act.astype(low)
        slope[:, columns] = rate.astype(low)

    drain(project(normed, w_up, emit_expand, 256))
    second.wait()

    def emit_out(columns, value):
        ended = stream[:, columns] + value + down_bias[:, columns]
        out[:, :, columns] = (ended * live[...]).astype(low).reshape(tokens // block, block, -1)

    drain(project(active, w_down, emit_out, 512))
    home.start()
    end.finish()

    def upstream(rows):
        part = cotangent[pl.ds(rows.start // block, ROWS // block)].astype(jnp.float32).reshape(ROWS, width)
        return part * live[rows, :]

    def lower(index, total):
        rows = at_rows(index, ROWS)
        value = upstream(rows)
        end_low[rows, :] = value.astype(low)
        return total + fold8(value)

    total = lax.fori_loop(0, tokens // ROWS, lower, jnp.zeros((8, width), jnp.float32))
    down_bias_out[...] = jnp.sum(total, axis=0, keepdims=True)

    def emit_active(columns, value):
        grad = value * slope[:, columns].astype(jnp.float32)
        up_bias_out[:, columns] = jnp.sum(grad, axis=0, keepdims=True)
        expand_low[:, columns] = grad.astype(low)

    drain(project_back(end_low, w_down, emit_active, 256))

    drain(outer(active, end_low, down_grad_h, down_stage, sems.at[pl.ds(2, 2)]))
    drain(outer(normed, expand_low, up_grad_h, up_stage, sems.at[pl.ds(4, 2)]))

    def emit_normed(columns, value):
        normed_grad[:, columns] = value

    drain(project_back(expand_low, w_up, emit_normed, 512))

    def write(index, rows, value):
        down[rows, :] = value

    norm_backward(lambda rows: stream[rows, :], gain, normed_grad, upstream, write, gain_out, shift_out)
    home.finish()


def blocks_of(weight, seq_count):
    parts, depth, size = weight.shape
    return jax.ShapeDtypeStruct((parts, 4, seq_count // 8, 2, depth // seq_count, size), jnp.bfloat16)


def stage_of(blocks):
    chips = max(1, 64 // blocks.shape[4])
    return pltpu.VMEM((2, blocks.shape[0], chips) + blocks.shape[3:], jnp.bfloat16)


def hidden_layer(micro, seq_count, dp_count, stream, live, gain, shift, up_bias, down_bias, cotangent, w_up, w_down):
    tokens, width = stream.shape
    hidden = up_bias.shape[1]
    parts = w_up.shape[0]
    low, full = jnp.bfloat16, jnp.float32
    shape = jax.ShapeDtypeStruct
    up_blocks, down_blocks = blocks_of(w_up, seq_count), blocks_of(w_down, seq_count)
    return pl.pallas_call(
        functools.partial(hidden_kernel, micro, seq_count, dp_count),
        out_shape=(
            shape(cotangent.shape, low),
            shape((tokens, width), full),
            up_blocks,
            down_blocks,
            shape((1, width), full),
            shape((1, width), full),
            shape((1, hidden), full),
            shape((1, width), full),
        ),
        in_specs=vmem(6) + hbm(3),
        out_specs=hbm(1) + vmem(1) + hbm(2) + vmem(4),
        scratch_shapes=[
            pltpu.VMEM((tokens, width), low),
            pltpu.VMEM((tokens, width), low),
            pltpu.VMEM((tokens, hidden), low),
            pltpu.VMEM((tokens, hidden), low),
            pltpu.VMEM((tokens, hidden), low),
            pltpu.VMEM((tokens, width), full),
            pltpu.VMEM(w_up.shape, low),
            pltpu.VMEM(w_down.shape, low),
            stage_of(up_blocks),
            stage_of(down_blocks),
            pltpu.VMEM(cotangent.shape, low),
            pltpu.VMEM(cotangent.shape, low),
            pltpu.SemaphoreType.DMA((6,)),
            pltpu.SemaphoreType.DMA((3,)),
            pltpu.SemaphoreType.DMA((3,)),
        ],
        compiler_params=pltpu.CompilerParams(
            collective_id=4, has_side_effects=True, vmem_limit_bytes=VMEM_LIMIT
        ),
        name="hidden_layer",
    )(stream, live, gain, shift, up_bias, down_bias, cotangent, w_up, w_down)

class Reduce:
    def __init__(self, place, order, partial_sum, rows, out, bufs, sems):
        self.place, self.order, self.rows = place, order, rows
        self.partial, self.out = partial_sum, out
        self.kept, self.from_core, self.from_third, self.from_second, self.from_first = bufs
        self.core_sems, self.third_sems, self.second_sems, self.first_sems = sems
        self.n = [place.size[axis] for axis in order]
        self.me = [place.at[axis] for axis in order]
        self.sent = []
        n1, n2, n3 = self.n
        self.pair = n3 == 2
        self.third_ticks = 0 if self.pair else n3
        self.ticks = 1 + self.third_ticks + n2 + (1 if n1 == 2 else n1)

    @staticmethod
    def scratch(order, sizes, rows, columns, dtype):
        size = dict(zip(("y", "z", "x"), sizes))
        n1, n2, n3 = [size[axis] for axis in order]
        left = (n2, n1) if n3 == 2 else tuple(size[a] for a in ("y", "z", "x") if a != order[2])
        slots = lambda count: 1 if count == 2 else count + 1
        return (
            [
                pltpu.VMEM(sizes + (rows, columns), dtype),
                pltpu.VMEM(sizes + (rows, columns), dtype),
                pltpu.VMEM((slots(n3),) + left + (rows, columns), dtype),
                pltpu.VMEM((slots(n2), n1, rows, columns), dtype),
                pltpu.VMEM((slots(n1), rows, columns), dtype),
            ],
            [
                pltpu.SemaphoreType.DMA((3,)),
                pltpu.SemaphoreType.DMA((2, n3 + 1, n2)),
                pltpu.SemaphoreType.DMA((2, n2 + 1)),
                pltpu.SemaphoreType.DMA((2, n1 + 1)),
            ],
        )

    def block(self, first, second, third):
        at = dict(zip(self.order, (first, second, third)))
        return self.kept.at[at["y"], at["z"], at["x"]]

    def core_copy(self):
        return pltpu.make_async_remote_copy(
            src_ref=self.partial.at[:, :, :, 1 - self.place.core, self.rows],
            dst_ref=self.from_core,
            send_sem=self.core_sems.at[0], recv_sem=self.core_sems.at[1],
            device_id=self.place.sibling(), device_id_type=MESH,
        )

    def own_copy(self):
        return pltpu.make_async_copy(
            self.partial.at[:, :, :, self.place.core, self.rows], self.kept, self.core_sems.at[2]
        )

    def add_rows(self, dst, src, index):
        rows = dst.shape[-2]

        def step(i):
            at = index + (at_rows(i, 16),)
            dst[at] = dst[at] + src[at]

        loop(rows // 16, step)

    def send(self, stage, slot_sem, src, dst, moved, recv_sem, condition=True):
        axis = self.order[stage]

        def copy():
            return pltpu.make_async_remote_copy(
                src_ref=src, dst_ref=dst, send_sem=slot_sem, recv_sem=recv_sem,
                device_id=self.place.device(**{axis: moved}), device_id_type=MESH,
            )

        when(condition, lambda: copy().start())
        self.sent.append((condition, copy))

    def arrived(self, sem, ref):
        pltpu.make_async_copy(ref, ref, sem).wait()

    def second_order(self):
        order = []
        for step in range(1, self.n[1] + 1):
            for index in (self.n[1] - step, step - 1):
                if index not in order:
                    order.append(index)
        return order

    def tick(self, now):
        n1, n2, n3 = self.n
        if now == 0:
            self.core_copy().start()
            self.own_copy().start()
            return
        if now == 1:
            self.own_copy().wait()
            self.arrived(self.core_sems.at[1], self.from_core)
            sizes = self.kept.shape[:3]

            def add(index):
                y, rest = index // (sizes[1] * sizes[2]), lax.rem(index, sizes[1] * sizes[2])
                at = (y, rest // sizes[2], lax.rem(rest, sizes[2]))
                self.add_rows(self.kept, self.from_core, at)

            loop(sizes[0] * sizes[1] * sizes[2], add)
            if self.pair:
                other = 1 - self.me[2]
                for second in self.second_order():
                    self.send(
                        2, self.third_sems.at[0, 0, second], self.block(slice(None), second, other),
                        self.from_third.at[0, second], other, self.third_sems.at[1, 0, second],
                    )
            return
        now = now - 2
        if not self.pair:
            if now < n3:
                self.line(2, now)
        now = now - self.third_ticks
        if 0 <= now < n2:
            self.line(1, now)
        now = now - n2
        if 0 <= now and now < (1 if n1 == 2 else n1):
            self.line(0, now)

    def stage_ref(self, stage, index):
        if stage == 2:
            return self.block(slice(None), slice(None), index)
        if stage == 1:
            return self.block(slice(None), index, self.me[2])
        return self.block(index, self.me[1], self.me[2])

    def buffers(self, stage):
        if stage == 2:
            return self.from_third, self.third_sems.at[0, :, 0], self.third_sems.at[1, :, 0]
        if stage == 1:
            return self.from_second, self.second_sems.at[0], self.second_sems.at[1]
        return self.from_first, self.first_sems.at[0], self.first_sems.at[1]

    def absorb(self, stage, index, buffer_slot):
        buffer, sems = (
            (self.from_third, lambda s: self.third_sems.at[1, s, 0]),
            (self.from_second, lambda s: self.second_sems.at[1, s]),
            (self.from_first, lambda s: self.first_sems.at[1, s]),
        )[2 - stage]
        self.arrived(sems(buffer_slot), buffer.at[buffer_slot])
        target = self.stage_ref(stage, index)
        source = buffer.at[buffer_slot]
        self.add_all(target, source)

    def add_all(self, target, source):
        lead = target.shape[:-2]
        count = 1
        for size in lead:
            count *= size

        def add(index):
            at, rest = (), index
            for size in reversed(lead):
                at = (lax.rem(rest, size),) + at
                rest = rest // size
            self.add_rows(target, source, at)

        if count == 1 and not lead:
            self.add_rows(target, source, ())
        else:
            loop(count, add)

    def third_ready(self, second):
        if not self.pair:
            return
        self.arrived(self.third_sems.at[1, 0, second], self.from_third.at[0, second])
        self.add_all(self.block(slice(None), second, self.me[2]), self.from_third.at[0, second])

    def line(self, stage, now):
        size, here = self.n[stage], self.me[stage]
        sems = (self.first_sems, self.second_sems, None)[stage]
        send_sem = lambda s: self.third_sems.at[0, s, 0] if stage == 2 else sems.at[0, s]
        recv_sem = lambda s: self.third_sems.at[1, s, 0] if stage == 2 else sems.at[1, s]
        buffer = (self.from_first, self.from_second, self.from_third)[stage]
        if size == 2:
            if stage == 1:
                if now == 0:
                    for second in range(2):
                        self.third_ready(second)
                    self.send(stage, send_sem(0), self.stage_ref(stage, 1 - here), buffer.at[0], 1 - here, recv_sem(0))
                if now == 1:
                    self.absorb(stage, here, 0)
                    self.start_first()
            if stage == 0:
                self.arrived(recv_sem(0), buffer.at[0])
                self.finish(buffer.at[0])
            return
        if now < size - 1:
            up = size - 1 - now + here
            goes_up = jnp.logical_and(here <= now, here < size - 1)

            def go_up():
                if stage == 1:
                    self.third_ready(up)
                pl.when(here > 0)(lambda: self.absorb(stage, up, up))

            up = jnp.minimum(up, size - 1)
            pl.when(goes_up)(go_up)
            self.send(stage, send_sem(up), self.stage_ref(stage, up), buffer.at[up], here + 1, recv_sem(up), goes_up)
            down = jnp.maximum(now + here - (size - 1), 0)
            goes_down = jnp.logical_and(size - 1 - here <= now, here > 0)

            def go_down():
                if stage == 1:
                    self.third_ready(down)
                pl.when(here < size - 1)(lambda: self.absorb(stage, down, down))

            pl.when(goes_down)(go_down)
            self.send(stage, send_sem(down), self.stage_ref(stage, down), buffer.at[self.down_slot(stage, down)],
                      here - 1, recv_sem(self.down_slot(stage, down)), goes_down)
            return
        if stage == 1:
            self.third_ready(here)
        pl.when(here > 0)(lambda: self.absorb(stage, here, here))
        pl.when(here < size - 1)(lambda: self.absorb(stage, here, size))
        if stage == 1:
            self.start_first()
        if stage == 0:
            self.finish(None)

    def down_slot(self, stage, target):
        here, size = self.me[stage], self.n[stage]
        return jnp.where(target == here - 1, size, target)

    def start_first(self):
        if self.n[0] == 2:
            other = 1 - self.me[0]
            self.send(0, self.first_sems.at[0, 0], self.stage_ref(0, other), self.from_first.at[0], other,
                      self.first_sems.at[1, 0])

    def finish(self, extra):
        own = self.stage_ref(0, self.me[0])

        def step(i):
            rows = at_rows(i, 16)
            value = own[rows, :].astype(jnp.float32)
            if extra is not None:
                value = value + extra[rows, :].astype(jnp.float32)
            self.out[pl.ds(pl.multiple_of(self.rows.start + i * 16, 16), 16), :] = value

        loop(own.shape[0] // 16, step)

    def finish_send(self):
        self.core_copy().wait_send()
        for condition, copy in self.sent:
            when(condition, lambda copy=copy: copy().wait_send())


def by_time(timed):
    times = sorted({entry[0] for entry in timed})
    return [[entry[-1] for entry in timed if entry[0] == time] for time in times]


def piece_ticks(pieces, offsets, begun=()):
    timed = []
    for piece in pieces:
        for e in range(2 if piece in begun else 0, piece.ticks + 1):
            own = offsets[piece.order[2]]
            when_at = own[e] if e < len(own) else own[-1] + e - len(own) + 1
            timed.append((when_at, functools.partial(piece.tick, e)))
    return by_time(timed)


LATE = (0, 1, 4, 5, 6, 7, 8)
OFFSETS = {"x": LATE, "y": LATE, "z": (0, 1, 1, 2, 3, 4, 5, 6, 7)}
END_OFFSETS = OFFSETS
PER_PIECE = 9


def weight_orders(index):
    third = ("x", "z", "y") if index % 2 == 0 else ("y", "z", "x")
    first = ("x", "y", "z") if index % 2 == 0 else ("y", "x", "z")
    return (("z", "x", "y"), ("z", "y", "x"), first, third)


def reduce_plan(blocked, parts=4):
    outs = [jax.ShapeDtypeStruct(p.shape[4:], jnp.float32) for p in blocked]
    plan = split_plan([o.shape[0] for o in outs], parts, weight_orders)
    scratch = []
    for index, first, rows, order in plan:
        bufs, sems = Reduce.scratch(order, blocked[index].shape[:3], rows, outs[index].shape[1], blocked[index].dtype)
        scratch += bufs + sems
    return plan, outs, scratch


def reduce_pieces(place, plan, partials, outs, scratch):
    pieces = []
    for number, (index, first, rows, order) in enumerate(plan):
        own = scratch[PER_PIECE * number : PER_PIECE * number + PER_PIECE]
        pieces.append(Reduce(place, order, partials[index], pl.ds(first, rows), outs[index], own[:5], own[5:]))
    return pieces


class Exchange:
    def __init__(self, place, src, dst, sems, micro, seq_count, forward):
        self.place, self.src, self.dst, self.sems = place, src, dst, sems
        self.micro, self.count, self.forward = micro, seq_count, forward
        self.each = src.shape[0] // (micro * seq_count)
        self.me = lax.axis_index("seq")

    def indices(self, peer):
        frames = self.count * self.each
        out = []
        for micro in range(self.micro):
            for f in range(self.each):
                by_frame = (micro * self.each + f) * self.count
                if self.forward:
                    out.append((by_frame + peer, micro * frames + self.me * self.each + f))
                else:
                    out.append((micro * frames + peer * self.each + f, by_frame + self.me))
        return out

    def greet(self):
        barrier = pltpu.get_barrier_semaphore()

        def one(step):
            peer = lax.rem(self.me + step + 1, self.count)
            pl.semaphore_signal(
                barrier, inc=1, device_id=(lax.axis_index("dp"), peer), device_id_type=MESH
            )

        loop(self.count - 1, one)
        return self.count - 1

    def start(self):
        for here, there in self.indices(self.me):
            pltpu.make_async_copy(self.src.at[here], self.dst.at[there], self.sems.at[2]).start()

        def one(step):
            peer = lax.rem(self.me + step + 1, self.count)
            for here, there in self.indices(peer):
                pltpu.make_async_remote_copy(
                    src_ref=self.src.at[here], dst_ref=self.dst.at[there],
                    send_sem=self.sems.at[0], recv_sem=self.sems.at[1],
                    device_id=(lax.axis_index("dp"), peer), device_id_type=MESH,
                ).start()

        loop(self.count - 1, one)

    def finish(self):
        own = self.micro * self.each
        most = self.dst.at[pl.ds(0, own * (self.count - 1))]
        pltpu.make_async_copy(most, most, self.sems.at[1]).wait()
        pltpu.make_async_copy(most, most, self.sems.at[0]).wait()
        few = self.dst.at[pl.ds(0, own)]
        pltpu.make_async_copy(few, few, self.sems.at[2]).wait()


def exchange_barrier(change):
    pl.semaphore_wait(pltpu.get_barrier_semaphore(), change.greet())

class Taker:
    def __init__(self, refs):
        self.refs = list(refs)

    def __call__(self, count):
        taken, self.refs = self.refs[:count], self.refs[count:]
        return taken


def batch_ticks(pieces, batches, stagger):
    timed = []
    for piece, batch in zip(pieces, batches):
        for e in range(piece.ticks + 1):
            timed.append((e + stagger[batch], batch, functools.partial(piece.tick, e)))
    timed.sort(key=lambda entry: entry[:2])
    times = sorted({entry[0] for entry in timed})
    last = {batch: max(times.index(entry[0]) for entry in timed if entry[1] == batch) for batch in set(batches)}
    return by_time(timed), last


def forward_kernel(tokens, group, micro, seq_count, dp_count, plan, count, tuning, *refs):
    batches, stagger, units = tuning
    take = Taker(refs)
    frames, onehot, allowed = take(3)
    shards = take(count)
    wholes = take(count)
    stream_out, stream_two = take(2)
    kept_one, kept_two = take(3), take(3)
    small, table_rows, v_small, source, landed, normed, v_in, v_out, sems, one_sems = take(10)
    place = Place(seq_count, dp_count)
    one = Exchange(place, source, landed, one_sems, micro, seq_count, True)
    entry_barrier(place, one)
    pieces = gather_pieces(place, plan, shards, wholes, take.refs)
    owners = [index for index, _, _, _ in plan]
    ticks, last = batch_ticks(pieces, [batches[index] for index in owners], stagger)
    across = seq_count // 8
    total, width = frames.shape
    cut = width // seq_count
    block = source.shape[1]
    low, full = jnp.bfloat16, jnp.float32

    def arrived(*indices):
        for piece, owner in zip(pieces, owners):
            if owner in indices:
                piece.finish_recv()

    def fetch(index, into, sem):
        rows = shards[index].shape[0]

        def copy(shard):
            src = wholes[index].at[:, shard // (2 * across), lax.rem(shard // 2, across), lax.rem(shard, 2)]
            pltpu.make_async_copy(src, into.at[:, at_rows(shard, rows)], sem).start()

        loop(seq_count, copy)
        return lambda: pltpu.make_async_copy(into, into, sem).wait()

    def space_read(rows):
        return frames[rows, :].astype(full) + table_rows[pl.ds(rows.start // tokens, 1), :]

    def space_base(columns):
        rows = frames[:, columns].astype(full).reshape(total // tokens, tokens, -1)
        return (rows + table_rows[:, columns][:, None, :]).reshape(total, -1)

    def space_put(columns, value):
        source[:, :, columns] = value.astype(low).reshape(total // block, block, -1)

    def time_read(rows):
        return landed[pl.ds(rows.start // block, ROWS // block)].astype(full).reshape(ROWS, width)

    def time_base(columns):
        return landed[:, :, columns].astype(full).reshape(total, -1)

    def time_put(columns, value):
        stream_two[:, columns] = value

    def work():
        yield 0
        arrived(0, 1, 2)
        ready_in, ready_out = fetch(1, v_in, sems.at[0]), fetch(2, v_out, sems.at[1])
        Fetch(wholes[0].at[0], v_small, sems.at[2]).start().wait()
        small[...] = jnp.zeros_like(small)
        for shard in range(seq_count):
            tile = pl.ds(shard * cut // 128 * 128, 128)
            piece = v_small[shard // (2 * across), shard // 2 % across, shard % 2]
            small[:, tile] = small[:, tile] + piece.astype(full)
        rows = onehot[:, 0:1] * small[6:7, :]
        for action in range(1, ACTIONS):
            rows = rows + onehot[:, action : action + 1] * small[6 + action : 7 + action, :]
        table_rows[...] = rows
        yield
        yield from attend_forward_work(
            space_read, space_base, None, small.at[0:1], small.at[3:4], v_in, v_out, ready_in, ready_out,
            space_put, *kept_one, normed, tokens,
        )
        one.start()
        yield 1
        arrived(3, 4)
        ready_in, ready_out = fetch(3, v_in, sems.at[0]), fetch(4, v_out, sems.at[1])
        yield
        one.finish()
        yield
        yield from attend_forward_work(
            time_read, time_base, allowed, small.at[1:2], small.at[4:5], v_in, v_out, ready_in, ready_out,
            time_put, *kept_two, normed, group,
        )

    weave(work(), ticks, units, last)
    leave = Fetch(landed, stream_out, sems.at[3]).start()
    arrived(*range(5, count))
    for piece in pieces:
        piece.finish_send()
    leave.wait()


def forward(frames, onehot, allowed, shards, tokens, group, micro, seq_count, dp_count, block, tuning):
    total, width = frames.shape
    low, full = jnp.bfloat16, jnp.float32
    shape = jax.ShapeDtypeStruct
    plan, wholes, scratch = gather_plan(shards, seq_count, dp_count)
    heads = width // HDIM
    kept = [
        [shape((total, 3 * width), low), shape((total // size * heads, size, size), low), shape((total, width), low)]
        for size in (tokens, group)
    ]
    blocks = (total // block, block, width)
    count = len(shards)
    result = pl.pallas_call(
        functools.partial(forward_kernel, tokens, group, micro, seq_count, dp_count, plan, count, tuning),
        out_shape=tuple(wholes + [shape(blocks, low), shape((total, width), full)] + kept[0] + kept[1]),
        in_specs=vmem(3) + hbm(count),
        out_specs=hbm(count + 1) + vmem(7),
        scratch_shapes=[
            pltpu.VMEM((32, width), full),
            pltpu.VMEM((total // tokens, width), full),
            pltpu.VMEM(wholes[0].shape[1:], low),
            pltpu.VMEM(blocks, low),
            pltpu.VMEM(blocks, low),
            pltpu.VMEM((total, width), low),
            pltpu.VMEM((dp_count, width, 3 * width // dp_count), low),
            pltpu.VMEM((dp_count, width, width // dp_count), low),
            pltpu.SemaphoreType.DMA((4,)),
            pltpu.SemaphoreType.DMA((3,)),
        ] + scratch,
        compiler_params=pltpu.CompilerParams(
            collective_id=1, has_side_effects=True, vmem_limit_bytes=VMEM_LIMIT
        ),
        name="forward",
    )(frames, onehot, allowed, *shards)
    wholes, rest = result[:count], result[count:]
    return wholes, rest[0], rest[1], rest[2:5], rest[5:8]


def backward_scratch(total, width, packed, probs, w_in, w_out, in_blocks, out_blocks):
    low, full = jnp.bfloat16, jnp.float32
    return [
        pltpu.VMEM((total, width), low),
        pltpu.VMEM((total, width), low),
        pltpu.VMEM((total, 3 * width), low),
        pltpu.VMEM((total, width), full),
        pltpu.VMEM(packed.shape, low),
        pltpu.VMEM(probs.shape, low),
        pltpu.VMEM(w_in.shape, low),
        pltpu.VMEM(w_out.shape, low),
        stage_of(in_blocks),
        stage_of(out_blocks),
        pltpu.SemaphoreType.DMA((8,)),
    ]


def time_backward_kernel(tokens, micro, seq_count, dp_count, plan, count, ratio, *refs):
    take = Taker(refs)
    up, stream, gain, shift, packed_h, probs_h, mixed, w_in_h, w_out_h = take(9)
    partials = take(count)
    arrived, w_in_grad, w_out_grad, gain_out, shift_out = take(5)
    outs = take(count)
    own = take(11)
    down, change_sems = take(2)
    place = Place(seq_count, dp_count)
    change = Exchange(place, down, arrived, change_sems, micro, seq_count, False)
    entry_barrier(place, change)
    pieces = reduce_pieces(place, plan, partials, outs, take.refs)

    def work():
        yield from attend_backward_work(
            False, tokens, up, stream, None, gain, shift, packed_h, probs_h, mixed, w_in_h, w_out_h,
            down, w_in_grad, w_out_grad, gain_out, shift_out, None, *own
        )
        change.start()

    weave(work(), piece_ticks(pieces, OFFSETS), ratio)
    change.finish()
    for piece in pieces:
        piece.finish_send()


def time_backward(tokens, block, micro, seq_count, dp_count, partials, ratio,
                  up, stream, gain, shift, packed, probs, mixed, w_in, w_out):
    total, width = stream.shape
    low, full = jnp.bfloat16, jnp.float32
    shape = jax.ShapeDtypeStruct
    plan, sums_out, scratch = reduce_plan(partials)
    blocks = (total // block, block, width)
    in_blocks, out_blocks = blocks_of(w_in, seq_count), blocks_of(w_out, seq_count)
    outs = [
        shape(blocks, low), in_blocks, out_blocks, shape((1, width), full), shape((1, width), full)
    ]
    got = pl.pallas_call(
        functools.partial(time_backward_kernel, tokens, micro, seq_count, dp_count, plan, len(partials), ratio),
        out_shape=tuple(outs + sums_out),
        in_specs=vmem(4) + hbm(2) + vmem(1) + hbm(2 + len(partials)),
        out_specs=hbm(3) + vmem(2 + len(partials)),
        scratch_shapes=backward_scratch(total, width, packed, probs, w_in, w_out, in_blocks, out_blocks)
        + [pltpu.VMEM(blocks, low), pltpu.SemaphoreType.DMA((3,))]
        + scratch,
        compiler_params=pltpu.CompilerParams(
            collective_id=2, has_side_effects=True, vmem_limit_bytes=VMEM_LIMIT
        ),
        name="time_backward",
    )(up, stream, gain, shift, packed, probs, mixed, w_in, w_out, *partials)
    return got[:5], got[5:]


def space_backward_kernel(tokens, seq_count, dp_count, plans, counts, units, *refs):
    take = Taker(refs)
    up, stream, extra, gain, shift, packed_h, probs_h, mixed, w_in_h, w_out_h = take(10)
    onehot, gain_two, gain_three, shift_two, shift_three, up_bias, down_bias = take(7)
    partials = take(counts[0])
    down, w_in_grad, w_out_grad = take(3)
    outs = take(counts[0])
    last_outs = take(3)
    own = take(11)
    gain_out, shift_out, sums, rows, small_part = take(5)
    place = Place(seq_count, dp_count)
    entry_barrier(place)
    scratch = take(counts[1])
    pieces = reduce_pieces(place, plans[0], partials, outs, scratch)
    ends = reduce_pieces(place, plans[1], (w_in_grad, w_out_grad, small_part), last_outs, take.refs)
    width, hidden = stream.shape[1], up_bias.shape[1]
    low = jnp.bfloat16

    def small_rows():
        top = [gain_out, gain_two, gain_three, shift_out, shift_two, shift_three]
        rows[...] = jnp.zeros_like(rows)
        for at, row in enumerate(top):
            rows[at : at + 1, :] = row[...]
        for action in range(ACTIONS):
            total = onehot[0:1, action : action + 1] * sums[0:1, :]
            for frame in range(1, sums.shape[0]):
                total = total + onehot[frame : frame + 1, action : action + 1] * sums[frame : frame + 1, :]
            rows[6 + action : 7 + action, :] = total
        rows[14:15, :] = down_bias[...]
        across = seq_count // 8
        lane_row = lax.broadcasted_iota(jnp.int32, (16, 128), 0)
        for shard in range(seq_count):
            tile = shard * (width // seq_count) // 128 * 128
            first = rows[:, tile : tile + 128].astype(low)
            second = jnp.zeros((16, 128), jnp.float32)
            each = hidden // seq_count
            for part in range(each // 128):
                start = shard * each + part * 128
                second = jnp.where(lane_row == part, up_bias[:, start : start + 128], second)
            for part in range(dp_count):
                at = (part, shard // (2 * across), shard // 2 % across, shard % 2)
                small_part[at + (slice(0, 16),)] = first
                small_part[at + (slice(16, 32),)] = second.astype(low)

    matrices = [piece for piece, (index, _, _, _) in zip(ends, plans[1]) if index < 2]

    def early(event):
        for piece in matrices:
            piece.tick(event)

    def work():
        yield from attend_backward_work(
            True, tokens, up, stream, extra, gain, shift, packed_h, probs_h, mixed, w_in_h, w_out_h,
            down, w_in_grad, w_out_grad, gain_out, shift_out, sums, *own,
            have_grads=lambda: early(0), have_normed=lambda: early(1),
        )
        small_rows()
        yield

    weave(work(), piece_ticks(pieces, OFFSETS), units)
    for events in piece_ticks(ends, END_OFFSETS, matrices):
        for event in events:
            event()
    for piece in pieces + ends:
        piece.finish_send()


def space_backward(tokens, seq_count, dp_count, partials, units,
                   up, stream, extra, gain, shift, packed, probs, mixed, w_in, w_out,
                   onehot, gain_two, gain_three, shift_two, shift_three, up_bias, down_bias):
    total, width = stream.shape
    low, full = jnp.bfloat16, jnp.float32
    shape = jax.ShapeDtypeStruct
    in_blocks, out_blocks = blocks_of(w_in, seq_count), blocks_of(w_out, seq_count)
    small = shape(in_blocks.shape[:4] + (32, 128), low)
    plan, sums_out, scratch = reduce_plan(partials)
    end_plan, end_out, end_scratch = reduce_plan([in_blocks, out_blocks, small])
    outs = [shape((total // 16, 16, width), low), in_blocks, out_blocks]
    count = len(partials)
    got = pl.pallas_call(
        functools.partial(
            space_backward_kernel, tokens, seq_count, dp_count, (plan, end_plan), (count, len(scratch)), units
        ),
        out_shape=tuple(outs + sums_out + end_out),
        in_specs=vmem(5) + hbm(2) + vmem(1) + hbm(2) + vmem(7) + hbm(count),
        out_specs=vmem(1) + hbm(2) + vmem(count + 3),
        scratch_shapes=backward_scratch(total, width, packed, probs, w_in, w_out, in_blocks, out_blocks)
        + [
            pltpu.VMEM((1, width), full),
            pltpu.VMEM((1, width), full),
            pltpu.VMEM((total // tokens, width), full),
            pltpu.VMEM((16, width), full),
            pltpu.VMEM(small.shape, low),
        ]
        + scratch + end_scratch,
        compiler_params=pltpu.CompilerParams(
            collective_id=3, has_side_effects=True, vmem_limit_bytes=VMEM_LIMIT
        ),
        name="space_backward",
    )(up, stream, extra, gain, shift, packed, probs, mixed, w_in, w_out,
      onehot, gain_two, gain_three, shift_two, shift_three, up_bias, down_bias, *partials)
    return got[0], got[3 : 3 + count], got[3 + count :]

ACTIONS = 8
FRAMES = 16
FORWARD = ((0, 0, 0, 1, 1, 2, 2), (0, 3, 6), (14,))
TIME_UNITS = (7, 6, 6, 4)
SPACE_UNITS = (6, 4, 4, 4, 4, 2)


def body(
    frames_in,
    cotangent,
    lengths,
    actions,
    spatial_in,
    spatial_out,
    temporal_in,
    temporal_out,
    hidden_in,
    hidden_out,
    norm_gains,
    norm_shifts,
    bias_up,
    bias_down,
    action_table,
):
    seq_count, dp_count = lax.axis_size("seq"), lax.axis_size("dp")
    micro, frame_count, spatial, width = frames_in.shape
    tokens = micro * frame_count * spatial
    frames = seq_count * frame_count
    places = spatial // seq_count
    group = frames * places
    cut = norm_gains.shape[1]
    low, full = jnp.bfloat16, jnp.float32

    up_rows = bias_up.shape[0] // cut
    small = jnp.concatenate(
        [norm_gains, norm_shifts, action_table, bias_down[None], bias_up.reshape(up_rows, cut)], axis=0
    )
    used = small.shape[0]
    small = jnp.pad(small, ((0, 32 - used), (0, 0)))
    lane = lax.rem(lax.axis_index("seq") * cut, 128)
    small = lax.dynamic_update_slice(jnp.zeros((32, 128), low), small, (0, lane))
    shards = [small, spatial_in, spatial_out, temporal_in, temporal_out, hidden_in, hidden_out]

    at = jnp.arange(group, dtype=jnp.int32)
    frame, place = at // places, at % places
    video, frame = frame // FRAMES, frame % FRAMES
    span = lengths[:, video]
    alive = frame[None] < span
    allowed = (
        (place[:, None] == place[None]) & (video[:, None] == video[None]) & (frame[:, None] <= frame[None])
    )[None] & alive[:, :, None]
    allowed = allowed.astype(full)
    live = alive.astype(full).reshape(tokens, 1)
    onehot = (actions.reshape(-1)[:, None] == jnp.arange(ACTIONS)[None, :]).astype(full)

    frames_flat = frames_in.reshape(tokens, width)
    blocks = (tokens // places, places, width)
    wholes, stream_one, stream_two, kept_one, kept_two = forward(
        frames_flat, onehot, allowed, shards, spatial, group, micro, seq_count, dp_count,
        places, FORWARD,
    )
    w_sin, w_sout, w_tin, w_tout, w_hin, w_hout = [
        whole.reshape(dp_count, shard.shape[0] * seq_count, shard.shape[1])
        for whole, shard in zip(wholes[1:], shards[1:])
    ]
    small = wholes[0][0].reshape(seq_count // (128 // cut), 128 // cut, 32, 128).astype(full).sum(axis=1)
    rows = small.transpose(1, 0, 2).reshape(32, width)
    gain, shift = [rows[i : i + 1] for i in range(3)], [rows[i : i + 1] for i in range(3, 6)]
    table, down_bias = rows[6:14], rows[14:15]
    up_bias = rows[used - up_rows : used].reshape(up_rows, seq_count, cut).transpose(1, 0, 2).reshape(1, -1)
    row_pair = jnp.dot(onehot, table, precision=lax.Precision.HIGHEST)
    stream_one = stream_one.reshape(tokens, width)
    layer_out, two_grad, hin_grad, hout_grad, gain_three, shift_three, up_grad, down_grad = hidden_layer(
        micro, seq_count, dp_count, stream_two, live, gain[2], shift[2], up_bias, down_bias, cotangent.reshape(blocks),
        w_hin, w_hout,
    )
    (one_grad, tin_grad, tout_grad, gain_two, shift_two), hidden_sums = time_backward(
        group, places, micro, seq_count, dp_count, [hin_grad, hout_grad], TIME_UNITS,
        two_grad, stream_one, gain[1], shift[1], *kept_two, w_tin, w_tout,
    )
    in_grad, time_sums, (*space_sums, small) = space_backward(
        spatial, seq_count, dp_count, [tin_grad, tout_grad], SPACE_UNITS,
        one_grad.reshape(tokens, width), frames_flat, row_pair, gain[0], shift[0], *kept_one, w_sin, w_sout,
        onehot, gain_two, gain_three, shift_two, shift_three, up_grad, down_grad,
    )
    up_sum = small[16 : 16 + bias_up.shape[0] // 128].reshape(-1)
    small = lax.dynamic_slice(small, (0, lane), (16, cut))
    return (
        layer_out.reshape(frames_in.shape),
        in_grad.reshape(frames_in.shape),
        *space_sums,
        *time_sums,
        *hidden_sums,
        small[0:3],
        small[3:6],
        up_sum,
        small[14],
        small[6:14],
    )


def solution(mesh):
    rows = P(None, ("dp", "seq"), None, None)
    matrix = P("seq", "dp")
    cut = P(None, "seq")
    in_specs = (rows, rows, P(None, "dp"), P(None, ("dp", "seq"))) + (matrix,) * 6 + (cut, cut, P("seq"), P("seq"), cut)
    out_specs = (rows, rows) + (matrix,) * 6 + (cut, cut, P("seq"), P("seq"), cut)
    return jax.shard_map(body, mesh=mesh, in_specs=in_specs, out_specs=out_specs, check_vma=False)
```
